256 devices in a mesh: seq: 16 (over y, x), ctx: 16 (over z, core).
Axes of the slice: x: 4, y: 4, z: 8, core: 2. Of those that a mesh axis runs over, the one named last changes fastest.
Arguments:
- queries: bfloat16 [32768, 20, 128], P(('seq', 'ctx')), parts along dimension 0, may hold values from -1.6953125 to 1.6953125
- keys: bfloat16 [32768, 20, 128], P(('seq', 'ctx')), parts along dimension 0, may hold values from -1.6953125 to 1.6953125
- values: bfloat16 [32768, 20, 128], P(('seq', 'ctx')), parts along dimension 0, may hold values from -6 to 6
- outputs: bfloat16 [32768, 20, 128], P(('seq', 'ctx')), parts along dimension 0, may hold values from -6 to 6
- grad_out: bfloat16 [32768, 20, 128], P(('seq', 'ctx')), parts along dimension 0, may hold values from -6 to 6
- log_norm: bfloat16 [32768, 20], P(('seq', 'ctx')), parts along dimension 0, as said below
- block_position: int32 [256], P('seq'), parts along dimension 0, may hold values from 0 to 15, as said below
Outputs:
- grad_queries: bfloat16 [32768, 20, 128], P(('seq', 'ctx')), parts along dimension 0
- grad_keys: bfloat16 [32768, 20, 128], P(('seq', 'ctx')), parts along dimension 0
- grad_values: bfloat16 [32768, 20, 128], P(('seq', 'ctx')), parts along dimension 0
The draws below stay inside these ranges and needn't reach their ends.
There are 16 independent parts, one for each index of `seq`. The reference program is written for one: setup_inputs(seed, part) draws one part's arguments, and reference() takes and returns one part's arrays. A program takes and returns all parts, laid end to end along the dimension named above; each array names one. Nothing has to cross between parts.
Inputs may be any that keep to these rules, and one draw needn't show every extreme that they name: `block_position`: a permutation of the block numbers. log_norm[r, h] lies between log(p + 1) + 0.2 and log(p + 1) + 1.2 before rounding to bfloat16, with p = position[r].
All inputs are finite; a program needn't handle non-finite values.
Results may differ from the reference program's by a relative error of at most 0.0095.
Values may be sent and summed in bfloat16 or wider, within the bound.
A program may use at most 128 MiB of HBM per device.

```python
import math
import jax
import jax.numpy as jnp
from jax import lax

HEADS = 20
HEAD_DIM = 128
BLK = 128
SEQ = 2048
N_CTX = 16


def shared_order(key):
    return jax.random.permutation(key, N_CTX).astype(jnp.int32)


def draw_block_position(key, part):
    order = shared_order(key)
    return order


def draw_log_norm(key, part):
    order = shared_order(key)
    key = jax.random.fold_in(key, 7)
    offsets = jnp.arange(BLK, dtype=jnp.int32)
    position = (order[:, None] * BLK + offsets[None, :]).reshape(SEQ).astype(jnp.float32)
    spread = jax.random.uniform(key, (SEQ, HEADS), jnp.float32, 0.2, 1.2)
    return (jnp.log(position + 1.0)[:, None] + spread).astype(jnp.bfloat16)


def level_of(rng, shape, pieces, least, top_value):
    def one(dim, parts):
        heights = jax.random.uniform(jax.random.fold_in(jax.random.fold_in(rng, 6), dim), (parts,), jnp.float32, least / len(pieces), top_value / len(pieces))
        return jnp.repeat(jnp.exp(heights), shape[dim] // parts).reshape((-1,) + (1,) * (len(shape) - dim - 1))

    gain = one(*pieces[0])
    for cut in pieces[1:]:
        gain = gain * one(*cut)
    return gain


def centred(stream_key, dims, scale, bound, shards=(), kind=jnp.bfloat16):
    drawn = jax.random.normal(stream_key, dims, jnp.float32) * scale
    if len(shards) > 0:
        drawn = level_of(stream_key, dims, shards, -0.22, 0.18) * drawn
    return jnp.clip(drawn, min=-bound, max=bound).astype(kind)


def setup_inputs(seed: int = 0, part: int = 0) -> dict:
    splits = jax.random.split(jax.random.key(seed), 8)
    part_splits = jax.random.split(jax.random.fold_in(splits[7], part), 8)
    return {
        "queries": jnp.clip(jax.random.uniform(part_splits[0], (SEQ, HEADS, HEAD_DIM), jnp.float32, -1.6953125, 1.6953125) * level_of(part_splits[0], (SEQ, HEADS, HEAD_DIM), ((0, 16),), -0.4, 0.0), -1.6953125, 1.6953125).astype(jnp.bfloat16),
        "keys": jnp.clip(jax.random.uniform(part_splits[1], (SEQ, HEADS, HEAD_DIM), jnp.float32, -1.6953125, 1.6953125) * level_of(part_splits[1], (SEQ, HEADS, HEAD_DIM), ((0, 16),), -0.4, 0.0), -1.6953125, 1.6953125).astype(jnp.bfloat16),
        "values": centred(part_splits[2], (SEQ, HEADS, HEAD_DIM), 1.0, 6.0, ((0, 16),)),
        "outputs": centred(part_splits[3], (SEQ, HEADS, HEAD_DIM), 1.0, 6.0, ((0, 16),)),
        "grad_out": centred(part_splits[4], (SEQ, HEADS, HEAD_DIM), 1.0, 6.0, ((0, 16),)),
        "log_norm": draw_log_norm(jax.random.fold_in(jax.random.fold_in(splits[7], part), 71), part),
        "block_position": draw_block_position(jax.random.fold_in(jax.random.fold_in(splits[7], part), 71), part),
    }


def rounded(values_in):
    return lax.optimization_barrier(values_in.astype(jnp.bfloat16)).astype(jnp.float32)

def reference(queries, keys, values, outputs, grad_out, log_norm, block_position):
    total_rows, head_count, head_width = queries.shape
    block_rows = total_rows // N_CTX
    score_scale = 1.0 / math.sqrt(head_width)
    row_ids = jnp.arange(total_rows, dtype=jnp.int32)
    position = block_position[row_ids // block_rows].astype(jnp.int32) * block_rows + row_ids % block_rows
    query_f32 = queries.astype(jnp.float32)
    grad_f32 = grad_out.astype(jnp.float32)
    row_delta = rounded(lax.optimization_barrier(jnp.sum(grad_f32 * outputs.astype(jnp.float32), axis=2)))
    norm_f32 = log_norm.astype(jnp.float32)

    def one_block(dq_total, block_index):
        first_row = (block_index * block_rows).astype(jnp.int32)
        key_block = lax.dynamic_slice_in_dim(keys, first_row, block_rows, 0).astype(jnp.float32)
        value_block = lax.dynamic_slice_in_dim(values, first_row, block_rows, 0).astype(jnp.float32)
        key_pos = lax.dynamic_slice_in_dim(position, first_row, block_rows, 0)
        scores = jnp.einsum('qhc,khc->hqk', query_f32, key_block) * score_scale
        visible = key_pos[None, None, :] <= position[None, :, None]
        attn_weights = jnp.where(visible, jnp.exp(scores - norm_f32.T[:, :, None]), 0.0)
        grad_weights = jnp.einsum('qhc,khc->hqk', grad_f32, value_block)
        grad_scores = rounded(attn_weights * (grad_weights - row_delta.T[:, :, None]))
        weights_low = rounded(attn_weights)
        grad_values = jnp.einsum('hqk,qhc->khc', weights_low, grad_f32).astype(jnp.bfloat16)
        grad_keys = (jnp.einsum('hqk,qhc->khc', grad_scores, query_f32) * score_scale).astype(jnp.bfloat16)
        dq_part = rounded(jnp.einsum('hqk,khc->qhc', grad_scores, key_block))
        return (dq_total + dq_part, (grad_keys, grad_values))
    start_total = jnp.zeros((total_rows, head_count, head_width), jnp.float32)
    dq_total, (key_grads, value_grads) = lax.scan(one_block, start_total, jnp.arange(N_CTX, dtype=jnp.int32))
    grad_queries = (dq_total * score_scale).astype(jnp.bfloat16)
    return (grad_queries, key_grads.reshape(total_rows, head_count, head_width), value_grads.reshape(total_rows, head_count, head_width))
```

```python
import math

import jax
import jax.numpy as jnp
from jax import lax
from jax.experimental import pallas as pl
from jax.experimental.pallas import tpu as pltpu
from jax.sharding import PartitionSpec as P

N = 16
ROWS = 128
WIDTH = 128
HEADS = 20
EXTRA = HEADS - N
STRIDE = N // EXTRA
CHIPS = N // 2
PAIR = 2 * ROWS
LOG2E = math.log2(math.e)
SCALE = 1.0 / math.sqrt(WIDTH)
HIDE = 1e30
K, V, Q, G, AUX = range(5)
DQ, DK, DV = range(3)


def swing(step):
    return (step + 1) // 2 * (2 * (step % 2) - 1)


def mm(a, b):
    return lax.dot_general(a, b, (((1,), (0,)), ((), ())), preferred_element_type=jnp.float32)


def mm_nt(a, b):
    return lax.dot_general(a, b, (((1,), (1,)), ((), ())), preferred_element_type=jnp.float32)


def kernel(
    q_ref, k_ref, v_ref, o_ref, g_ref, ln_ref, pos_ref,
    dq_ref, dk_ref, dv_ref,
    kb, vb, qb, gb, auxb, ov, gv, auxs, kt, dka, dva, dqo, dko, dvo,
    load_sem, in_send, in_recv, out_send, out_recv,
):
    me = lax.axis_index("ctx")
    chip = me // 2
    two = me % STRIDE == 0
    extra_head = N + me // STRIDE
    sources = (k_ref, v_ref, q_ref, g_ref, auxs)
    landing = (kb, vb, qb, gb, auxb)
    staged = (dqo, dko, dvo)
    results = (dq_ref, dk_ref, dv_ref)

    def wait(ref, sem):
        pltpu.make_async_copy(ref, ref, sem).wait()

    def send(kind, head, slot, dest):
        pltpu.make_async_remote_copy(
            src_ref=sources[kind].at[head],
            dst_ref=landing[kind].at[slot, me],
            send_sem=in_send.at[kind, head],
            recv_sem=in_recv.at[kind, slot, me],
            device_id={"ctx": dest},
            device_id_type=pl.DeviceIdType.MESH,
        ).start()

    def keep(kind, head, slot):
        pltpu.make_async_copy(
            sources[kind].at[head], landing[kind].at[slot, me], in_recv.at[kind, slot, me]
        ).start()

    def send_extra(kinds):
        def one(i, carry):
            which = (me // STRIDE + i) % EXTRA
            dest = which * STRIDE

            @pl.when(dest != me)
            def _():
                for kind in kinds:
                    send(kind, N + which, 0, dest)

            @pl.when(dest == me)
            def _():
                for kind in kinds:
                    keep(kind, N + which, 0)

            return carry

        lax.fori_loop(0, EXTRA, one, 0)

    def send_main(kinds):
        for kind in kinds:
            keep(kind, me, 1)

        def one(i, carry):
            dest = (me + swing(i) + N) % N
            for kind in kinds:
                send(kind, dest, 1, dest)
            return carry

        lax.fori_loop(1, N, one, 0)

    load_g = pltpu.make_async_copy(g_ref, gv, load_sem.at[0])
    load_o = pltpu.make_async_copy(o_ref, ov, load_sem.at[1])
    load_g.start()
    load_o.start()
    barrier = pltpu.get_barrier_semaphore()

    def greet(i, carry):
        pl.semaphore_signal(
            barrier, inc=1, device_id={"ctx": (me + i) % N}, device_id_type=pl.DeviceIdType.MESH
        )
        return carry

    lax.fori_loop(1, N, greet, 0)
    pl.semaphore_wait(barrier, N - 1)

    send_extra((K, V, Q, G))

    load_g.wait()
    load_o.wait()
    norm = ln_ref[...].astype(jnp.float32) * LOG2E
    ones = jnp.ones((8, WIDTH), jnp.bfloat16)
    upper = lax.broadcasted_iota(jnp.int32, (8, ROWS), 0) < 4
    for h in range(HEADS):
        product = gv[h].astype(jnp.float32) * ov[h].astype(jnp.float32)
        high = product.astype(jnp.bfloat16)
        low = (product - high.astype(jnp.float32)).astype(jnp.bfloat16)
        delta = (mm_nt(ones, high) + mm_nt(ones, low)).astype(jnp.bfloat16).astype(jnp.float32)
        auxs[h] = jnp.where(upper, norm[h : h + 1, :], delta)
    send_extra((AUX,))
    send_main((AUX,))
    send_main((K, V))
    send_main((Q, G))

    rows_k = lax.broadcasted_iota(jnp.int32, (ROWS, ROWS), 0)
    rows_q = lax.broadcasted_iota(jnp.int32, (ROWS, ROWS), 1)

    def one_pair(step, carry):
        slot = step // CHIPS
        turn = step % CHIPS
        head = jnp.where(slot == 0, extra_head, me)

        @pl.when(turn == 0)
        def _():
            dka[...] = jnp.zeros_like(dka)
            dva[...] = jnp.zeros_like(dva)

            def arrived(i, c):
                for kind in (K, V):
                    wait(landing[kind].at[slot, i], in_recv.at[kind, slot, i])
                return c

            lax.fori_loop(0, N, arrived, 0)
            for t in range(CHIPS):
                kt[t] = kb[slot, 2 * t : 2 * t + 2].reshape(PAIR, WIDTH).T

        c = (chip + swing(turn) + CHIPS) % CHIPS
        for b in range(2):
            for kind in (AUX, Q, G):
                wait(landing[kind].at[slot, 2 * c + b], in_recv.at[kind, slot, 2 * c + b])
        pair = pl.ds(2 * c, 2)
        queries = qb[slot, pair].reshape(PAIR, WIDTH)
        grads = gb[slot, pair].reshape(PAIR, WIDTH)
        queries_t = queries.T
        grads_t = grads.T
        norms = [auxb[slot, 2 * c + b, 0:1, :] for b in range(2)]
        delta = jnp.concatenate([auxb[slot, 2 * c + b, 4:5, :] for b in range(2)], axis=1)
        dq_t = jnp.zeros((WIDTH, PAIR), jnp.float32)
        for t in range(CHIPS):
            tile = (c + t) % CHIPS
            spot = pl.ds(2 * tile, 2)
            keys = kb[slot, spot].reshape(PAIR, WIDTH)
            vals = vb[slot, spot].reshape(PAIR, WIDTH)
            scores = mm(keys, queries_t) * (SCALE * LOG2E)
            grad_weights = mm(vals, grads_t)
            parts = []
            for kblock in range(2):
                bias = []
                for qblock in range(2):
                    later = pos_ref[2 * tile + kblock] > pos_ref[2 * c + qblock]
                    row = norms[qblock] + jnp.where(later, HIDE, 0.0)
                    if t == 0:
                        if kblock == qblock:
                            row = row + jnp.where(rows_k > rows_q, HIDE, 0.0)
                        else:
                            row = jnp.broadcast_to(row, (ROWS, ROWS))
                    bias.append(row)
                parts.append(
                    jnp.exp2(
                        scores[kblock * ROWS : (kblock + 1) * ROWS] - jnp.concatenate(bias, axis=1)
                    )
                )
            weights = jnp.concatenate(parts, axis=0)
            grad_scores = (weights * (grad_weights - delta)).astype(jnp.bfloat16)
            dva[tile] += mm(weights.astype(jnp.bfloat16), grads)
            dka[tile] += mm(grad_scores, queries)
            dq_t += mm(kt[tile], grad_scores)
        dqo[slot, pair] = (dq_t * SCALE).T.astype(jnp.bfloat16).reshape(2, ROWS, WIDTH)

        def give(kind, dest):
            src = staged[kind].at[slot, dest]
            dst = results[kind].at[head]

            @pl.when(dest != me)
            def _():
                pltpu.make_async_remote_copy(
                    src_ref=src,
                    dst_ref=dst,
                    send_sem=out_send.at[kind, slot, dest],
                    recv_sem=out_recv.at[kind, head],
                    device_id={"ctx": dest},
                    device_id_type=pl.DeviceIdType.MESH,
                ).start()

            @pl.when(dest == me)
            def _():
                pltpu.make_async_copy(src, dst, out_recv.at[kind, head]).start()

        for b in range(2):
            give(DQ, 2 * c + b)

        @pl.when(turn == CHIPS - 1)
        def _():
            def finish(i, carry):
                spot_chip = (chip + swing(i) + CHIPS) % CHIPS
                spot = pl.ds(2 * spot_chip, 2)
                dko[slot, spot] = (dka[spot_chip] * SCALE).astype(jnp.bfloat16).reshape(2, ROWS, WIDTH)
                dvo[slot, spot] = dva[spot_chip].astype(jnp.bfloat16).reshape(2, ROWS, WIDTH)
                for b in range(2):
                    give(DK, 2 * spot_chip + b)
                    give(DV, 2 * spot_chip + b)
                return carry

            lax.fori_loop(0, CHIPS, finish, 0)

        return carry

    lax.fori_loop(jnp.where(two, 0, CHIPS), 2 * CHIPS, one_pair, 0)

    def drain_in(h, carry):
        owner = jnp.where(h < N, h, (h - N) * STRIDE)

        @pl.when(owner != me)
        def _():
            for kind in range(5):
                wait(sources[kind].at[h], in_send.at[kind, h])

        return carry

    lax.fori_loop(0, HEADS, drain_in, 0)

    def drain_out(step, carry):
        slot = step // N
        dest = step % N

        @pl.when(dest != me)
        def _():
            for kind in range(3):
                wait(staged[kind].at[slot, dest], out_send.at[kind, slot, dest])

        return carry

    lax.fori_loop(jnp.where(two, 0, N), 2 * N, drain_out, 0)

    def collect(h, carry):
        for kind in range(3):
            wait(results[kind].at[h], out_recv.at[kind, h])
        return carry

    lax.fori_loop(0, HEADS, collect, 0)


def body(queries, keys, values, outputs, grad_out, log_norm, block_position):
    by_head = [jnp.transpose(x, (1, 0, 2)) for x in (queries, keys, values, outputs, grad_out)]
    whole = jax.ShapeDtypeStruct((HEADS, ROWS, WIDTH), jnp.bfloat16)
    blocks = pltpu.VMEM((2, N, ROWS, WIDTH), jnp.bfloat16)
    totals = pltpu.VMEM((CHIPS, PAIR, WIDTH), jnp.float32)
    results = pl.pallas_call(
        kernel,
        out_shape=(whole, whole, whole),
        in_specs=[pl.BlockSpec(memory_space=pl.ANY)] * 5
        + [pl.BlockSpec(memory_space=pltpu.VMEM), pl.BlockSpec(memory_space=pltpu.SMEM)],
        out_specs=[pl.BlockSpec(memory_space=pl.ANY)] * 3,
        scratch_shapes=[
            blocks, blocks, blocks, blocks,
            pltpu.VMEM((2, N, 8, ROWS), jnp.float32),
            pltpu.VMEM((HEADS, ROWS, WIDTH), jnp.bfloat16),
            pltpu.VMEM((HEADS, ROWS, WIDTH), jnp.bfloat16),
            pltpu.VMEM((HEADS, 8, ROWS), jnp.float32),
            pltpu.VMEM((CHIPS, WIDTH, PAIR), jnp.bfloat16),
            totals, totals,
            blocks, blocks, blocks,
            pltpu.SemaphoreType.DMA((2,)),
            pltpu.SemaphoreType.DMA((5, HEADS)),
            pltpu.SemaphoreType.DMA((5, 2, N)),
            pltpu.SemaphoreType.DMA((3, 2, N)),
            pltpu.SemaphoreType.DMA((3, HEADS)),
        ],
        compiler_params=pltpu.CompilerParams(
            collective_id=0, has_side_effects=True, vmem_limit_bytes=48 * 1024 * 1024
        ),
        name="attention_backward",
    )(*by_head, log_norm.T, block_position)
    return tuple(jnp.transpose(x, (1, 0, 2)) for x in results)


def solution(mesh):
    rows = P(("seq", "ctx"), None, None)
    return jax.shard_map(
        body,
        mesh=mesh,
        in_specs=(rows, rows, rows, rows, rows, P(("seq", "ctx"), None), P("seq")),
        out_specs=(rows, rows, rows),
        check_vma=False,
    )
```

```python
import math

import jax
import jax.numpy as jnp
from jax import lax
from jax.experimental import pallas as pl
from jax.experimental.pallas import tpu as pltpu
from jax.sharding import PartitionSpec as P

N = 16
ROWS = 128
WIDTH = 128
HEADS = 20
EXTRA = HEADS - N
STRIDE = N // EXTRA
CHIPS = N // 2
PAIR = 2 * ROWS
LOG2E = math.log2(math.e)
SCALE = 1.0 / math.sqrt(WIDTH)
HIDE = 1e30
K, V, Q, G, AUX = range(5)
DQ, DK, DV = range(3)


def swing(step):
    return (step + 1) // 2 * (2 * (step % 2) - 1)


def mm(a, b):
    return lax.dot_general(a, b, (((1,), (0,)), ((), ())), preferred_element_type=jnp.float32)


def mm_nt(a, b):
    return lax.dot_general(a, b, (((1,), (1,)), ((), ())), preferred_element_type=jnp.float32)


def kernel(
    q_ref, k_ref, v_ref, o_ref, g_ref, ln_ref, pos_ref,
    dq_ref, dk_ref, dv_ref,
    kb, vb, qb, gb, auxb, ov, gv, auxs, qt, gt, tri, dqa, dqo, dko, dvo,
    load_sem, in_send, in_recv, out_send, out_recv,
):
    me = lax.axis_index("ctx")
    chip = me // 2
    two = me % STRIDE == 0
    extra_head = N + me // STRIDE
    sources = (k_ref, v_ref, q_ref, g_ref, auxs)
    landing = (kb, vb, qb, gb, auxb)
    staged = (dqo, dko, dvo)
    results = (dq_ref, dk_ref, dv_ref)

    def wait(ref, sem):
        pltpu.make_async_copy(ref, ref, sem).wait()

    def send(kind, head, slot, dest):
        pltpu.make_async_remote_copy(
            src_ref=sources[kind].at[head],
            dst_ref=landing[kind].at[slot, me],
            send_sem=in_send.at[kind, head],
            recv_sem=in_recv.at[kind, slot, me],
            device_id={"ctx": dest},
            device_id_type=pl.DeviceIdType.MESH,
        ).start()

    def keep(kind, head, slot):
        pltpu.make_async_copy(
            sources[kind].at[head], landing[kind].at[slot, me], in_recv.at[kind, slot, me]
        ).start()

    def send_extra(kinds):
        def one(i, carry):
            which = (me // STRIDE + i) % EXTRA
            dest = which * STRIDE

            @pl.when(dest != me)
            def _():
                for kind in kinds:
                    send(kind, N + which, 0, dest)

            @pl.when(dest == me)
            def _():
                for kind in kinds:
                    keep(kind, N + which, 0)

            return carry

        lax.fori_loop(0, EXTRA, one, 0)

    def send_main(kinds):
        for kind in kinds:
            keep(kind, me, 1)

        def one(i, carry):
            dest = (me + swing(i) + N) % N
            for kind in kinds:
                send(kind, dest, 1, dest)
            return carry

        lax.fori_loop(1, N, one, 0)

    load_g = pltpu.make_async_copy(g_ref, gv, load_sem.at[0])
    load_o = pltpu.make_async_copy(o_ref, ov, load_sem.at[1])
    load_g.start()
    load_o.start()
    barrier = pltpu.get_barrier_semaphore()

    def greet(i, carry):
        pl.semaphore_signal(
            barrier, inc=1, device_id={"ctx": (me + i) % N}, device_id_type=pl.DeviceIdType.MESH
        )
        return carry

    lax.fori_loop(1, N, greet, 0)
    pl.semaphore_wait(barrier, N - 1)

    send_extra((Q, G))

    load_g.wait()
    load_o.wait()
    norm = ln_ref[...].astype(jnp.float32) * LOG2E
    ones = jnp.ones((8, WIDTH), jnp.bfloat16)
    upper = lax.broadcasted_iota(jnp.int32, (8, ROWS), 0) < 4
    for h in range(HEADS):
        product = gv[h].astype(jnp.float32) * ov[h].astype(jnp.float32)
        high = product.astype(jnp.bfloat16)
        low = (product - high.astype(jnp.float32)).astype(jnp.bfloat16)
        delta = (mm_nt(ones, high) + mm_nt(ones, low)).astype(jnp.bfloat16).astype(jnp.float32)
        auxs[h] = jnp.where(upper, norm[h : h + 1, :], delta)
    send_extra((AUX,))
    send_main((AUX,))
    send_extra((K, V))
    send_main((Q, G))
    send_main((K, V))

    below = lax.broadcasted_iota(jnp.int32, (ROWS, ROWS), 0) > lax.broadcasted_iota(
        jnp.int32, (ROWS, ROWS), 1
    )
    tri[0] = jnp.zeros((ROWS, ROWS), jnp.float32)
    tri[1] = jnp.where(below, HIDE, 0.0)

    def one_pair(step, carry):
        slot = step // CHIPS
        turn = step % CHIPS
        head = jnp.where(slot == 0, extra_head, me)

        def give(kind, dest):
            src = staged[kind].at[slot, dest]
            dst = results[kind].at[head]

            @pl.when(dest != me)
            def _():
                pltpu.make_async_remote_copy(
                    src_ref=src,
                    dst_ref=dst,
                    send_sem=out_send.at[kind, slot, dest],
                    recv_sem=out_recv.at[kind, head],
                    device_id={"ctx": dest},
                    device_id_type=pl.DeviceIdType.MESH,
                ).start()

            @pl.when(dest == me)
            def _():
                pltpu.make_async_copy(src, dst, out_recv.at[kind, head]).start()

        def around(i):
            return (chip + swing(i) + CHIPS) % CHIPS

        @pl.when(turn == 0)
        def _():
            dqa[...] = jnp.zeros_like(dqa)

            def arrived(i, carry):
                c = around(i)
                for b in range(2):
                    for kind in (AUX, Q, G):
                        wait(landing[kind].at[slot, 2 * c + b], in_recv.at[kind, slot, 2 * c + b])
                qt[c] = qb[slot, pl.ds(2 * c, 2)].reshape(PAIR, WIDTH).T
                gt[c] = gb[slot, pl.ds(2 * c, 2)].reshape(PAIR, WIDTH).T
                return carry

            lax.fori_loop(0, CHIPS, arrived, 0)

        c = around(turn)
        for b in range(2):
            for kind in (K, V):
                wait(landing[kind].at[slot, 2 * c + b], in_recv.at[kind, slot, 2 * c + b])
        pair = pl.ds(2 * c, 2)
        keys = kb[slot, pair].reshape(PAIR, WIDTH)
        vals = vb[slot, pair].reshape(PAIR, WIDTH)
        keys_t = keys.T
        dk = jnp.zeros((PAIR, WIDTH), jnp.float32)
        dv = jnp.zeros((PAIR, WIDTH), jnp.float32)
        for t in range(CHIPS):
            spot = slice(2 * t, 2 * t + 2)
            queries = qb[slot, spot].reshape(PAIR, WIDTH)
            grads = gb[slot, spot].reshape(PAIR, WIDTH)
            norms = [auxb[slot, 2 * t + b, 0:1, :] for b in range(2)]
            delta = jnp.concatenate([auxb[slot, 2 * t + b, 4:5, :] for b in range(2)], axis=1)
            diagonal = tri[jnp.where(c == t, 1, 0)]
            scores = mm(keys, qt[t]) * (SCALE * LOG2E)
            grad_weights = mm(vals, gt[t])
            parts = []
            for kblock in range(2):
                bias = []
                for qblock in range(2):
                    later = pos_ref[2 * c + kblock] > pos_ref[2 * t + qblock]
                    row = norms[qblock] + jnp.where(later, HIDE, 0.0)
                    bias.append(row + diagonal if kblock == qblock else jnp.broadcast_to(row, (ROWS, ROWS)))
                part = scores[kblock * ROWS : (kblock + 1) * ROWS]
                parts.append(jnp.exp2(part - jnp.concatenate(bias, axis=1)))
            weights = jnp.concatenate(parts, axis=0)
            grad_scores = (weights * (grad_weights - delta)).astype(jnp.bfloat16)
            dv += mm(weights.astype(jnp.bfloat16), grads)
            dk += mm(grad_scores, queries)
            dqa[t] += mm(keys_t, grad_scores)
        dko[slot, pair] = (dk * SCALE).astype(jnp.bfloat16).reshape(2, ROWS, WIDTH)
        dvo[slot, pair] = dv.astype(jnp.bfloat16).reshape(2, ROWS, WIDTH)
        for b in range(2):
            give(DK, 2 * c + b)
            give(DV, 2 * c + b)

        @pl.when(turn == CHIPS - 1)
        def _():
            def finish(i, carry):
                c = around(i)
                done = (dqa[c] * SCALE).T.astype(jnp.bfloat16)
                dqo[slot, pl.ds(2 * c, 2)] = done.reshape(2, ROWS, WIDTH)
                for b in range(2):
                    give(DQ, 2 * c + b)
                return carry

            lax.fori_loop(0, CHIPS, finish, 0)

        return carry

    lax.fori_loop(jnp.where(two, 0, CHIPS), 2 * CHIPS, one_pair, 0)

    def drain_in(h, carry):
        owner = jnp.where(h < N, h, (h - N) * STRIDE)

        @pl.when(owner != me)
        def _():
            for kind in range(5):
                wait(sources[kind].at[h], in_send.at[kind, h])

        return carry

    lax.fori_loop(0, HEADS, drain_in, 0)

    def drain_out(step, carry):
        slot = step // N
        dest = step % N

        @pl.when(dest != me)
        def _():
            for kind in range(3):
                wait(staged[kind].at[slot, dest], out_send.at[kind, slot, dest])

        return carry

    lax.fori_loop(jnp.where(two, 0, N), 2 * N, drain_out, 0)

    def collect(h, carry):
        for kind in range(3):
            wait(results[kind].at[h], out_recv.at[kind, h])
        return carry

    lax.fori_loop(0, HEADS, collect, 0)


def body(queries, keys, values, outputs, grad_out, log_norm, block_position):
    by_head = [jnp.transpose(x, (1, 0, 2)) for x in (queries, keys, values, outputs, grad_out)]
    whole = jax.ShapeDtypeStruct((HEADS, ROWS, WIDTH), jnp.bfloat16)
    blocks = pltpu.VMEM((2, N, ROWS, WIDTH), jnp.bfloat16)
    results = pl.pallas_call(
        kernel,
        out_shape=(whole, whole, whole),
        in_specs=[pl.BlockSpec(memory_space=pl.ANY)] * 5
        + [pl.BlockSpec(memory_space=pltpu.VMEM), pl.BlockSpec(memory_space=pltpu.SMEM)],
        out_specs=[pl.BlockSpec(memory_space=pl.ANY)] * 3,
        scratch_shapes=[
            blocks, blocks, blocks, blocks,
            pltpu.VMEM((2, N, 8, ROWS), jnp.float32),
            pltpu.VMEM((HEADS, ROWS, WIDTH), jnp.bfloat16),
            pltpu.VMEM((HEADS, ROWS, WIDTH), jnp.bfloat16),
            pltpu.VMEM((HEADS, 8, ROWS), jnp.float32),
            pltpu.VMEM((CHIPS, WIDTH, PAIR), jnp.bfloat16),
            pltpu.VMEM((CHIPS, WIDTH, PAIR), jnp.bfloat16),
            pltpu.VMEM((2, ROWS, ROWS), jnp.float32),
            pltpu.VMEM((CHIPS, WIDTH, PAIR), jnp.float32),
            blocks, blocks, blocks,
            pltpu.SemaphoreType.DMA((2,)),
            pltpu.SemaphoreType.DMA((5, HEADS)),
            pltpu.SemaphoreType.DMA((5, 2, N)),
            pltpu.SemaphoreType.DMA((3, 2, N)),
            pltpu.SemaphoreType.DMA((3, HEADS)),
        ],
        compiler_params=pltpu.CompilerParams(
            collective_id=0, has_side_effects=True, vmem_limit_bytes=62 * 1024 * 1024
        ),
        name="attention_backward",
    )(*by_head, log_norm.T, block_position)
    return tuple(jnp.transpose(x, (1, 0, 2)) for x in results)


def solution(mesh):
    rows = P(("seq", "ctx"), None, None)
    return jax.shard_map(
        body,
        mesh=mesh,
        in_specs=(rows, rows, rows, rows, rows, P(("seq", "ctx"), None), P("seq")),
        out_specs=(rows, rows, rows),
        check_vma=False,
    )
```

```python
import math

import jax
import jax.numpy as jnp
from jax import lax
from jax.experimental import pallas as pl
from jax.experimental.pallas import tpu as pltpu
from jax.sharding import PartitionSpec as P

N = 16
ROWS = 128
WIDTH = 128
HEADS = 20
EXTRA = HEADS - N
STRIDE = N // EXTRA
CHIPS = N // 2
PAIR = 2 * ROWS
LOG2E = math.log2(math.e)
SCALE = 1.0 / math.sqrt(WIDTH)
HIDE = 1e30
K, V, Q, G, AUX = range(5)
DQ, DK, DV = range(3)


def swing(step):
    return (step + 1) // 2 * (2 * (step % 2) - 1)


def mm(a, b):
    return lax.dot_general(a, b, (((1,), (0,)), ((), ())), preferred_element_type=jnp.float32)


def mm_nt(a, b):
    return lax.dot_general(a, b, (((1,), (1,)), ((), ())), preferred_element_type=jnp.float32)


def kernel(
    q_ref, k_ref, v_ref, o_ref, g_ref, ln_ref, pos_ref,
    dq_ref, dk_ref, dv_ref,
    kb, vb, qb, gb, auxb, ov, gv, auxs, qt, gt, tri, dqa, dqo, dko, dvo,
    load_sem, in_send, in_recv, out_send, out_recv,
):
    me = lax.axis_index("ctx")
    chip = me // 2
    sign = 1 - 2 * (me % 2)
    two = me % STRIDE == 0
    extra_head = N + me // STRIDE
    sources = (k_ref, v_ref, q_ref, g_ref, auxs)
    landing = (kb, vb, qb, gb, auxb)
    staged = (dqo, dko, dvo)
    results = (dq_ref, dk_ref, dv_ref)

    def wait(ref, sem):
        pltpu.make_async_copy(ref, ref, sem).wait()

    def send(kind, head, slot, dest):
        pltpu.make_async_remote_copy(
            src_ref=sources[kind].at[head],
            dst_ref=landing[kind].at[slot, me],
            send_sem=in_send.at[kind, head],
            recv_sem=in_recv.at[kind, slot, me],
            device_id={"ctx": dest},
            device_id_type=pl.DeviceIdType.MESH,
        ).start()

    def keep(kind, head, slot):
        pltpu.make_async_copy(
            sources[kind].at[head], landing[kind].at[slot, me], in_recv.at[kind, slot, me]
        ).start()

    def send_extra(kinds):
        def one(i, carry):
            which = (me // STRIDE + i) % EXTRA
            dest = which * STRIDE

            @pl.when(dest != me)
            def _():
                for kind in kinds:
                    send(kind, N + which, 0, dest)

            @pl.when(dest == me)
            def _():
                for kind in kinds:
                    keep(kind, N + which, 0)

            return carry

        lax.fori_loop(0, EXTRA, one, 0)

    def send_main(kinds):
        for kind in kinds:
            keep(kind, me, 1)

        def one(i, carry):
            dest = (me + sign * swing(i) + N) % N
            for kind in kinds:
                send(kind, dest, 1, dest)
            return carry

        lax.fori_loop(1, N, one, 0)

    load_g = pltpu.make_async_copy(g_ref, gv, load_sem.at[0])
    load_o = pltpu.make_async_copy(o_ref, ov, load_sem.at[1])
    load_g.start()
    load_o.start()
    barrier = pltpu.get_barrier_semaphore()

    def greet(i, carry):
        pl.semaphore_signal(
            barrier, inc=1, device_id={"ctx": (me + i) % N}, device_id_type=pl.DeviceIdType.MESH
        )
        return carry

    lax.fori_loop(1, N, greet, 0)
    pl.semaphore_wait(barrier, N - 1)

    send_extra((Q, G))

    load_g.wait()
    load_o.wait()
    norm = ln_ref[...].astype(jnp.float32) * LOG2E
    ones = jnp.ones((8, WIDTH), jnp.bfloat16)
    upper = lax.broadcasted_iota(jnp.int32, (8, ROWS), 0) < 4
    for h in range(HEADS):
        product = gv[h].astype(jnp.float32) * ov[h].astype(jnp.float32)
        high = product.astype(jnp.bfloat16)
        low = (product - high.astype(jnp.float32)).astype(jnp.bfloat16)
        delta = (mm_nt(ones, high) + mm_nt(ones, low)).astype(jnp.bfloat16).astype(jnp.float32)
        auxs[h] = jnp.where(upper, norm[h : h + 1, :], delta)
    send_extra((AUX,))
    send_main((AUX,))
    send_extra((K, V))
    send_main((Q, G))
    send_main((K, V))

    below = lax.broadcasted_iota(jnp.int32, (ROWS, ROWS), 0) > lax.broadcasted_iota(
        jnp.int32, (ROWS, ROWS), 1
    )
    tri[0] = jnp.zeros((ROWS, ROWS), jnp.float32)
    tri[1] = jnp.where(below, HIDE, 0.0)

    def one_pair(step, carry):
        slot = step // CHIPS
        turn = step % CHIPS
        head = jnp.where(slot == 0, extra_head, me)

        def give(kind, dest):
            src = staged[kind].at[slot, dest]
            dst = results[kind].at[head]

            @pl.when(dest != me)
            def _():
                pltpu.make_async_remote_copy(
                    src_ref=src,
                    dst_ref=dst,
                    send_sem=out_send.at[kind, slot, dest],
                    recv_sem=out_recv.at[kind, head],
                    device_id={"ctx": dest},
                    device_id_type=pl.DeviceIdType.MESH,
                ).start()

            @pl.when(dest == me)
            def _():
                pltpu.make_async_copy(src, dst, out_recv.at[kind, head]).start()

        def around(i):
            return (chip + sign * swing(i) + CHIPS) % CHIPS

        @pl.when(turn == 0)
        def _():
            dqa[...] = jnp.zeros_like(dqa)

            def arrived(i, carry):
                c = around(i)
                for b in range(2):
                    for kind in (AUX, Q, G):
                        wait(landing[kind].at[slot, 2 * c + b], in_recv.at[kind, slot, 2 * c + b])
                qt[c] = qb[slot, pl.ds(2 * c, 2)].reshape(PAIR, WIDTH).T
                gt[c] = gb[slot, pl.ds(2 * c, 2)].reshape(PAIR, WIDTH).T
                return carry

            lax.fori_loop(0, CHIPS, arrived, 0)

        c = around(turn)
        for b in range(2):
            for kind in (K, V):
                wait(landing[kind].at[slot, 2 * c + b], in_recv.at[kind, slot, 2 * c + b])
        pair = pl.ds(2 * c, 2)
        keys = kb[slot, pair].reshape(PAIR, WIDTH)
        vals = vb[slot, pair].reshape(PAIR, WIDTH)
        keys_t = keys.T
        dk = jnp.zeros((PAIR, WIDTH), jnp.float32)
        dv = jnp.zeros((PAIR, WIDTH), jnp.float32)
        for t in range(CHIPS):
            spot = slice(2 * t, 2 * t + 2)
            queries = qb[slot, spot].reshape(PAIR, WIDTH)
            grads = gb[slot, spot].reshape(PAIR, WIDTH)
            norms = [auxb[slot, 2 * t + b, 0:1, :] for b in range(2)]
            delta = jnp.concatenate([auxb[slot, 2 * t + b, 4:5, :] for b in range(2)], axis=1)
            diagonal = tri[jnp.where(c == t, 1, 0)]
            scores = mm(keys, qt[t]) * (SCALE * LOG2E)
            grad_weights = mm(vals, gt[t])
            parts = []
            for kblock in range(2):
                bias = []
                for qblock in range(2):
                    later = pos_ref[2 * c + kblock] > pos_ref[2 * t + qblock]
                    row = norms[qblock] + jnp.where(later, HIDE, 0.0)
                    bias.append(row + diagonal if kblock == qblock else jnp.broadcast_to(row, (ROWS, ROWS)))
                part = scores[kblock * ROWS : (kblock + 1) * ROWS]
                parts.append(jnp.exp2(part - jnp.concatenate(bias, axis=1)))
            weights = jnp.concatenate(parts, axis=0)
            grad_scores = (weights * (grad_weights - delta)).astype(jnp.bfloat16)
            dv += mm(weights.astype(jnp.bfloat16), grads)
            dk += mm(grad_scores, queries)
            dqa[t] += mm(keys_t, grad_scores)
        dko[slot, pair] = (dk * SCALE).astype(jnp.bfloat16).reshape(2, ROWS, WIDTH)
        dvo[slot, pair] = dv.astype(jnp.bfloat16).reshape(2, ROWS, WIDTH)
        for b in range(2):
            give(DK, 2 * c + b)
            give(DV, 2 * c + b)

        @pl.when(turn == CHIPS - 1)
        def _():
            def finish(i, carry):
                c = around(i)
                done = (dqa[c] * SCALE).T.astype(jnp.bfloat16)
                dqo[slot, pl.ds(2 * c, 2)] = done.reshape(2, ROWS, WIDTH)
                for b in range(2):
                    give(DQ, 2 * c + b)
                return carry

            lax.fori_loop(0, CHIPS, finish, 0)

        return carry

    lax.fori_loop(jnp.where(two, 0, CHIPS), 2 * CHIPS, one_pair, 0)

    def drain_in(h, carry):
        owner = jnp.where(h < N, h, (h - N) * STRIDE)

        @pl.when(owner != me)
        def _():
            for kind in range(5):
                wait(sources[kind].at[h], in_send.at[kind, h])

        return carry

    lax.fori_loop(0, HEADS, drain_in, 0)

    def drain_out(step, carry):
        slot = step // N
        dest = step % N

        @pl.when(dest != me)
        def _():
            for kind in range(3):
                wait(staged[kind].at[slot, dest], out_send.at[kind, slot, dest])

        return carry

    lax.fori_loop(jnp.where(two, 0, N), 2 * N, drain_out, 0)

    def collect(h, carry):
        for kind in range(3):
            wait(results[kind].at[h], out_recv.at[kind, h])
        return carry

    lax.fori_loop(0, HEADS, collect, 0)


def hand_on(dq_ref, dk_ref, dv_ref, dq_out, dk_out, dv_out, sem):
    copies = [
        pltpu.make_async_copy(src, dst, sem.at[i])
        for i, (src, dst) in enumerate(((dq_ref, dq_out), (dk_ref, dk_out), (dv_ref, dv_out)))
    ]
    for copy in copies:
        copy.start()
    for copy in copies:
        copy.wait()


def body(queries, keys, values, outputs, grad_out, log_norm, block_position):
    by_head = [jnp.transpose(x, (1, 0, 2)) for x in (queries, keys, values, outputs, grad_out)]
    whole = jax.ShapeDtypeStruct((HEADS, ROWS, WIDTH), jnp.bfloat16)
    blocks = pltpu.VMEM((2, N, ROWS, WIDTH), jnp.bfloat16)
    results = pl.pallas_call(
        kernel,
        out_shape=(whole, whole, whole),
        in_specs=[pl.BlockSpec(memory_space=pl.ANY)] * 5
        + [pl.BlockSpec(memory_space=pltpu.VMEM), pl.BlockSpec(memory_space=pltpu.SMEM)],
        out_specs=[pl.BlockSpec(memory_space=pl.ANY)] * 3,
        scratch_shapes=[
            blocks, blocks, blocks, blocks,
            pltpu.VMEM((2, N, 8, ROWS), jnp.float32),
            pltpu.VMEM((HEADS, ROWS, WIDTH), jnp.bfloat16),
            pltpu.VMEM((HEADS, ROWS, WIDTH), jnp.bfloat16),
            pltpu.VMEM((HEADS, 8, ROWS), jnp.float32),
            pltpu.VMEM((CHIPS, WIDTH, PAIR), jnp.bfloat16),
            pltpu.VMEM((CHIPS, WIDTH, PAIR), jnp.bfloat16),
            pltpu.VMEM((2, ROWS, ROWS), jnp.float32),
            pltpu.VMEM((CHIPS, WIDTH, PAIR), jnp.float32),
            blocks, blocks, blocks,
            pltpu.SemaphoreType.DMA((2,)),
            pltpu.SemaphoreType.DMA((5, HEADS)),
            pltpu.SemaphoreType.DMA((5, 2, N)),
            pltpu.SemaphoreType.DMA((3, 2, N)),
            pltpu.SemaphoreType.DMA((3, HEADS)),
        ],
        compiler_params=pltpu.CompilerParams(
            collective_id=0, has_side_effects=True, vmem_limit_bytes=62 * 1024 * 1024
        ),
        name="attention_backward",
    )(*by_head, log_norm.T, block_position)
    results = pl.pallas_call(
        hand_on,
        out_shape=(whole, whole, whole),
        in_specs=[pl.BlockSpec(memory_space=pl.ANY)] * 3,
        out_specs=[pl.BlockSpec(memory_space=pl.ANY)] * 3,
        scratch_shapes=[pltpu.SemaphoreType.DMA((3,))],
        compiler_params=pltpu.CompilerParams(vmem_limit_bytes=62 * 1024 * 1024),
        name="hand_on",
    )(*results)
    return tuple(jnp.transpose(x, (1, 0, 2)) for x in results)


def solution(mesh):
    rows = P(("seq", "ctx"), None, None)
    return jax.shard_map(
        body,
        mesh=mesh,
        in_specs=(rows, rows, rows, rows, rows, P(("seq", "ctx"), None), P("seq")),
        out_specs=(rows, rows, rows),
        check_vma=False,
    )
```

```python
import math

import jax
import jax.numpy as jnp
from jax import lax
from jax.experimental import pallas as pl
from jax.experimental.pallas import tpu as pltpu
from jax.sharding import PartitionSpec as P

N = 16
ROWS = 128
WIDTH = 128
HEADS = 20
EXTRA = HEADS - N
STRIDE = N // EXTRA
CHIPS = N // 2
PIECES = 4
PAIR = 2 * ROWS
LOG2E = math.log2(math.e)
SCALE = 1.0 / math.sqrt(WIDTH)
HIDE = 1e30
K, V, Q, G, AUX = range(5)
DQ, DK, DV = range(3)


FAR_AND_NEAR = (4, 1, 5, 2, 7, 3, 6)


def arrival(step):
    offset = 0
    for i, sent in enumerate(FAR_AND_NEAR):
        offset = jnp.where(step == i + 1, CHIPS - sent, offset)
    return offset


def mm(a, b):
    return lax.dot_general(a, b, (((1,), (0,)), ((), ())), preferred_element_type=jnp.float32)


def mm_nt(a, b):
    return lax.dot_general(a, b, (((1,), (1,)), ((), ())), preferred_element_type=jnp.float32)


def kernel(
    q_ref, k_ref, v_ref, o_ref, g_ref, ln_ref, pos_ref,
    dq_ref, dk_ref, dv_ref,
    kb, vb, qb, gb, auxb, ov, gv, auxs, qt, gt, tri, dqa, dqo, dko, dvo,
    load_sem, in_send, in_recv, out_send, out_recv,
):
    me = lax.axis_index("ctx")
    chip = me // 2
    core = me % 2
    two = me % STRIDE == 0
    extra_head = N + me // STRIDE
    sources = (k_ref, v_ref, q_ref, g_ref, auxs)
    landing = (kb, vb, qb, gb, auxb)
    staged = (dqo, dko, dvo)
    results = (dq_ref, dk_ref, dv_ref)

    def wait(ref, sem):
        pltpu.make_async_copy(ref, ref, sem).wait()

    def send(kind, head, slot, dest):
        pltpu.make_async_remote_copy(
            src_ref=sources[kind].at[head],
            dst_ref=landing[kind].at[slot, me],
            send_sem=in_send.at[kind, head],
            recv_sem=in_recv.at[kind, slot, me],
            device_id={"ctx": dest},
            device_id_type=pl.DeviceIdType.MESH,
        ).start()

    def keep(kind, head, slot):
        pltpu.make_async_copy(
            sources[kind].at[head], landing[kind].at[slot, me], in_recv.at[kind, slot, me]
        ).start()

    def send_extra(kinds):
        def one(i, carry):
            which = (me // STRIDE + i) % EXTRA
            dest = which * STRIDE

            @pl.when(dest != me)
            def _():
                for kind in kinds:
                    send(kind, N + which, 0, dest)

            @pl.when(dest == me)
            def _():
                for kind in kinds:
                    keep(kind, N + which, 0)

            return carry

        lax.fori_loop(0, EXTRA, one, 0)

    def send_main(kinds):
        for kind in kinds:
            keep(kind, me, 1)

        dests = [2 * chip + 1 - core]
        for offset in FAR_AND_NEAR:
            for b in range(2):
                dests.append(2 * ((chip + offset) % CHIPS) + (core + b) % 2)
        for dest in dests:
            for kind in kinds:
                send(kind, dest, 1, dest)

    load_g = pltpu.make_async_copy(g_ref, gv, load_sem.at[0])
    load_o = pltpu.make_async_copy(o_ref, ov, load_sem.at[1])
    load_g.start()
    load_o.start()
    barrier = pltpu.get_barrier_semaphore()

    def greet(i, carry):
        pl.semaphore_signal(
            barrier, inc=1, device_id={"ctx": (me + i) % N}, device_id_type=pl.DeviceIdType.MESH
        )
        return carry

    lax.fori_loop(1, N, greet, 0)
    pl.semaphore_wait(barrier, N - 1)

    send_extra((Q, G))

    load_g.wait()
    load_o.wait()
    norm = ln_ref[...].astype(jnp.float32) * LOG2E
    ones = jnp.ones((8, WIDTH), jnp.bfloat16)
    upper = lax.broadcasted_iota(jnp.int32, (8, ROWS), 0) < 4
    for h in range(HEADS):
        product = gv[h].astype(jnp.float32) * ov[h].astype(jnp.float32)
        high = product.astype(jnp.bfloat16)
        low = (product - high.astype(jnp.float32)).astype(jnp.bfloat16)
        delta = (mm_nt(ones, high) + mm_nt(ones, low)).astype(jnp.bfloat16).astype(jnp.float32)
        auxs[h] = jnp.where(upper, norm[h : h + 1, :], delta)
    send_extra((AUX,))
    send_main((AUX,))
    send_extra((K, V))
    send_main((Q, G))
    send_main((K, V))

    below = lax.broadcasted_iota(jnp.int32, (ROWS, ROWS), 0) > lax.broadcasted_iota(
        jnp.int32, (ROWS, ROWS), 1
    )
    tri[0] = jnp.zeros((ROWS, ROWS), jnp.float32)
    tri[1] = jnp.where(below, HIDE, 0.0)

    def one_pair(step, carry):
        slot = step // CHIPS
        turn = step % CHIPS
        head = jnp.where(slot == 0, extra_head, me)

        def give(kind, dest):
            src = staged[kind].at[slot, dest]
            dst = results[kind].at[head]

            @pl.when(dest != me)
            def _():
                pltpu.make_async_remote_copy(
                    src_ref=src,
                    dst_ref=dst,
                    send_sem=out_send.at[kind, slot, dest],
                    recv_sem=out_recv.at[kind, head],
                    device_id={"ctx": dest},
                    device_id_type=pl.DeviceIdType.MESH,
                ).start()

            @pl.when(dest == me)
            def _():
                pltpu.make_async_copy(src, dst, out_recv.at[kind, head]).start()

        def around(i):
            return (chip + arrival(i)) % CHIPS

        @pl.when(turn == 0)
        def _():
            dqa[...] = jnp.zeros_like(dqa)

            def arrived(i, carry):
                c = around(i)
                for b in range(2):
                    for kind in (AUX, Q, G):
                        wait(landing[kind].at[slot, 2 * c + b], in_recv.at[kind, slot, 2 * c + b])
                qt[c] = qb[slot, pl.ds(2 * c, 2)].reshape(PAIR, WIDTH).T
                gt[c] = gb[slot, pl.ds(2 * c, 2)].reshape(PAIR, WIDTH).T
                return carry

            lax.fori_loop(0, CHIPS, arrived, 0)

        c = around(turn)
        for b in range(2):
            for kind in (K, V):
                wait(landing[kind].at[slot, 2 * c + b], in_recv.at[kind, slot, 2 * c + b])
        pair = pl.ds(2 * c, 2)
        keys = kb[slot, pair].reshape(PAIR, WIDTH)
        vals = vb[slot, pair].reshape(PAIR, WIDTH)
        keys_t = keys.T
        dk = jnp.zeros((PAIR, WIDTH), jnp.float32)
        dv = jnp.zeros((PAIR, WIDTH), jnp.float32)
        for t in range(CHIPS):
            spot = slice(2 * t, 2 * t + 2)
            queries = qb[slot, spot].reshape(PAIR, WIDTH)
            grads = gb[slot, spot].reshape(PAIR, WIDTH)
            norms = [auxb[slot, 2 * t + b, 0:1, :] for b in range(2)]
            delta = jnp.concatenate([auxb[slot, 2 * t + b, 4:5, :] for b in range(2)], axis=1)
            diagonal = tri[jnp.where(c == t, 1, 0)]
            scores = mm(keys, qt[t]) * (SCALE * LOG2E)
            grad_weights = mm(vals, gt[t])
            parts = []
            for kblock in range(2):
                bias = []
                for qblock in range(2):
                    later = pos_ref[2 * c + kblock] > pos_ref[2 * t + qblock]
                    row = norms[qblock] + jnp.where(later, HIDE, 0.0)
                    bias.append(row + diagonal if kblock == qblock else jnp.broadcast_to(row, (ROWS, ROWS)))
                part = scores[kblock * ROWS : (kblock + 1) * ROWS]
                parts.append(jnp.exp2(part - jnp.concatenate(bias, axis=1)))
            weights = jnp.concatenate(parts, axis=0)
            grad_scores = (weights * (grad_weights - delta)).astype(jnp.bfloat16)
            dv += mm(weights.astype(jnp.bfloat16), grads)
            dk += mm(grad_scores, queries)
            dqa[t] += mm(keys_t, grad_scores)
        dko[slot, pair] = (dk * SCALE).astype(jnp.bfloat16).reshape(2, ROWS, WIDTH)
        dvo[slot, pair] = dv.astype(jnp.bfloat16).reshape(2, ROWS, WIDTH)
        for b in range(2):
            give(DK, 2 * c + b)
            give(DV, 2 * c + b)

        @pl.when(turn == CHIPS - 1)
        def _():
            def finish(i, carry):
                c = around(i)
                done = (dqa[c] * SCALE).T.astype(jnp.bfloat16)
                dqo[slot, pl.ds(2 * c, 2)] = done.reshape(2, ROWS, WIDTH)
                for b in range(2):
                    give(DQ, 2 * c + b)
                return carry

            lax.fori_loop(0, CHIPS, finish, 0)

        return carry

    lax.fori_loop(jnp.where(two, 0, CHIPS), 2 * CHIPS, one_pair, 0)

    def drain_in(h, carry):
        owner = jnp.where(h < N, h, (h - N) * STRIDE)

        @pl.when(owner != me)
        def _():
            for kind in range(5):
                wait(sources[kind].at[h], in_send.at[kind, h])

        return carry

    lax.fori_loop(0, HEADS, drain_in, 0)

    def drain_out(step, carry):
        slot = step // N
        dest = step % N

        @pl.when(dest != me)
        def _():
            for kind in range(3):
                wait(staged[kind].at[slot, dest], out_send.at[kind, slot, dest])

        return carry

    lax.fori_loop(jnp.where(two, 0, N), 2 * N, drain_out, 0)

    def collect(h, carry):
        for kind in range(3):
            wait(results[kind].at[h], out_recv.at[kind, h])
        return carry

    lax.fori_loop(0, HEADS, collect, 0)


def hand_on(dq_ref, dk_ref, dv_ref, dq_out, dk_out, dv_out, held, load_sem, store_sem):
    loads, stores = [], []
    for i, (src, dst) in enumerate(((dq_ref, dq_out), (dk_ref, dk_out), (dv_ref, dv_out))):
        for j in range(PIECES):
            part = pl.ds(j * (HEADS // PIECES), HEADS // PIECES)
            loads.append(pltpu.make_async_copy(src.at[part], held.at[i, part], load_sem.at[i, j]))
            stores.append(pltpu.make_async_copy(held.at[i, part], dst.at[part], store_sem.at[i, j]))
    for load in loads:
        load.start()
    for load, store in zip(loads, stores):
        load.wait()
        store.start()
    for store in stores:
        store.wait()


def body(queries, keys, values, outputs, grad_out, log_norm, block_position):
    by_head = [jnp.transpose(x, (1, 0, 2)) for x in (queries, keys, values, outputs, grad_out)]
    whole = jax.ShapeDtypeStruct((HEADS, ROWS, WIDTH), jnp.bfloat16)
    blocks = pltpu.VMEM((2, N, ROWS, WIDTH), jnp.bfloat16)
    results = pl.pallas_call(
        kernel,
        out_shape=(whole, whole, whole),
        in_specs=[pl.BlockSpec(memory_space=pl.ANY)] * 5
        + [pl.BlockSpec(memory_space=pltpu.VMEM), pl.BlockSpec(memory_space=pltpu.SMEM)],
        out_specs=[pl.BlockSpec(memory_space=pl.ANY)] * 3,
        scratch_shapes=[
            blocks, blocks, blocks, blocks,
            pltpu.VMEM((2, N, 8, ROWS), jnp.float32),
            pltpu.VMEM((HEADS, ROWS, WIDTH), jnp.bfloat16),
            pltpu.VMEM((HEADS, ROWS, WIDTH), jnp.bfloat16),
            pltpu.VMEM((HEADS, 8, ROWS), jnp.float32),
            pltpu.VMEM((CHIPS, WIDTH, PAIR), jnp.bfloat16),
            pltpu.VMEM((CHIPS, WIDTH, PAIR), jnp.bfloat16),
            pltpu.VMEM((2, ROWS, ROWS), jnp.float32),
            pltpu.VMEM((CHIPS, WIDTH, PAIR), jnp.float32),
            blocks, blocks, blocks,
            pltpu.SemaphoreType.DMA((2,)),
            pltpu.SemaphoreType.DMA((5, HEADS)),
            pltpu.SemaphoreType.DMA((5, 2, N)),
            pltpu.SemaphoreType.DMA((3, 2, N)),
            pltpu.SemaphoreType.DMA((3, HEADS)),
        ],
        compiler_params=pltpu.CompilerParams(
            collective_id=0, has_side_effects=True, vmem_limit_bytes=62 * 1024 * 1024
        ),
        name="attention_backward",
    )(*by_head, log_norm.T, block_position)
    results = pl.pallas_call(
        hand_on,
        out_shape=(whole, whole, whole),
        in_specs=[pl.BlockSpec(memory_space=pl.ANY)] * 3,
        out_specs=[pl.BlockSpec(memory_space=pl.ANY)] * 3,
        scratch_shapes=[
            pltpu.VMEM((3, HEADS, ROWS, WIDTH), jnp.bfloat16),
            pltpu.SemaphoreType.DMA((3, PIECES)),
            pltpu.SemaphoreType.DMA((3, PIECES)),
        ],
        compiler_params=pltpu.CompilerParams(vmem_limit_bytes=62 * 1024 * 1024),
        name="hand_on",
    )(*results)
    return tuple(jnp.transpose(x, (1, 0, 2)) for x in results)


def solution(mesh):
    rows = P(("seq", "ctx"), None, None)
    return jax.shard_map(
        body,
        mesh=mesh,
        in_specs=(rows, rows, rows, rows, rows, P(("seq", "ctx"), None), P("seq")),
        out_specs=(rows, rows, rows),
        check_vma=False,
    )
```

```python
import math

import jax
import jax.numpy as jnp
from jax import lax
from jax.experimental import pallas as pl
from jax.experimental.pallas import tpu as pltpu
from jax.sharding import PartitionSpec as P

N = 16
ROWS = 128
WIDTH = 128
HEADS = 20
EXTRA = HEADS - N
CHIPS = N // 2
HALF = CHIPS // 2
PIECES = 4
PAIR = 2 * ROWS
LOG2E = math.log2(math.e)
SCALE = 1.0 / math.sqrt(WIDTH)
HIDE = 1e30
K, V, Q, G, AUX = range(5)
DQ, DK, DV = range(3)


FAR_AND_NEAR = (4, 1, 5, 2, 7, 3, 6)


def arrival(step):
    offset = 0
    for i, sent in enumerate(FAR_AND_NEAR):
        offset = jnp.where(step == i + 1, CHIPS - sent, offset)
    return offset


def mm(a, b):
    return lax.dot_general(a, b, (((1,), (0,)), ((), ())), preferred_element_type=jnp.float32)


def mm_nt(a, b):
    return lax.dot_general(a, b, (((1,), (1,)), ((), ())), preferred_element_type=jnp.float32)


def kernel(
    q_ref, k_ref, v_ref, o_ref, g_ref, ln_ref, pos_ref,
    dq_ref, dk_ref, dv_ref,
    kb, vb, qb, gb, auxb, ov, gv, auxs, qt, gt, tri, dqa, dqo, dko, dvo, dqn, part_out, part_in,
    load_sem, in_send, in_recv, fwd_send, part_send, part_recv, out_send, out_recv,
):
    me = lax.axis_index("ctx")
    chip = me // 2
    core = me % 2
    shares = core == 0
    toward = 2 * (chip % 2) - 1
    partner = me - 2 * toward
    sources = (k_ref, v_ref, q_ref, g_ref, auxs)
    landing = (kb, vb, qb, gb, auxb)
    staged = (dqo, dko, dvo)
    results = (dq_ref, dk_ref, dv_ref)

    def wait(ref, sem):
        pltpu.make_async_copy(ref, ref, sem).wait()

    def near(i):
        return (chip + toward * i + CHIPS) % CHIPS

    def far(i):
        return (chip - toward * (i + 1) + CHIPS) % CHIPS

    def nearer(which):
        offset = (chip - 2 * which + CHIPS) % CHIPS
        side = jnp.where((offset >= 1) & (offset <= CHIPS // 2), 1, 0)
        return 2 * (2 * which + side)

    def send(kind, head, slot, dest):
        pltpu.make_async_remote_copy(
            src_ref=sources[kind].at[head],
            dst_ref=landing[kind].at[slot, me],
            send_sem=in_send.at[kind, head],
            recv_sem=in_recv.at[kind, slot, me],
            device_id={"ctx": dest},
            device_id_type=pl.DeviceIdType.MESH,
        ).start()

    def keep(kind, head, slot):
        pltpu.make_async_copy(
            sources[kind].at[head], landing[kind].at[slot, me], in_recv.at[kind, slot, me]
        ).start()

    def send_extra(kinds):
        def one(i, carry):
            which = (chip // 2 + i) % EXTRA
            dest = nearer(which)

            @pl.when(dest != me)
            def _():
                for kind in kinds:
                    send(kind, N + which, 0, dest)

            @pl.when(dest == me)
            def _():
                for kind in kinds:
                    keep(kind, N + which, 0)

            return carry

        lax.fori_loop(0, EXTRA, one, 0)

    def send_main(kinds):
        for kind in kinds:
            keep(kind, me, 1)

        dests = [2 * chip + 1 - core]
        for offset in FAR_AND_NEAR:
            for b in range(2):
                dests.append(2 * ((chip + offset) % CHIPS) + (core + b) % 2)
        for dest in dests:
            for kind in kinds:
                send(kind, dest, 1, dest)

    load_g = pltpu.make_async_copy(g_ref, gv, load_sem.at[0])
    load_o = pltpu.make_async_copy(o_ref, ov, load_sem.at[1])
    load_g.start()
    load_o.start()
    barrier = pltpu.get_barrier_semaphore()

    def greet(i, carry):
        pl.semaphore_signal(
            barrier, inc=1, device_id={"ctx": (me + i) % N}, device_id_type=pl.DeviceIdType.MESH
        )
        return carry

    lax.fori_loop(1, N, greet, 0)
    pl.semaphore_wait(barrier, N - 1)

    send_extra((Q, G))

    load_g.wait()
    load_o.wait()
    norm = ln_ref[...].astype(jnp.float32) * LOG2E
    ones = jnp.ones((8, WIDTH), jnp.bfloat16)
    upper = lax.broadcasted_iota(jnp.int32, (8, ROWS), 0) < 4
    for h in range(HEADS):
        product = gv[h].astype(jnp.float32) * ov[h].astype(jnp.float32)
        high = product.astype(jnp.bfloat16)
        low = (product - high.astype(jnp.float32)).astype(jnp.bfloat16)
        delta = (mm_nt(ones, high) + mm_nt(ones, low)).astype(jnp.bfloat16).astype(jnp.float32)
        auxs[h] = jnp.where(upper, norm[h : h + 1, :], delta)
    send_extra((AUX,))
    send_main((AUX,))
    send_extra((K, V))

    @pl.when(shares)
    def _():
        def forward(i, carry):
            for b in range(2):
                block = 2 * near(i) + b
                for kind in (AUX, Q, G):
                    wait(landing[kind].at[0, block], in_recv.at[kind, 0, block])
                    pltpu.make_async_remote_copy(
                        src_ref=landing[kind].at[0, block],
                        dst_ref=landing[kind].at[0, block],
                        send_sem=fwd_send.at[kind - Q, block],
                        recv_sem=in_recv.at[kind, 0, block],
                        device_id={"ctx": partner},
                        device_id_type=pl.DeviceIdType.MESH,
                    ).start()
            return carry

        lax.fori_loop(0, HALF, forward, 0)

    send_main((Q, G))
    send_main((K, V))

    below = lax.broadcasted_iota(jnp.int32, (ROWS, ROWS), 0) > lax.broadcasted_iota(
        jnp.int32, (ROWS, ROWS), 1
    )
    tri[0] = jnp.zeros((ROWS, ROWS), jnp.float32)
    tri[1] = jnp.where(below, HIDE, 0.0)

    def give(kind, slot, head, dest):
        src = staged[kind].at[slot, dest]
        dst = results[kind].at[head]

        @pl.when(dest != me)
        def _():
            pltpu.make_async_remote_copy(
                src_ref=src,
                dst_ref=dst,
                send_sem=out_send.at[kind, slot, dest],
                recv_sem=out_recv.at[kind, head],
                device_id={"ctx": dest},
                device_id_type=pl.DeviceIdType.MESH,
            ).start()

        @pl.when(dest == me)
        def _():
            pltpu.make_async_copy(src, dst, out_recv.at[kind, head]).start()

    def around(i):
        return (chip + arrival(i)) % CHIPS

    def pass_part(i):
        return pltpu.make_async_remote_copy(
            src_ref=part_out.at[i],
            dst_ref=part_in.at[i],
            send_sem=part_send.at[i],
            recv_sem=part_recv.at[i],
            device_id={"ctx": partner},
            device_id_type=pl.DeviceIdType.MESH,
        )

    def turned(slot, c):
        qt[c] = qb[slot, pl.ds(2 * c, 2)].reshape(PAIR, WIDTH).T
        gt[c] = gb[slot, pl.ds(2 * c, 2)].reshape(PAIR, WIDTH).T

    def queries_arrived(slot, c):
        for b in range(2):
            for kind in (AUX, Q, G):
                wait(landing[kind].at[slot, 2 * c + b], in_recv.at[kind, slot, 2 * c + b])
        turned(slot, c)

    def one_pair(step, carry):
        slot = jnp.where(step < HALF, 0, 1)
        turn = step - HALF * slot
        head = jnp.where(slot == 0, N + chip // 2, me)

        @pl.when(turn == 0)
        def _():
            dqa[...] = jnp.zeros_like(dqa)

        @pl.when(step == 0)
        def _():
            def ready(i, carry):
                turned(0, near(i))
                queries_arrived(0, far(i))
                return carry

            lax.fori_loop(0, HALF, ready, 0)

        @pl.when(step == HALF)
        def _():
            def ready(i, carry):
                queries_arrived(1, around(i))
                return carry

            lax.fori_loop(0, CHIPS, ready, 0)

        c = jnp.where(slot == 0, near(turn), around(turn))
        for b in range(2):
            for kind in (K, V):
                wait(landing[kind].at[slot, 2 * c + b], in_recv.at[kind, slot, 2 * c + b])
        pair = pl.ds(2 * c, 2)
        keys = kb[slot, pair].reshape(PAIR, WIDTH)
        vals = vb[slot, pair].reshape(PAIR, WIDTH)
        keys_t = keys.T
        dk = jnp.zeros((PAIR, WIDTH), jnp.float32)
        dv = jnp.zeros((PAIR, WIDTH), jnp.float32)
        for t in range(CHIPS):
            spot = slice(2 * t, 2 * t + 2)
            queries = qb[slot, spot].reshape(PAIR, WIDTH)
            grads = gb[slot, spot].reshape(PAIR, WIDTH)
            norms = [auxb[slot, 2 * t + b, 0:1, :] for b in range(2)]
            delta = jnp.concatenate([auxb[slot, 2 * t + b, 4:5, :] for b in range(2)], axis=1)
            diagonal = tri[jnp.where(c == t, 1, 0)]
            scores = mm(keys, qt[t]) * (SCALE * LOG2E)
            grad_weights = mm(vals, gt[t])
            parts = []
            for kblock in range(2):
                bias = []
                for qblock in range(2):
                    later = pos_ref[2 * c + kblock] > pos_ref[2 * t + qblock]
                    row = norms[qblock] + jnp.where(later, HIDE, 0.0)
                    bias.append(row + diagonal if kblock == qblock else jnp.broadcast_to(row, (ROWS, ROWS)))
                part = scores[kblock * ROWS : (kblock + 1) * ROWS]
                parts.append(jnp.exp2(part - jnp.concatenate(bias, axis=1)))
            weights = jnp.concatenate(parts, axis=0)
            grad_scores = (weights * (grad_weights - delta)).astype(jnp.bfloat16)
            dv += mm(weights.astype(jnp.bfloat16), grads)
            dk += mm(grad_scores, queries)
            dqa[t] += mm(keys_t, grad_scores)
        dko[slot, pair] = (dk * SCALE).astype(jnp.bfloat16).reshape(2, ROWS, WIDTH)
        dvo[slot, pair] = dv.astype(jnp.bfloat16).reshape(2, ROWS, WIDTH)
        for b in range(2):
            give(DK, slot, head, 2 * c + b)
            give(DV, slot, head, 2 * c + b)

        @pl.when(step == HALF - 1)
        def _():
            def part(i, carry):
                part_out[i] = dqa[far(i)].T.astype(jnp.bfloat16)
                pass_part(i).start()
                dqn[i] = dqa[near(i)].T
                return carry

            lax.fori_loop(0, HALF, part, 0)

        @pl.when(shares & (step == HALF + 5))
        def _():
            def total(i, carry):
                pass_part(i).wait_recv()
                done = ((dqn[i] + part_in[i].astype(jnp.float32)) * SCALE).astype(jnp.bfloat16)
                c = near(i)
                dqo[0, pl.ds(2 * c, 2)] = done.reshape(2, ROWS, WIDTH)
                for b in range(2):
                    give(DQ, 0, N + chip // 2, 2 * c + b)
                return carry

            lax.fori_loop(0, HALF, total, 0)

        @pl.when(step == HALF + CHIPS - 1)
        def _():
            def finish(i, carry):
                c = around(i)
                done = (dqa[c] * SCALE).T.astype(jnp.bfloat16)
                dqo[1, pl.ds(2 * c, 2)] = done.reshape(2, ROWS, WIDTH)
                for b in range(2):
                    give(DQ, 1, me, 2 * c + b)
                return carry

            lax.fori_loop(0, CHIPS, finish, 0)

        return carry

    lax.fori_loop(jnp.where(shares, 0, HALF), HALF + CHIPS, one_pair, 0)

    def drain_in(h, carry):
        owner = jnp.where(h < N, h, nearer(jnp.maximum(h - N, 0)))

        @pl.when(owner != me)
        def _():
            for kind in range(5):
                wait(sources[kind].at[h], in_send.at[kind, h])

        return carry

    lax.fori_loop(0, HEADS, drain_in, 0)

    def drain_out(slot, dest):
        @pl.when(dest != me)
        def _():
            for kind in range(3):
                wait(staged[kind].at[slot, dest], out_send.at[kind, slot, dest])

    def drain_main(dest, carry):
        drain_out(1, dest)
        return carry

    lax.fori_loop(0, N, drain_main, 0)

    @pl.when(shares)
    def _():
        def drain_shared(i, carry):
            pass_part(i).wait_send()
            for b in range(2):
                block = 2 * near(i) + b
                drain_out(0, block)
                for kind in (AUX, Q, G):
                    wait(landing[kind].at[0, block], fwd_send.at[kind - Q, block])
            return carry

        lax.fori_loop(0, HALF, drain_shared, 0)

    def collect(h, carry):
        for kind in range(3):
            wait(results[kind].at[h], out_recv.at[kind, h])
        return carry

    lax.fori_loop(0, HEADS, collect, 0)


def hand_on(dq_ref, dk_ref, dv_ref, dq_out, dk_out, dv_out, held, load_sem, store_sem):
    loads, stores = [], []
    for i, (src, dst) in enumerate(((dq_ref, dq_out), (dk_ref, dk_out), (dv_ref, dv_out))):
        for j in range(PIECES):
            part = pl.ds(j * (HEADS // PIECES), HEADS // PIECES)
            loads.append(pltpu.make_async_copy(src.at[part], held.at[i, part], load_sem.at[i, j]))
            stores.append(pltpu.make_async_copy(held.at[i, part], dst.at[part], store_sem.at[i, j]))
    for load in loads:
        load.start()
    for load, store in zip(loads, stores):
        load.wait()
        store.start()
    for store in stores:
        store.wait()


def body(queries, keys, values, outputs, grad_out, log_norm, block_position):
    by_head = [jnp.transpose(x, (1, 0, 2)) for x in (queries, keys, values, outputs, grad_out)]
    whole = jax.ShapeDtypeStruct((HEADS, ROWS, WIDTH), jnp.bfloat16)
    blocks = pltpu.VMEM((2, N, ROWS, WIDTH), jnp.bfloat16)
    results = pl.pallas_call(
        kernel,
        out_shape=(whole, whole, whole),
        in_specs=[pl.BlockSpec(memory_space=pl.ANY)] * 5
        + [pl.BlockSpec(memory_space=pltpu.VMEM), pl.BlockSpec(memory_space=pltpu.SMEM)],
        out_specs=[pl.BlockSpec(memory_space=pl.ANY)] * 3,
        scratch_shapes=[
            blocks, blocks, blocks, blocks,
            pltpu.VMEM((2, N, 8, ROWS), jnp.float32),
            pltpu.VMEM((HEADS, ROWS, WIDTH), jnp.bfloat16),
            pltpu.VMEM((HEADS, ROWS, WIDTH), jnp.bfloat16),
            pltpu.VMEM((HEADS, 8, ROWS), jnp.float32),
            pltpu.VMEM((CHIPS, WIDTH, PAIR), jnp.bfloat16),
            pltpu.VMEM((CHIPS, WIDTH, PAIR), jnp.bfloat16),
            pltpu.VMEM((2, ROWS, ROWS), jnp.float32),
            pltpu.VMEM((CHIPS, WIDTH, PAIR), jnp.float32),
            blocks, blocks, blocks,
            pltpu.VMEM((HALF, PAIR, WIDTH), jnp.float32),
            pltpu.VMEM((HALF, PAIR, WIDTH), jnp.bfloat16),
            pltpu.VMEM((HALF, PAIR, WIDTH), jnp.bfloat16),
            pltpu.SemaphoreType.DMA((2,)),
            pltpu.SemaphoreType.DMA((5, HEADS)),
            pltpu.SemaphoreType.DMA((5, 2, N)),
            pltpu.SemaphoreType.DMA((3, N)),
            pltpu.SemaphoreType.DMA((HALF,)),
            pltpu.SemaphoreType.DMA((HALF,)),
            pltpu.SemaphoreType.DMA((3, 2, N)),
            pltpu.SemaphoreType.DMA((3, HEADS)),
        ],
        compiler_params=pltpu.CompilerParams(
            collective_id=0, has_side_effects=True, vmem_limit_bytes=62 * 1024 * 1024
        ),
        name="attention_backward",
    )(*by_head, log_norm.T, block_position)
    results = pl.pallas_call(
        hand_on,
        out_shape=(whole, whole, whole),
        in_specs=[pl.BlockSpec(memory_space=pl.ANY)] * 3,
        out_specs=[pl.BlockSpec(memory_space=pl.ANY)] * 3,
        scratch_shapes=[
            pltpu.VMEM((3, HEADS, ROWS, WIDTH), jnp.bfloat16),
            pltpu.SemaphoreType.DMA((3, PIECES)),
            pltpu.SemaphoreType.DMA((3, PIECES)),
        ],
        compiler_params=pltpu.CompilerParams(vmem_limit_bytes=62 * 1024 * 1024),
        name="hand_on",
    )(*results)
    return tuple(jnp.transpose(x, (1, 0, 2)) for x in results)


def solution(mesh):
    rows = P(("seq", "ctx"), None, None)
    return jax.shard_map(
        body,
        mesh=mesh,
        in_specs=(rows, rows, rows, rows, rows, P(("seq", "ctx"), None), P("seq")),
        out_specs=(rows, rows, rows),
        check_vma=False,
    )
```

```python
import math

import jax
import jax.numpy as jnp
from jax import lax
from jax.experimental import pallas as pl
from jax.experimental.pallas import tpu as pltpu
from jax.sharding import PartitionSpec as P

N = 16
ROWS = 128
WIDTH = 128
HEADS = 20
EXTRA = HEADS - N
CHIPS = N // 2
HALF = CHIPS // 2
PIECES = 4
PAIR = 2 * ROWS
LOG2E = math.log2(math.e)
SCALE = 1.0 / math.sqrt(WIDTH)
HIDE = 1e30
K, V, Q, G, AUX = range(5)
DQ, DK, DV = range(3)


FAR_AND_NEAR = (1, 5, 2, 7, 3, 6, 4)


def arrival(step):
    offset = 0
    for i, sent in enumerate(FAR_AND_NEAR):
        offset = jnp.where(step == i + 1, CHIPS - sent, offset)
    return offset


def mm(a, b):
    return lax.dot_general(a, b, (((1,), (0,)), ((), ())), preferred_element_type=jnp.float32)


def mm_nt(a, b):
    return lax.dot_general(a, b, (((1,), (1,)), ((), ())), preferred_element_type=jnp.float32)


def kernel(
    q_ref, k_ref, v_ref, o_ref, g_ref, ln_ref, pos_ref,
    dq_ref, dk_ref, dv_ref,
    kb, vb, qb, gb, auxb, ov, gv, auxs, qt, gt, tri, dqa, dqo, dko, dvo, dqn, part_out, part_in, pass_in, pass_out,
    load_sem, in_send, in_recv, fwd_send, part_send, part_recv, out_send, out_recv,
    pass_in_send, pass_in_recv, pass_out_send, pass_out_recv,
):
    me = lax.axis_index("ctx")
    chip = me // 2
    core = me % 2
    shares = core == 0
    toward = 2 * (chip % 2) - 1
    partner = me - 2 * toward
    way = 2 - 4 * core
    opposite = (chip + HALF) % CHIPS
    by = 2 * ((chip + way + CHIPS) % CHIPS) + core
    passed_from = 2 * ((chip - way + CHIPS) % CHIPS) + core

    def passed_to(b):
        return 2 * ((chip + way + CHIPS) % CHIPS) + (core + b) % 2

    def remote(src, dst, send_sem, recv_sem, dest):
        return pltpu.make_async_remote_copy(
            src_ref=src,
            dst_ref=dst,
            send_sem=send_sem,
            recv_sem=recv_sem,
            device_id={"ctx": dest},
            device_id_type=pl.DeviceIdType.MESH,
        )
    sources = (k_ref, v_ref, q_ref, g_ref, auxs)
    landing = (kb, vb, qb, gb, auxb)
    staged = (dqo, dko, dvo)
    results = (dq_ref, dk_ref, dv_ref)

    def wait(ref, sem):
        pltpu.make_async_copy(ref, ref, sem).wait()

    def near(i):
        return (chip + toward * i + CHIPS) % CHIPS

    def far(i):
        return (chip - toward * (i + 1) + CHIPS) % CHIPS

    def nearer(which):
        offset = (chip - 2 * which + CHIPS) % CHIPS
        side = jnp.where((offset >= 1) & (offset <= CHIPS // 2), 1, 0)
        return 2 * (2 * which + side)

    def send(kind, head, slot, dest):
        pltpu.make_async_remote_copy(
            src_ref=sources[kind].at[head],
            dst_ref=landing[kind].at[slot, me],
            send_sem=in_send.at[kind, head],
            recv_sem=in_recv.at[kind, slot, me],
            device_id={"ctx": dest},
            device_id_type=pl.DeviceIdType.MESH,
        ).start()

    def keep(kind, head, slot):
        pltpu.make_async_copy(
            sources[kind].at[head], landing[kind].at[slot, me], in_recv.at[kind, slot, me]
        ).start()

    def send_extra(kinds):
        def one(i, carry):
            which = (chip // 2 + i) % EXTRA
            dest = nearer(which)

            @pl.when(dest != me)
            def _():
                for kind in kinds:
                    send(kind, N + which, 0, dest)

            @pl.when(dest == me)
            def _():
                for kind in kinds:
                    keep(kind, N + which, 0)

            return carry

        lax.fori_loop(0, EXTRA, one, 0)

    def send_main(kinds):
        for kind in kinds:
            keep(kind, me, 1)

        if AUX not in kinds:
            for b in range(2):
                dest = 2 * opposite + (core + b) % 2
                for kind in kinds:
                    remote(
                        sources[kind].at[dest], pass_in.at[kind, b],
                        in_send.at[kind, dest], pass_in_recv.at[kind, b], by,
                    ).start()
        dests = [2 * chip + 1 - core]
        for offset in FAR_AND_NEAR:
            if offset != HALF or AUX in kinds:
                for b in range(2):
                    dests.append(2 * ((chip + offset) % CHIPS) + (core + b) % 2)
        for dest in dests:
            for kind in kinds:
                send(kind, dest, 1, dest)

    def pass_inputs(kinds):
        for b in range(2):
            for kind in kinds:
                wait(pass_in.at[kind, b], pass_in_recv.at[kind, b])
                remote(
                    pass_in.at[kind, b], landing[kind].at[1, passed_from],
                    pass_in_send.at[kind, b], in_recv.at[kind, 1, passed_from], passed_to(b),
                ).start()

    def pass_results(kinds):
        for kind in kinds:
            for b in range(2):
                wait(pass_out.at[kind, b], pass_out_recv.at[kind, b])
                remote(
                    pass_out.at[kind, b], results[kind].at[passed_from],
                    pass_out_send.at[kind, b], out_recv.at[kind, passed_from], passed_to(b),
                ).start()

    load_g = pltpu.make_async_copy(g_ref, gv, load_sem.at[0])
    load_o = pltpu.make_async_copy(o_ref, ov, load_sem.at[1])
    load_g.start()
    load_o.start()
    barrier = pltpu.get_barrier_semaphore()

    def greet(i, carry):
        pl.semaphore_signal(
            barrier, inc=1, device_id={"ctx": (me + i) % N}, device_id_type=pl.DeviceIdType.MESH
        )
        return carry

    lax.fori_loop(1, N, greet, 0)
    pl.semaphore_wait(barrier, N - 1)

    send_extra((Q, G))

    load_g.wait()
    load_o.wait()
    norm = ln_ref[...].astype(jnp.float32) * LOG2E
    ones = jnp.ones((8, WIDTH), jnp.bfloat16)
    upper = lax.broadcasted_iota(jnp.int32, (8, ROWS), 0) < 4
    for h in range(HEADS):
        product = gv[h].astype(jnp.float32) * ov[h].astype(jnp.float32)
        high = product.astype(jnp.bfloat16)
        low = (product - high.astype(jnp.float32)).astype(jnp.bfloat16)
        delta = (mm_nt(ones, high) + mm_nt(ones, low)).astype(jnp.bfloat16).astype(jnp.float32)
        auxs[h] = jnp.where(upper, norm[h : h + 1, :], delta)
    send_extra((AUX,))
    send_main((AUX,))
    send_extra((K, V))

    @pl.when(shares)
    def _():
        def forward(i, carry):
            for b in range(2):
                block = 2 * near(i) + b
                for kind in (AUX, Q, G):
                    wait(landing[kind].at[0, block], in_recv.at[kind, 0, block])
                    pltpu.make_async_remote_copy(
                        src_ref=landing[kind].at[0, block],
                        dst_ref=landing[kind].at[0, block],
                        send_sem=fwd_send.at[kind - Q, block],
                        recv_sem=in_recv.at[kind, 0, block],
                        device_id={"ctx": partner},
                        device_id_type=pl.DeviceIdType.MESH,
                    ).start()
            return carry

        lax.fori_loop(0, HALF, forward, 0)

    send_main((Q, G))
    pass_inputs((Q, G))
    send_main((K, V))

    below = lax.broadcasted_iota(jnp.int32, (ROWS, ROWS), 0) > lax.broadcasted_iota(
        jnp.int32, (ROWS, ROWS), 1
    )
    tri[0] = jnp.zeros((ROWS, ROWS), jnp.float32)
    tri[1] = jnp.where(below, HIDE, 0.0)

    def give(kind, slot, head, dest):
        src = staged[kind].at[slot, dest]
        dst = results[kind].at[head]

        passed = (slot == 1) & (dest // 2 == opposite)

        @pl.when(passed)
        def _():
            b = (dest + core) % 2
            remote(
                src, pass_out.at[kind, b], out_send.at[kind, slot, dest], pass_out_recv.at[kind, b], by
            ).start()

        @pl.when((dest != me) & jnp.logical_not(passed))
        def _():
            remote(
                src, dst, out_send.at[kind, slot, dest], out_recv.at[kind, head], dest
            ).start()

        @pl.when(dest == me)
        def _():
            pltpu.make_async_copy(src, dst, out_recv.at[kind, head]).start()

    def around(i):
        return (chip + arrival(i)) % CHIPS

    def pass_part(i):
        return pltpu.make_async_remote_copy(
            src_ref=part_out.at[i],
            dst_ref=part_in.at[i],
            send_sem=part_send.at[i],
            recv_sem=part_recv.at[i],
            device_id={"ctx": partner},
            device_id_type=pl.DeviceIdType.MESH,
        )

    def turned(slot, c):
        qt[c] = qb[slot, pl.ds(2 * c, 2)].reshape(PAIR, WIDTH).T
        gt[c] = gb[slot, pl.ds(2 * c, 2)].reshape(PAIR, WIDTH).T

    def queries_arrived(slot, c):
        for b in range(2):
            for kind in (AUX, Q, G):
                wait(landing[kind].at[slot, 2 * c + b], in_recv.at[kind, slot, 2 * c + b])
        turned(slot, c)

    def one_pair(step, carry):
        slot = jnp.where(step < HALF, 0, 1)
        turn = step - HALF * slot
        head = jnp.where(slot == 0, N + chip // 2, me)

        @pl.when(turn == 0)
        def _():
            dqa[...] = jnp.zeros_like(dqa)

        @pl.when(step == 0)
        def _():
            def ready(i, carry):
                turned(0, near(i))
                queries_arrived(0, far(i))
                return carry

            lax.fori_loop(0, HALF, ready, 0)

        @pl.when(step == HALF)
        def _():
            def ready(i, carry):
                queries_arrived(1, around(i))
                return carry

            lax.fori_loop(0, CHIPS, ready, 0)
            pass_inputs((K, V))

        c = jnp.where(slot == 0, near(turn), around(turn))
        for b in range(2):
            for kind in (K, V):
                wait(landing[kind].at[slot, 2 * c + b], in_recv.at[kind, slot, 2 * c + b])
        pair = pl.ds(2 * c, 2)
        keys = kb[slot, pair].reshape(PAIR, WIDTH)
        vals = vb[slot, pair].reshape(PAIR, WIDTH)
        keys_t = keys.T
        dk = jnp.zeros((PAIR, WIDTH), jnp.float32)
        dv = jnp.zeros((PAIR, WIDTH), jnp.float32)
        for t in range(CHIPS):
            spot = slice(2 * t, 2 * t + 2)
            queries = qb[slot, spot].reshape(PAIR, WIDTH)
            grads = gb[slot, spot].reshape(PAIR, WIDTH)
            norms = [auxb[slot, 2 * t + b, 0:1, :] for b in range(2)]
            delta = jnp.concatenate([auxb[slot, 2 * t + b, 4:5, :] for b in range(2)], axis=1)
            diagonal = tri[jnp.where(c == t, 1, 0)]
            scores = mm(keys, qt[t]) * (SCALE * LOG2E)
            grad_weights = mm(vals, gt[t])
            parts = []
            for kblock in range(2):
                bias = []
                for qblock in range(2):
                    later = pos_ref[2 * c + kblock] > pos_ref[2 * t + qblock]
                    row = norms[qblock] + jnp.where(later, HIDE, 0.0)
                    bias.append(row + diagonal if kblock == qblock else jnp.broadcast_to(row, (ROWS, ROWS)))
                part = scores[kblock * ROWS : (kblock + 1) * ROWS]
                parts.append(jnp.exp2(part - jnp.concatenate(bias, axis=1)))
            weights = jnp.concatenate(parts, axis=0)
            grad_scores = (weights * (grad_weights - delta)).astype(jnp.bfloat16)
            dv += mm(weights.astype(jnp.bfloat16), grads)
            dk += mm(grad_scores, queries)
            dqa[t] += mm(keys_t, grad_scores)
        dko[slot, pair] = (dk * SCALE).astype(jnp.bfloat16).reshape(2, ROWS, WIDTH)
        dvo[slot, pair] = dv.astype(jnp.bfloat16).reshape(2, ROWS, WIDTH)
        for b in range(2):
            give(DK, slot, head, 2 * c + b)
            give(DV, slot, head, 2 * c + b)

        @pl.when(step == HALF - 1)
        def _():
            def part(i, carry):
                part_out[i] = dqa[far(i)].T.astype(jnp.bfloat16)
                pass_part(i).start()
                dqn[i] = dqa[near(i)].T
                return carry

            lax.fori_loop(0, HALF, part, 0)

        @pl.when(shares & (step == HALF + 5))
        def _():
            def total(i, carry):
                pass_part(i).wait_recv()
                done = ((dqn[i] + part_in[i].astype(jnp.float32)) * SCALE).astype(jnp.bfloat16)
                c = near(i)
                dqo[0, pl.ds(2 * c, 2)] = done.reshape(2, ROWS, WIDTH)
                for b in range(2):
                    give(DQ, 0, N + chip // 2, 2 * c + b)
                return carry

            lax.fori_loop(0, HALF, total, 0)

        @pl.when(step == HALF + CHIPS - 1)
        def _():
            def finish(i, carry):
                c = around((i + CHIPS - 1) % CHIPS)
                done = (dqa[c] * SCALE).T.astype(jnp.bfloat16)
                dqo[1, pl.ds(2 * c, 2)] = done.reshape(2, ROWS, WIDTH)
                for b in range(2):
                    give(DQ, 1, me, 2 * c + b)
                return carry

            lax.fori_loop(0, CHIPS, finish, 0)

        return carry

    lax.fori_loop(jnp.where(shares, 0, HALF), HALF + CHIPS, one_pair, 0)
    pass_results((DK, DV, DQ))

    def drain_in(h, carry):
        owner = jnp.where(h < N, h, nearer(jnp.maximum(h - N, 0)))

        @pl.when(owner != me)
        def _():
            for kind in range(5):
                wait(sources[kind].at[h], in_send.at[kind, h])

        return carry

    lax.fori_loop(0, HEADS, drain_in, 0)

    def drain_out(slot, dest):
        @pl.when(dest != me)
        def _():
            for kind in range(3):
                wait(staged[kind].at[slot, dest], out_send.at[kind, slot, dest])

    def drain_main(dest, carry):
        drain_out(1, dest)
        return carry

    lax.fori_loop(0, N, drain_main, 0)

    @pl.when(shares)
    def _():
        def drain_shared(i, carry):
            pass_part(i).wait_send()
            for b in range(2):
                block = 2 * near(i) + b
                drain_out(0, block)
                for kind in (AUX, Q, G):
                    wait(landing[kind].at[0, block], fwd_send.at[kind - Q, block])
            return carry

        lax.fori_loop(0, HALF, drain_shared, 0)

    def collect(h, carry):
        for kind in range(3):
            wait(results[kind].at[h], out_recv.at[kind, h])
        return carry

    lax.fori_loop(0, HEADS, collect, 0)
    for b in range(2):
        for kind in (K, V, Q, G):
            wait(pass_in.at[kind, b], pass_in_send.at[kind, b])
        for kind in (DQ, DK, DV):
            wait(pass_out.at[kind, b], pass_out_send.at[kind, b])


def hand_on(dq_ref, dk_ref, dv_ref, dq_out, dk_out, dv_out, held, load_sem, store_sem):
    loads, stores = [], []
    for i, (src, dst) in enumerate(((dq_ref, dq_out), (dk_ref, dk_out), (dv_ref, dv_out))):
        for j in range(PIECES):
            part = pl.ds(j * (HEADS // PIECES), HEADS // PIECES)
            loads.append(pltpu.make_async_copy(src.at[part], held.at[i, part], load_sem.at[i, j]))
            stores.append(pltpu.make_async_copy(held.at[i, part], dst.at[part], store_sem.at[i, j]))
    for load in loads:
        load.start()
    for load, store in zip(loads, stores):
        load.wait()
        store.start()
    for store in stores:
        store.wait()


def body(queries, keys, values, outputs, grad_out, log_norm, block_position):
    by_head = [jnp.transpose(x, (1, 0, 2)) for x in (queries, keys, values, outputs, grad_out)]
    whole = jax.ShapeDtypeStruct((HEADS, ROWS, WIDTH), jnp.bfloat16)
    blocks = pltpu.VMEM((2, N, ROWS, WIDTH), jnp.bfloat16)
    results = pl.pallas_call(
        kernel,
        out_shape=(whole, whole, whole),
        in_specs=[pl.BlockSpec(memory_space=pl.ANY)] * 5
        + [pl.BlockSpec(memory_space=pltpu.VMEM), pl.BlockSpec(memory_space=pltpu.SMEM)],
        out_specs=[pl.BlockSpec(memory_space=pl.ANY)] * 3,
        scratch_shapes=[
            blocks, blocks, blocks, blocks,
            pltpu.VMEM((2, N, 8, ROWS), jnp.float32),
            pltpu.VMEM((HEADS, ROWS, WIDTH), jnp.bfloat16),
            pltpu.VMEM((HEADS, ROWS, WIDTH), jnp.bfloat16),
            pltpu.VMEM((HEADS, 8, ROWS), jnp.float32),
            pltpu.VMEM((CHIPS, WIDTH, PAIR), jnp.bfloat16),
            pltpu.VMEM((CHIPS, WIDTH, PAIR), jnp.bfloat16),
            pltpu.VMEM((2, ROWS, ROWS), jnp.float32),
            pltpu.VMEM((CHIPS, WIDTH, PAIR), jnp.float32),
            blocks, blocks, blocks,
            pltpu.VMEM((HALF, PAIR, WIDTH), jnp.float32),
            pltpu.VMEM((HALF, PAIR, WIDTH), jnp.bfloat16),
            pltpu.VMEM((HALF, PAIR, WIDTH), jnp.bfloat16),
            pltpu.VMEM((4, 2, ROWS, WIDTH), jnp.bfloat16),
            pltpu.VMEM((3, 2, ROWS, WIDTH), jnp.bfloat16),
            pltpu.SemaphoreType.DMA((2,)),
            pltpu.SemaphoreType.DMA((5, HEADS)),
            pltpu.SemaphoreType.DMA((5, 2, N)),
            pltpu.SemaphoreType.DMA((3, N)),
            pltpu.SemaphoreType.DMA((HALF,)),
            pltpu.SemaphoreType.DMA((HALF,)),
            pltpu.SemaphoreType.DMA((3, 2, N)),
            pltpu.SemaphoreType.DMA((3, HEADS)),
            pltpu.SemaphoreType.DMA((4, 2)),
            pltpu.SemaphoreType.DMA((4, 2)),
            pltpu.SemaphoreType.DMA((3, 2)),
            pltpu.SemaphoreType.DMA((3, 2)),
        ],
        compiler_params=pltpu.CompilerParams(
            collective_id=0, has_side_effects=True, vmem_limit_bytes=62 * 1024 * 1024
        ),
        name="attention_backward",
    )(*by_head, log_norm.T, block_position)
    results = pl.pallas_call(
        hand_on,
        out_shape=(whole, whole, whole),
        in_specs=[pl.BlockSpec(memory_space=pl.ANY)] * 3,
        out_specs=[pl.BlockSpec(memory_space=pl.ANY)] * 3,
        scratch_shapes=[
            pltpu.VMEM((3, HEADS, ROWS, WIDTH), jnp.bfloat16),
            pltpu.SemaphoreType.DMA((3, PIECES)),
            pltpu.SemaphoreType.DMA((3, PIECES)),
        ],
        compiler_params=pltpu.CompilerParams(vmem_limit_bytes=62 * 1024 * 1024),
        name="hand_on",
    )(*results)
    return tuple(jnp.transpose(x, (1, 0, 2)) for x in results)


def solution(mesh):
    rows = P(("seq", "ctx"), None, None)
    return jax.shard_map(
        body,
        mesh=mesh,
        in_specs=(rows, rows, rows, rows, rows, P(("seq", "ctx"), None), P("seq")),
        out_specs=(rows, rows, rows),
        check_vma=False,
    )
```

```python
import math

import jax
import jax.numpy as jnp
from jax import lax
from jax.experimental import pallas as pl
from jax.experimental.pallas import tpu as pltpu
from jax.sharding import PartitionSpec as P

N = 16
ROWS = 128
WIDTH = 128
HEADS = 20
EXTRA = HEADS - N
CHIPS = N // 2
HALF = CHIPS // 2
PAIR = 2 * ROWS
LOG2E = math.log2(math.e)
SCALE = 1.0 / math.sqrt(WIDTH)
HIDE = 1e30
K, V, Q, G, AUX = range(5)
DQ, DK, DV = range(3)


FAR_AND_NEAR = (4, 1, 5, 2, 7, 3, 6)


def arrival(step):
    offset = 0
    for i, sent in enumerate(FAR_AND_NEAR):
        offset = jnp.where(step == i + 1, CHIPS - sent, offset)
    return offset


def mm(a, b):
    return lax.dot_general(a, b, (((1,), (0,)), ((), ())), preferred_element_type=jnp.float32)


def mm_nt(a, b):
    return lax.dot_general(a, b, (((1,), (1,)), ((), ())), preferred_element_type=jnp.float32)


def kernel(
    q_ref, k_ref, v_ref, o_ref, g_ref, ln_ref, pos_ref,
    dq_ref, dk_ref, dv_ref,
    kb, vb, qb, gb, auxb, ov, gv, auxs, qt, gt, tri, dqa, dqo, dko, dvo, dqn, part_out, part_in,
    load_sem, in_send, in_recv, fwd_send, part_send, part_recv, out_send, out_recv,
):
    me = lax.axis_index("ctx")
    chip = me // 2
    core = me % 2
    shares = core == 0
    toward = 2 * (chip % 2) - 1
    partner = me - 2 * toward
    sources = (k_ref, v_ref, q_ref, g_ref, auxs)
    landing = (kb, vb, qb, gb, auxb)
    staged = (dqo, dko, dvo)
    results = (dq_ref, dk_ref, dv_ref)

    def wait(ref, sem):
        pltpu.make_async_copy(ref, ref, sem).wait()

    def near(i):
        return (chip + toward * i + CHIPS) % CHIPS

    def far(i):
        return (chip - toward * (i + 1) + CHIPS) % CHIPS

    def nearer(which):
        offset = (chip - 2 * which + CHIPS) % CHIPS
        side = jnp.where((offset >= 1) & (offset <= CHIPS // 2), 1, 0)
        return 2 * (2 * which + side)

    def send(kind, head, slot, dest):
        pltpu.make_async_remote_copy(
            src_ref=sources[kind].at[head],
            dst_ref=landing[kind].at[slot, me],
            send_sem=in_send.at[kind, head],
            recv_sem=in_recv.at[kind, slot, me],
            device_id={"ctx": dest},
            device_id_type=pl.DeviceIdType.MESH,
        ).start()

    def keep(kind, head, slot):
        pltpu.make_async_copy(
            sources[kind].at[head], landing[kind].at[slot, me], in_recv.at[kind, slot, me]
        ).start()

    def send_extra(kinds, i):
        which = (chip // 2 + i) % EXTRA
        dest = nearer(which)

        @pl.when(dest != me)
        def _():
            for kind in kinds:
                send(kind, N + which, 0, dest)

        @pl.when(dest == me)
        def _():
            for kind in kinds:
                keep(kind, N + which, 0)

    def send_own_chip(kinds):
        for kind in kinds:
            keep(kind, me, 1)
        for kind in kinds:
            send(kind, 2 * chip + 1 - core, 1, 2 * chip + 1 - core)

    def send_main(kinds, i):
        for b in range(2):
            dest = 2 * ((chip + FAR_AND_NEAR[i]) % CHIPS) + (core + b) % 2
            for kind in kinds:
                send(kind, dest, 1, dest)

    load_g = pltpu.make_async_copy(g_ref, gv, load_sem.at[0])
    load_o = pltpu.make_async_copy(o_ref, ov, load_sem.at[1])
    load_g.start()
    load_o.start()
    barrier = pltpu.get_barrier_semaphore()

    def greet(i, carry):
        pl.semaphore_signal(
            barrier, inc=1, device_id={"ctx": (me + i) % N}, device_id_type=pl.DeviceIdType.MESH
        )
        return carry

    lax.fori_loop(1, N, greet, 0)
    pl.semaphore_wait(barrier, N - 1)

    send_own_chip((Q, G))
    for i in range(2):
        send_main((Q, G), i)
        send_extra((Q, G), i)

    load_g.wait()
    load_o.wait()
    norm = ln_ref[...].astype(jnp.float32) * LOG2E
    ones = jnp.ones((8, WIDTH), jnp.bfloat16)
    upper = lax.broadcasted_iota(jnp.int32, (8, ROWS), 0) < 4
    for h in range(HEADS):
        product = gv[h].astype(jnp.float32) * ov[h].astype(jnp.float32)
        high = product.astype(jnp.bfloat16)
        low = (product - high.astype(jnp.float32)).astype(jnp.bfloat16)
        delta = (mm_nt(ones, high) + mm_nt(ones, low)).astype(jnp.bfloat16).astype(jnp.float32)
        auxs[h] = jnp.where(upper, norm[h : h + 1, :], delta)
    for i in range(EXTRA):
        send_extra((AUX,), i)
    send_own_chip((AUX,))
    for i in range(CHIPS - 1):
        send_main((AUX,), i)
    for i in range(2, CHIPS - 1):
        send_main((Q, G), i)
        if i < EXTRA:
            send_extra((Q, G), i)
        if i < 2 + EXTRA:
            send_extra((K, V), i - 2)

    @pl.when(shares)
    def _():
        def forward(i, carry):
            for b in range(2):
                block = 2 * near(i) + b
                for kind in (AUX, Q, G):
                    wait(landing[kind].at[0, block], in_recv.at[kind, 0, block])
                    pltpu.make_async_remote_copy(
                        src_ref=landing[kind].at[0, block],
                        dst_ref=landing[kind].at[0, block],
                        send_sem=fwd_send.at[kind - Q, block],
                        recv_sem=in_recv.at[kind, 0, block],
                        device_id={"ctx": partner},
                        device_id_type=pl.DeviceIdType.MESH,
                    ).start()
            return carry

        lax.fori_loop(0, HALF, forward, 0)

    send_own_chip((K, V))
    for i in range(CHIPS - 1):
        send_main((K, V), i)

    below = lax.broadcasted_iota(jnp.int32, (ROWS, ROWS), 0) > lax.broadcasted_iota(
        jnp.int32, (ROWS, ROWS), 1
    )
    tri[0] = jnp.zeros((ROWS, ROWS), jnp.float32)
    tri[1] = jnp.where(below, HIDE, 0.0)

    def give(kind, slot, head, dest):
        src = staged[kind].at[slot, dest]
        dst = results[kind].at[head]

        @pl.when(dest != me)
        def _():
            pltpu.make_async_remote_copy(
                src_ref=src,
                dst_ref=dst,
                send_sem=out_send.at[kind, slot, dest],
                recv_sem=out_recv.at[kind, head],
                device_id={"ctx": dest},
                device_id_type=pl.DeviceIdType.MESH,
            ).start()

        @pl.when(dest == me)
        def _():
            pltpu.make_async_copy(src, dst, out_recv.at[kind, head]).start()

    def around(i):
        return (chip + arrival(i)) % CHIPS

    def pass_part(i):
        return pltpu.make_async_remote_copy(
            src_ref=part_out.at[i],
            dst_ref=part_in.at[i],
            send_sem=part_send.at[i],
            recv_sem=part_recv.at[i],
            device_id={"ctx": partner},
            device_id_type=pl.DeviceIdType.MESH,
        )

    def turned(slot, c):
        qt[c] = qb[slot, pl.ds(2 * c, 2)].reshape(PAIR, WIDTH).T
        gt[c] = gb[slot, pl.ds(2 * c, 2)].reshape(PAIR, WIDTH).T

    def queries_arrived(slot, c):
        for b in range(2):
            for kind in (AUX, Q, G):
                wait(landing[kind].at[slot, 2 * c + b], in_recv.at[kind, slot, 2 * c + b])
        turned(slot, c)

    def one_pair(step, carry):
        slot = jnp.where(step < HALF, 0, 1)
        turn = step - HALF * slot
        head = jnp.where(slot == 0, N + chip // 2, me)

        @pl.when(turn == 0)
        def _():
            dqa[...] = jnp.zeros_like(dqa)

        @pl.when(step == 0)
        def _():
            def ready(i, carry):
                turned(0, near(i))
                queries_arrived(0, far(i))
                return carry

            lax.fori_loop(0, HALF, ready, 0)

        @pl.when(step == HALF)
        def _():
            def ready(i, carry):
                queries_arrived(1, around(i))
                return carry

            lax.fori_loop(0, CHIPS, ready, 0)

        c = jnp.where(slot == 0, near(turn), around(turn))
        for b in range(2):
            for kind in (K, V):
                wait(landing[kind].at[slot, 2 * c + b], in_recv.at[kind, slot, 2 * c + b])
        pair = pl.ds(2 * c, 2)
        keys = kb[slot, pair].reshape(PAIR, WIDTH)
        vals = vb[slot, pair].reshape(PAIR, WIDTH)
        keys_t = keys.T
        dk = jnp.zeros((PAIR, WIDTH), jnp.float32)
        dv = jnp.zeros((PAIR, WIDTH), jnp.float32)
        for t in range(CHIPS):
            spot = slice(2 * t, 2 * t + 2)
            queries = qb[slot, spot].reshape(PAIR, WIDTH)
            grads = gb[slot, spot].reshape(PAIR, WIDTH)
            norms = [auxb[slot, 2 * t + b, 0:1, :] for b in range(2)]
            delta = jnp.concatenate([auxb[slot, 2 * t + b, 4:5, :] for b in range(2)], axis=1)
            diagonal = tri[jnp.where(c == t, 1, 0)]
            scores = mm(keys, qt[t]) * (SCALE * LOG2E)
            grad_weights = mm(vals, gt[t])
            parts = []
            for kblock in range(2):
                bias = []
                for qblock in range(2):
                    later = pos_ref[2 * c + kblock] > pos_ref[2 * t + qblock]
                    row = norms[qblock] + jnp.where(later, HIDE, 0.0)
                    bias.append(row + diagonal if kblock == qblock else jnp.broadcast_to(row, (ROWS, ROWS)))
                part = scores[kblock * ROWS : (kblock + 1) * ROWS]
                parts.append(jnp.exp2(part - jnp.concatenate(bias, axis=1)))
            weights = jnp.concatenate(parts, axis=0)
            grad_scores = (weights * (grad_weights - delta)).astype(jnp.bfloat16)
            dv += mm(weights.astype(jnp.bfloat16), grads)
            dk += mm(grad_scores, queries)
            dqa[t] += mm(keys_t, grad_scores)
        dko[slot, pair] = (dk * SCALE).astype(jnp.bfloat16).reshape(2, ROWS, WIDTH)
        dvo[slot, pair] = dv.astype(jnp.bfloat16).reshape(2, ROWS, WIDTH)
        for b in range(2):
            give(DK, slot, head, 2 * c + b)
            give(DV, slot, head, 2 * c + b)

        @pl.when(step == HALF - 1)
        def _():
            def part(i, carry):
                part_out[i] = dqa[far(i)].T.astype(jnp.bfloat16)
                pass_part(i).start()
                dqn[i] = dqa[near(i)].T
                return carry

            lax.fori_loop(0, HALF, part, 0)

        @pl.when(shares & (step == HALF + 5))
        def _():
            def total(i, carry):
                pass_part(i).wait_recv()
                done = ((dqn[i] + part_in[i].astype(jnp.float32)) * SCALE).astype(jnp.bfloat16)
                c = near(i)
                dqo[0, pl.ds(2 * c, 2)] = done.reshape(2, ROWS, WIDTH)
                for b in range(2):
                    give(DQ, 0, N + chip // 2, 2 * c + b)
                return carry

            lax.fori_loop(0, HALF, total, 0)

        @pl.when(step == HALF + CHIPS - 1)
        def _():
            def finish(i, carry):
                c = around(i)
                done = (dqa[c] * SCALE).T.astype(jnp.bfloat16)
                dqo[1, pl.ds(2 * c, 2)] = done.reshape(2, ROWS, WIDTH)
                for b in range(2):
                    give(DQ, 1, me, 2 * c + b)
                return carry

            lax.fori_loop(0, CHIPS, finish, 0)

        return carry

    lax.fori_loop(jnp.where(shares, 0, HALF), HALF + CHIPS, one_pair, 0)

    def drain_in(h, carry):
        owner = jnp.where(h < N, h, nearer(jnp.maximum(h - N, 0)))

        @pl.when(owner != me)
        def _():
            for kind in range(5):
                wait(sources[kind].at[h], in_send.at[kind, h])

        return carry

    lax.fori_loop(0, HEADS, drain_in, 0)

    def drain_out(slot, dest):
        @pl.when(dest != me)
        def _():
            for kind in range(3):
                wait(staged[kind].at[slot, dest], out_send.at[kind, slot, dest])

    def drain_main(dest, carry):
        drain_out(1, dest)
        return carry

    lax.fori_loop(0, N, drain_main, 0)

    @pl.when(shares)
    def _():
        def drain_shared(i, carry):
            pass_part(i).wait_send()
            for b in range(2):
                block = 2 * near(i) + b
                drain_out(0, block)
                for kind in (AUX, Q, G):
                    wait(landing[kind].at[0, block], fwd_send.at[kind - Q, block])
            return carry

        lax.fori_loop(0, HALF, drain_shared, 0)

    def collect(h, carry):
        for kind in range(3):
            wait(results[kind].at[h], out_recv.at[kind, h])
        return carry

    lax.fori_loop(0, HEADS, collect, 0)


def hand_on(dq_ref, dk_ref, dv_ref, dq_out, dk_out, dv_out, sem):
    copies = [
        pltpu.make_async_copy(src, dst, sem.at[i])
        for i, (src, dst) in enumerate(((dq_ref, dq_out), (dk_ref, dk_out), (dv_ref, dv_out)))
    ]
    for copy in copies:
        copy.start()
    for copy in copies:
        copy.wait()


def body(queries, keys, values, outputs, grad_out, log_norm, block_position):
    by_head = [jnp.transpose(x, (1, 0, 2)) for x in (queries, keys, values, outputs, grad_out)]
    whole = jax.ShapeDtypeStruct((HEADS, ROWS, WIDTH), jnp.bfloat16)
    landed = pltpu.VMEM((HEADS, ROWS, WIDTH), jnp.bfloat16)
    blocks = pltpu.VMEM((2, N, ROWS, WIDTH), jnp.bfloat16)
    results = pl.pallas_call(
        kernel,
        out_shape=(landed, landed, landed),
        in_specs=[pl.BlockSpec(memory_space=pl.ANY)] * 5
        + [pl.BlockSpec(memory_space=pltpu.VMEM), pl.BlockSpec(memory_space=pltpu.SMEM)],
        out_specs=[pl.BlockSpec(memory_space=pltpu.VMEM)] * 3,
        scratch_shapes=[
            blocks, blocks, blocks, blocks,
            pltpu.VMEM((2, N, 8, ROWS), jnp.float32),
            pltpu.VMEM((HEADS, ROWS, WIDTH), jnp.bfloat16),
            pltpu.VMEM((HEADS, ROWS, WIDTH), jnp.bfloat16),
            pltpu.VMEM((HEADS, 8, ROWS), jnp.float32),
            pltpu.VMEM((CHIPS, WIDTH, PAIR), jnp.bfloat16),
            pltpu.VMEM((CHIPS, WIDTH, PAIR), jnp.bfloat16),
            pltpu.VMEM((2, ROWS, ROWS), jnp.float32),
            pltpu.VMEM((CHIPS, WIDTH, PAIR), jnp.float32),
            blocks, blocks, blocks,
            pltpu.VMEM((HALF, PAIR, WIDTH), jnp.float32),
            pltpu.VMEM((HALF, PAIR, WIDTH), jnp.bfloat16),
            pltpu.VMEM((HALF, PAIR, WIDTH), jnp.bfloat16),
            pltpu.SemaphoreType.DMA((2,)),
            pltpu.SemaphoreType.DMA((5, HEADS)),
            pltpu.SemaphoreType.DMA((5, 2, N)),
            pltpu.SemaphoreType.DMA((3, N)),
            pltpu.SemaphoreType.DMA((HALF,)),
            pltpu.SemaphoreType.DMA((HALF,)),
            pltpu.SemaphoreType.DMA((3, 2, N)),
            pltpu.SemaphoreType.DMA((3, HEADS)),
        ],
        compiler_params=pltpu.CompilerParams(
            collective_id=0, has_side_effects=True, vmem_limit_bytes=60 * 1024 * 1024
        ),
        name="attention_backward",
    )(*by_head, log_norm.T, block_position)
    results = pl.pallas_call(
        hand_on,
        out_shape=(whole, whole, whole),
        in_specs=[pl.BlockSpec(memory_space=pltpu.VMEM)] * 3,
        out_specs=[pl.BlockSpec(memory_space=pl.ANY)] * 3,
        scratch_shapes=[pltpu.SemaphoreType.DMA((3,))],
        compiler_params=pltpu.CompilerParams(vmem_limit_bytes=8 * 1024 * 1024),
        name="hand_on",
    )(*results)
    return tuple(jnp.transpose(x, (1, 0, 2)) for x in results)


def solution(mesh):
    rows = P(("seq", "ctx"), None, None)
    return jax.shard_map(
        body,
        mesh=mesh,
        in_specs=(rows, rows, rows, rows, rows, P(("seq", "ctx"), None), P("seq")),
        out_specs=(rows, rows, rows),
        check_vma=False,
    )
```

```python
import math

import jax
import jax.numpy as jnp
from jax import lax
from jax.experimental import pallas as pl
from jax.experimental.pallas import tpu as pltpu
from jax.sharding import PartitionSpec as P

N = 16
ROWS = 128
WIDTH = 128
HEADS = 20
EXTRA = HEADS - N
CHIPS = N // 2
HALF = CHIPS // 2
PAIR = 2 * ROWS
LOG2E = math.log2(math.e)
SCALE = 1.0 / math.sqrt(WIDTH)
HIDE = 1e30
KV, QG, AUX = range(3)
DQ, DKV = range(2)


FAR_AND_NEAR = (4, 1, 5, 2, 7, 3, 6)


def arrival(step):
    offset = 0
    for i, sent in enumerate(FAR_AND_NEAR):
        offset = jnp.where(step == i + 1, CHIPS - sent, offset)
    return offset


def mm(a, b):
    return lax.dot_general(a, b, (((1,), (0,)), ((), ())), preferred_element_type=jnp.float32)


def mm_nt(a, b):
    return lax.dot_general(a, b, (((1,), (1,)), ((), ())), preferred_element_type=jnp.float32)


def kernel(
    q_ref, k_ref, v_ref, o_ref, g_ref, ln_ref, pos_ref,
    dq_ref, dkv_ref,
    kv, qg, auxs, kvb, qgb, auxb, ov, qt, gt, tri, dqa, dqo, dkvo, dqn, part_out, part_in,
    load_sem, in_send, in_recv, fwd_send, part_send, part_recv, out_send, out_recv,
):
    me = lax.axis_index("ctx")
    chip = me // 2
    core = me % 2
    shares = core == 0
    toward = 2 * (chip % 2) - 1
    partner = me - 2 * toward
    sources = (kv, qg, auxs)
    landing = (kvb, qgb, auxb)
    staged = (dqo, dkvo)
    results = (dq_ref, dkv_ref)

    def wait(ref, sem):
        pltpu.make_async_copy(ref, ref, sem).wait()

    def near(i):
        return (chip + toward * i + CHIPS) % CHIPS

    def far(i):
        return (chip - toward * (i + 1) + CHIPS) % CHIPS

    def nearer(which):
        offset = (chip - 2 * which + CHIPS) % CHIPS
        side = jnp.where((offset >= 1) & (offset <= CHIPS // 2), 1, 0)
        return 2 * (2 * which + side)

    def send(kind, head, slot, dest):
        pltpu.make_async_remote_copy(
            src_ref=sources[kind].at[head],
            dst_ref=landing[kind].at[slot, me],
            send_sem=in_send.at[kind, head],
            recv_sem=in_recv.at[kind, slot, me],
            device_id={"ctx": dest},
            device_id_type=pl.DeviceIdType.MESH,
        ).start()

    def keep(kind, head, slot):
        pltpu.make_async_copy(
            sources[kind].at[head], landing[kind].at[slot, me], in_recv.at[kind, slot, me]
        ).start()

    def send_extra(kinds, i):
        which = (chip // 2 + i) % EXTRA
        dest = nearer(which)

        @pl.when(dest != me)
        def _():
            for kind in kinds:
                send(kind, N + which, 0, dest)

        @pl.when(dest == me)
        def _():
            for kind in kinds:
                keep(kind, N + which, 0)

    def send_own_chip(kinds):
        for kind in kinds:
            keep(kind, me, 1)
        for kind in kinds:
            send(kind, 2 * chip + 1 - core, 1, 2 * chip + 1 - core)

    def send_main(kinds, i):
        for b in range(2):
            dest = 2 * ((chip + FAR_AND_NEAR[i]) % CHIPS) + (core + b) % 2
            for kind in kinds:
                send(kind, dest, 1, dest)

    loads = [
        pltpu.make_async_copy(src, dst, load_sem.at[i])
        for i, (src, dst) in enumerate(
            (
                (q_ref, qg.at[:, 0]),
                (g_ref, qg.at[:, 1]),
                (o_ref, ov),
                (k_ref, kv.at[:, 0]),
                (v_ref, kv.at[:, 1]),
            )
        )
    ]
    for load in loads:
        load.start()
    barrier = pltpu.get_barrier_semaphore()

    def greet(i, carry):
        pl.semaphore_signal(
            barrier, inc=1, device_id={"ctx": (me + i) % N}, device_id_type=pl.DeviceIdType.MESH
        )
        return carry

    lax.fori_loop(1, N, greet, 0)
    pl.semaphore_wait(barrier, N - 1)

    loads[0].wait()
    loads[1].wait()
    send_own_chip((QG,))
    for i in range(2):
        send_main((QG,), i)
        send_extra((QG,), i)

    loads[2].wait()
    norm = ln_ref[...].astype(jnp.float32) * LOG2E
    ones = jnp.ones((8, WIDTH), jnp.bfloat16)
    upper = lax.broadcasted_iota(jnp.int32, (8, ROWS), 0) < 4
    for h in range(HEADS):
        product = qg[h, 1].astype(jnp.float32) * ov[h].astype(jnp.float32)
        high = product.astype(jnp.bfloat16)
        low = (product - high.astype(jnp.float32)).astype(jnp.bfloat16)
        delta = (mm_nt(ones, high) + mm_nt(ones, low)).astype(jnp.bfloat16).astype(jnp.float32)
        auxs[h] = jnp.where(upper, norm[h : h + 1, :], delta)
    for i in range(EXTRA):
        send_extra((AUX,), i)
    send_own_chip((AUX,))
    for i in range(CHIPS - 1):
        send_main((AUX,), i)
    loads[3].wait()
    loads[4].wait()
    for i in range(2, CHIPS - 1):
        send_main((QG,), i)
        if i < EXTRA:
            send_extra((QG,), i)
        if i < 2 + EXTRA:
            send_extra((KV,), i - 2)

    @pl.when(shares)
    def _():
        def forward(i, carry):
            for b in range(2):
                block = 2 * near(i) + b
                for kind in (AUX, QG):
                    wait(landing[kind].at[0, block], in_recv.at[kind, 0, block])
                    pltpu.make_async_remote_copy(
                        src_ref=landing[kind].at[0, block],
                        dst_ref=landing[kind].at[0, block],
                        send_sem=fwd_send.at[kind - QG, block],
                        recv_sem=in_recv.at[kind, 0, block],
                        device_id={"ctx": partner},
                        device_id_type=pl.DeviceIdType.MESH,
                    ).start()
            return carry

        lax.fori_loop(0, HALF, forward, 0)

    send_own_chip((KV,))
    for i in range(CHIPS - 1):
        send_main((KV,), i)

    below = lax.broadcasted_iota(jnp.int32, (ROWS, ROWS), 0) > lax.broadcasted_iota(
        jnp.int32, (ROWS, ROWS), 1
    )
    tri[0] = jnp.zeros((ROWS, ROWS), jnp.float32)
    tri[1] = jnp.where(below, HIDE, 0.0)

    def give(kind, slot, head, dest):
        src = staged[kind].at[slot, dest]
        dst = results[kind].at[head]

        @pl.when(dest != me)
        def _():
            pltpu.make_async_remote_copy(
                src_ref=src,
                dst_ref=dst,
                send_sem=out_send.at[kind, slot, dest],
                recv_sem=out_recv.at[kind, head],
                device_id={"ctx": dest},
                device_id_type=pl.DeviceIdType.MESH,
            ).start()

        @pl.when(dest == me)
        def _():
            pltpu.make_async_copy(src, dst, out_recv.at[kind, head]).start()

    def around(i):
        return (chip + arrival(i)) % CHIPS

    def pass_part(i):
        return pltpu.make_async_remote_copy(
            src_ref=part_out.at[i],
            dst_ref=part_in.at[i],
            send_sem=part_send.at[i],
            recv_sem=part_recv.at[i],
            device_id={"ctx": partner},
            device_id_type=pl.DeviceIdType.MESH,
        )

    def turned(slot, c):
        qt[c] = qgb[slot, pl.ds(2 * c, 2), 0].reshape(PAIR, WIDTH).T
        gt[c] = qgb[slot, pl.ds(2 * c, 2), 1].reshape(PAIR, WIDTH).T

    def queries_arrived(slot, c):
        for b in range(2):
            for kind in (AUX, QG):
                wait(landing[kind].at[slot, 2 * c + b], in_recv.at[kind, slot, 2 * c + b])
        turned(slot, c)

    def one_pair(step, carry):
        slot = jnp.where(step < HALF, 0, 1)
        turn = step - HALF * slot
        head = jnp.where(slot == 0, N + chip // 2, me)

        @pl.when(turn == 0)
        def _():
            dqa[...] = jnp.zeros_like(dqa)

        @pl.when(step == 0)
        def _():
            def ready(i, carry):
                turned(0, near(i))
                queries_arrived(0, far(i))
                return carry

            lax.fori_loop(0, HALF, ready, 0)

        @pl.when(step == HALF)
        def _():
            def ready(i, carry):
                queries_arrived(1, around(i))
                return carry

            lax.fori_loop(0, CHIPS, ready, 0)

        c = jnp.where(slot == 0, near(turn), around(turn))
        for b in range(2):
            for kind in (KV,):
                wait(landing[kind].at[slot, 2 * c + b], in_recv.at[kind, slot, 2 * c + b])
        pair = pl.ds(2 * c, 2)
        keys = kvb[slot, pair, 0].reshape(PAIR, WIDTH)
        vals = kvb[slot, pair, 1].reshape(PAIR, WIDTH)
        keys_t = keys.T
        dk = jnp.zeros((PAIR, WIDTH), jnp.float32)
        dv = jnp.zeros((PAIR, WIDTH), jnp.float32)
        for t in range(CHIPS):
            spot = slice(2 * t, 2 * t + 2)
            queries = qgb[slot, spot, 0].reshape(PAIR, WIDTH)
            grads = qgb[slot, spot, 1].reshape(PAIR, WIDTH)
            norms = [auxb[slot, 2 * t + b, 0:1, :] for b in range(2)]
            delta = jnp.concatenate([auxb[slot, 2 * t + b, 4:5, :] for b in range(2)], axis=1)
            diagonal = tri[jnp.where(c == t, 1, 0)]
            scores = mm(keys, qt[t]) * (SCALE * LOG2E)
            grad_weights = mm(vals, gt[t])
            parts = []
            for kblock in range(2):
                bias = []
                for qblock in range(2):
                    later = pos_ref[2 * c + kblock] > pos_ref[2 * t + qblock]
                    row = norms[qblock] + jnp.where(later, HIDE, 0.0)
                    bias.append(row + diagonal if kblock == qblock else jnp.broadcast_to(row, (ROWS, ROWS)))
                part = scores[kblock * ROWS : (kblock + 1) * ROWS]
                parts.append(jnp.exp2(part - jnp.concatenate(bias, axis=1)))
            weights = jnp.concatenate(parts, axis=0)
            grad_scores = (weights * (grad_weights - delta)).astype(jnp.bfloat16)
            dv += mm(weights.astype(jnp.bfloat16), grads)
            dk += mm(grad_scores, queries)
            dqa[t] += mm(keys_t, grad_scores)
        dkvo[slot, pair, 0] = (dk * SCALE).astype(jnp.bfloat16).reshape(2, ROWS, WIDTH)
        dkvo[slot, pair, 1] = dv.astype(jnp.bfloat16).reshape(2, ROWS, WIDTH)
        for b in range(2):
            give(DKV, slot, head, 2 * c + b)

        @pl.when(step == HALF - 1)
        def _():
            def part(i, carry):
                part_out[i] = dqa[far(i)].T.astype(jnp.bfloat16)
                pass_part(i).start()
                dqn[i] = dqa[near(i)].T
                return carry

            lax.fori_loop(0, HALF, part, 0)

        @pl.when(shares & (step == HALF + 5))
        def _():
            def total(i, carry):
                pass_part(i).wait_recv()
                done = ((dqn[i] + part_in[i].astype(jnp.float32)) * SCALE).astype(jnp.bfloat16)
                c = near(i)
                dqo[0, pl.ds(2 * c, 2)] = done.reshape(2, ROWS, WIDTH)
                for b in range(2):
                    give(DQ, 0, N + chip // 2, 2 * c + b)
                return carry

            lax.fori_loop(0, HALF, total, 0)

        @pl.when(step == HALF + CHIPS - 1)
        def _():
            def finish(i, carry):
                c = around(i)
                done = (dqa[c] * SCALE).T.astype(jnp.bfloat16)
                dqo[1, pl.ds(2 * c, 2)] = done.reshape(2, ROWS, WIDTH)
                for b in range(2):
                    give(DQ, 1, me, 2 * c + b)
                return carry

            lax.fori_loop(0, CHIPS, finish, 0)

        return carry

    lax.fori_loop(jnp.where(shares, 0, HALF), HALF + CHIPS, one_pair, 0)

    def drain_in(h, carry):
        owner = jnp.where(h < N, h, nearer(jnp.maximum(h - N, 0)))

        @pl.when(owner != me)
        def _():
            for kind in range(3):
                wait(sources[kind].at[h], in_send.at[kind, h])

        return carry

    lax.fori_loop(0, HEADS, drain_in, 0)

    def drain_out(slot, dest):
        @pl.when(dest != me)
        def _():
            for kind in range(2):
                wait(staged[kind].at[slot, dest], out_send.at[kind, slot, dest])

    def drain_main(dest, carry):
        drain_out(1, dest)
        return carry

    lax.fori_loop(0, N, drain_main, 0)

    @pl.when(shares)
    def _():
        def drain_shared(i, carry):
            pass_part(i).wait_send()
            for b in range(2):
                block = 2 * near(i) + b
                drain_out(0, block)
                for kind in (AUX, QG):
                    wait(landing[kind].at[0, block], fwd_send.at[kind - QG, block])
            return carry

        lax.fori_loop(0, HALF, drain_shared, 0)

    def collect(h, carry):
        for kind in range(2):
            wait(results[kind].at[h], out_recv.at[kind, h])
        return carry

    lax.fori_loop(0, HEADS, collect, 0)


def hand_on(dq_ref, dkv_ref, dq_out, dk_out, dv_out, sem):
    copies = [
        pltpu.make_async_copy(src, dst, sem.at[i])
        for i, (src, dst) in enumerate(
            ((dq_ref, dq_out), (dkv_ref.at[:, 0], dk_out), (dkv_ref.at[:, 1], dv_out))
        )
    ]
    for copy in copies:
        copy.start()
    for copy in copies:
        copy.wait()


def body(queries, keys, values, outputs, grad_out, log_norm, block_position):
    by_head = [jnp.transpose(x, (1, 0, 2)) for x in (queries, keys, values, outputs, grad_out)]
    whole = jax.ShapeDtypeStruct((HEADS, ROWS, WIDTH), jnp.bfloat16)
    doubles = pltpu.VMEM((HEADS, 2, ROWS, WIDTH), jnp.bfloat16)
    blocks = pltpu.VMEM((2, N, ROWS, WIDTH), jnp.bfloat16)
    double_blocks = pltpu.VMEM((2, N, 2, ROWS, WIDTH), jnp.bfloat16)
    results = pl.pallas_call(
        kernel,
        out_shape=(pltpu.VMEM((HEADS, ROWS, WIDTH), jnp.bfloat16), doubles),
        in_specs=[pl.BlockSpec(memory_space=pl.ANY)] * 5
        + [pl.BlockSpec(memory_space=pltpu.VMEM), pl.BlockSpec(memory_space=pltpu.SMEM)],
        out_specs=[pl.BlockSpec(memory_space=pltpu.VMEM)] * 2,
        scratch_shapes=[
            doubles, doubles,
            pltpu.VMEM((HEADS, 8, ROWS), jnp.float32),
            double_blocks, double_blocks,
            pltpu.VMEM((2, N, 8, ROWS), jnp.float32),
            pltpu.VMEM((HEADS, ROWS, WIDTH), jnp.bfloat16),
            pltpu.VMEM((CHIPS, WIDTH, PAIR), jnp.bfloat16),
            pltpu.VMEM((CHIPS, WIDTH, PAIR), jnp.bfloat16),
            pltpu.VMEM((2, ROWS, ROWS), jnp.float32),
            pltpu.VMEM((CHIPS, WIDTH, PAIR), jnp.float32),
            blocks, double_blocks,
            pltpu.VMEM((HALF, PAIR, WIDTH), jnp.float32),
            pltpu.VMEM((HALF, PAIR, WIDTH), jnp.bfloat16),
            pltpu.VMEM((HALF, PAIR, WIDTH), jnp.bfloat16),
            pltpu.SemaphoreType.DMA((5,)),
            pltpu.SemaphoreType.DMA((3, HEADS)),
            pltpu.SemaphoreType.DMA((3, 2, N)),
            pltpu.SemaphoreType.DMA((2, N)),
            pltpu.SemaphoreType.DMA((HALF,)),
            pltpu.SemaphoreType.DMA((HALF,)),
            pltpu.SemaphoreType.DMA((2, 2, N)),
            pltpu.SemaphoreType.DMA((2, HEADS)),
        ],
        compiler_params=pltpu.CompilerParams(
            collective_id=0, has_side_effects=True, vmem_limit_bytes=60 * 1024 * 1024
        ),
        name="attention_backward",
    )(*by_head, log_norm.T, block_position)
    results = pl.pallas_call(
        hand_on,
        out_shape=(whole, whole, whole),
        in_specs=[pl.BlockSpec(memory_space=pltpu.VMEM)] * 2,
        out_specs=[pl.BlockSpec(memory_space=pl.ANY)] * 3,
        scratch_shapes=[pltpu.SemaphoreType.DMA((3,))],
        compiler_params=pltpu.CompilerParams(vmem_limit_bytes=8 * 1024 * 1024),
        name="hand_on",
    )(*results)
    return tuple(jnp.transpose(x, (1, 0, 2)) for x in results)


def solution(mesh):
    rows = P(("seq", "ctx"), None, None)
    return jax.shard_map(
        body,
        mesh=mesh,
        in_specs=(rows, rows, rows, rows, rows, P(("seq", "ctx"), None), P("seq")),
        out_specs=(rows, rows, rows),
        check_vma=False,
    )
```

```python
import math

import jax
import jax.numpy as jnp
from jax import lax
from jax.experimental import pallas as pl
from jax.experimental.pallas import tpu as pltpu
from jax.sharding import PartitionSpec as P

N = 16
ROWS = 128
WIDTH = 128
HEADS = 20
EXTRA = HEADS - N
CHIPS = N // 2
HALF = CHIPS // 2
TILE = 4
PAIR = 2 * ROWS
LOG2E = math.log2(math.e)
SCALE = 1.0 / math.sqrt(WIDTH)
HIDE = 1e30
KV, QG, AUX = range(3)
DQ, DKV = range(2)


FAR_AND_NEAR = (4, 1, 5, 2, 7, 3, 6)


def arrival(step):
    offset = 0
    for i, sent in enumerate(FAR_AND_NEAR):
        offset = jnp.where(step == i + 1, CHIPS - sent, offset)
    return offset


def mm(a, b):
    return lax.dot_general(a, b, (((1,), (0,)), ((), ())), preferred_element_type=jnp.float32)


def mm_nt(a, b):
    return lax.dot_general(a, b, (((1,), (1,)), ((), ())), preferred_element_type=jnp.float32)


def kernel(
    q_ref, k_ref, v_ref, o_ref, g_ref, ln_ref, pos_ref,
    dq_ref, dkv_ref,
    kv, qg, auxs, kvb, qgb, auxb, ov, qt, gt, tri, dqa, dqo, dkvo, dqn, part_out, part_in,
    load_sem, in_send, in_recv, fwd_send, part_send, part_recv, out_send, out_recv,
):
    me = lax.axis_index("ctx")
    chip = me // 2
    core = me % 2
    shares = core == 0
    toward = 2 * (chip % 2) - 1
    partner = me - 2 * toward
    sources = (kv, qg, auxs)
    landing = (kvb, qgb, auxb)
    staged = (dqo, dkvo)
    results = (dq_ref, dkv_ref)

    def wait(ref, sem):
        pltpu.make_async_copy(ref, ref, sem).wait()

    def near(i):
        return (chip + toward * i + CHIPS) % CHIPS

    def far(i):
        return (chip - toward * (i + 1) + CHIPS) % CHIPS

    def nearer(which):
        offset = (chip - 2 * which + CHIPS) % CHIPS
        side = jnp.where((offset >= 1) & (offset <= CHIPS // 2), 1, 0)
        return 2 * (2 * which + side)

    def send(kind, head, slot, dest):
        pltpu.make_async_remote_copy(
            src_ref=sources[kind].at[head],
            dst_ref=landing[kind].at[slot, me],
            send_sem=in_send.at[kind, head],
            recv_sem=in_recv.at[kind, slot, me],
            device_id={"ctx": dest},
            device_id_type=pl.DeviceIdType.MESH,
        ).start()

    def keep(kind, head, slot):
        pltpu.make_async_copy(
            sources[kind].at[head], landing[kind].at[slot, me], in_recv.at[kind, slot, me]
        ).start()

    def send_extra(kinds, i):
        which = (chip // 2 + i) % EXTRA
        dest = nearer(which)

        @pl.when(dest != me)
        def _():
            for kind in kinds:
                send(kind, N + which, 0, dest)

        @pl.when(dest == me)
        def _():
            for kind in kinds:
                keep(kind, N + which, 0)

    def send_own_chip(kinds):
        for kind in kinds:
            keep(kind, me, 1)
        for kind in kinds:
            send(kind, 2 * chip + 1 - core, 1, 2 * chip + 1 - core)

    def send_main(kinds, i):
        for b in range(2):
            dest = 2 * ((chip + FAR_AND_NEAR[i]) % CHIPS) + (core + b) % 2
            for kind in kinds:
                send(kind, dest, 1, dest)

    barrier = pltpu.get_barrier_semaphore()

    def greet(i, carry):
        pl.semaphore_signal(
            barrier, inc=1, device_id={"ctx": (me + i) % N}, device_id_type=pl.DeviceIdType.MESH
        )
        return carry

    lax.fori_loop(1, N, greet, 0)
    loads = [
        pltpu.make_async_copy(src, dst, load_sem.at[i])
        for i, (src, dst) in enumerate(
            (
                (q_ref, qg.at[:, 0]),
                (g_ref, qg.at[:, 1]),
                (o_ref, ov),
                (k_ref, kv.at[:, 0]),
                (v_ref, kv.at[:, 1]),
            )
        )
    ]
    for load in loads:
        load.start()
    pl.semaphore_wait(barrier, N - 1)

    loads[0].wait()
    loads[1].wait()
    send_own_chip((QG,))
    for i in range(2):
        send_main((QG,), i)
        send_extra((QG,), i)

    loads[2].wait()
    norm = ln_ref[...].astype(jnp.float32) * LOG2E
    ones = jnp.ones((8, WIDTH), jnp.bfloat16)
    first = lax.broadcasted_iota(jnp.int32, (2, ROWS), 0) == 0
    for h in range(HEADS):
        product = qg[h, 1].astype(jnp.float32) * ov[h].astype(jnp.float32)
        high = product.astype(jnp.bfloat16)
        low = (product - high.astype(jnp.float32)).astype(jnp.bfloat16)
        delta = (mm_nt(ones, high) + mm_nt(ones, low)).astype(jnp.bfloat16).astype(jnp.float32)
        auxs[h] = jnp.where(first, norm[h : h + 1, :], delta[:2])
    for i in range(EXTRA):
        send_extra((AUX,), i)
    send_own_chip((AUX,))
    for i in range(CHIPS - 1):
        send_main((AUX,), i)
    loads[3].wait()
    loads[4].wait()
    for i in range(2, CHIPS - 1):
        send_main((QG,), i)
        if i < EXTRA:
            send_extra((QG,), i)
        if i < 2 + EXTRA:
            send_extra((KV,), i - 2)

    @pl.when(shares)
    def _():
        def forward(i, carry):
            for b in range(2):
                block = 2 * near(i) + b
                for kind in (AUX, QG):
                    wait(landing[kind].at[0, block], in_recv.at[kind, 0, block])
                    pltpu.make_async_remote_copy(
                        src_ref=landing[kind].at[0, block],
                        dst_ref=landing[kind].at[0, block],
                        send_sem=fwd_send.at[kind - QG, block],
                        recv_sem=in_recv.at[kind, 0, block],
                        device_id={"ctx": partner},
                        device_id_type=pl.DeviceIdType.MESH,
                    ).start()
            return carry

        lax.fori_loop(0, HALF, forward, 0)

    send_own_chip((KV,))
    for i in range(CHIPS - 1):
        send_main((KV,), i)

    below = lax.broadcasted_iota(jnp.int32, (ROWS, ROWS), 0) > lax.broadcasted_iota(
        jnp.int32, (ROWS, ROWS), 1
    )
    tri[0] = jnp.zeros((ROWS, ROWS), jnp.float32)
    tri[1] = jnp.where(below, HIDE, 0.0)

    def give(kind, slot, head, dest):
        src = staged[kind].at[slot, dest]
        dst = results[kind].at[head]

        @pl.when(dest != me)
        def _():
            pltpu.make_async_remote_copy(
                src_ref=src,
                dst_ref=dst,
                send_sem=out_send.at[kind, slot, dest],
                recv_sem=out_recv.at[kind, head],
                device_id={"ctx": dest},
                device_id_type=pl.DeviceIdType.MESH,
            ).start()

        @pl.when(dest == me)
        def _():
            pltpu.make_async_copy(src, dst, out_recv.at[kind, head]).start()

    def around(i):
        return (chip + arrival(i)) % CHIPS

    def pass_part(i):
        return pltpu.make_async_remote_copy(
            src_ref=part_out.at[i],
            dst_ref=part_in.at[i],
            send_sem=part_send.at[i],
            recv_sem=part_recv.at[i],
            device_id={"ctx": partner},
            device_id_type=pl.DeviceIdType.MESH,
        )

    def turned(slot, c):
        qt[c] = qgb[slot, pl.ds(2 * c, 2), 0].reshape(PAIR, WIDTH).T
        gt[c] = qgb[slot, pl.ds(2 * c, 2), 1].reshape(PAIR, WIDTH).T

    def queries_arrived(slot, c):
        for b in range(2):
            for kind in (AUX, QG):
                wait(landing[kind].at[slot, 2 * c + b], in_recv.at[kind, slot, 2 * c + b])
        turned(slot, c)

    def one_pair(step, carry):
        slot = jnp.where(step < HALF, 0, 1)
        turn = step - HALF * slot
        head = jnp.where(slot == 0, N + chip // 2, me)

        @pl.when(turn == 0)
        def _():
            dqa[...] = jnp.zeros_like(dqa)

        @pl.when(step == 0)
        def _():
            def ready(i, carry):
                turned(0, near(i))
                queries_arrived(0, far(i))
                return carry

            lax.fori_loop(0, HALF, ready, 0)

        @pl.when(step == HALF)
        def _():
            def ready(i, carry):
                queries_arrived(1, around(i))
                return carry

            lax.fori_loop(0, CHIPS, ready, 0)

        c = jnp.where(slot == 0, near(turn), around(turn))
        for b in range(2):
            for kind in (KV,):
                wait(landing[kind].at[slot, 2 * c + b], in_recv.at[kind, slot, 2 * c + b])
        pair = pl.ds(2 * c, 2)
        keys = kvb[slot, pair, 0].reshape(PAIR, WIDTH)
        vals = kvb[slot, pair, 1].reshape(PAIR, WIDTH)
        keys_t = keys.T
        dk = jnp.zeros((PAIR, WIDTH), jnp.float32)
        dv = jnp.zeros((PAIR, WIDTH), jnp.float32)
        for t in range(0, N, TILE):
            spot = slice(t, t + TILE)
            queries = qgb[slot, spot, 0].reshape(TILE * ROWS, WIDTH)
            grads = qgb[slot, spot, 1].reshape(TILE * ROWS, WIDTH)
            chips = range(t // 2, (t + TILE) // 2)
            norms = [auxb[slot, t + b, 0:1, :] for b in range(TILE)]
            delta = jnp.concatenate([auxb[slot, t + b, 1:2, :] for b in range(TILE)], axis=1)
            diagonal = [tri[jnp.where(c == u, 1, 0)] for u in chips]
            scores = mm(keys, jnp.concatenate([qt[u] for u in chips], axis=1)) * (SCALE * LOG2E)
            grad_weights = mm(vals, jnp.concatenate([gt[u] for u in chips], axis=1))
            parts = []
            for kblock in range(2):
                bias = []
                for b in range(TILE):
                    later = pos_ref[2 * c + kblock] > pos_ref[t + b]
                    row = norms[b] + jnp.where(later, HIDE, 0.0)
                    bias.append(
                        row + diagonal[b // 2]
                        if kblock == b % 2
                        else jnp.broadcast_to(row, (ROWS, ROWS))
                    )
                part = scores[kblock * ROWS : (kblock + 1) * ROWS]
                parts.append(jnp.exp2(part - jnp.concatenate(bias, axis=1)))
            weights = jnp.concatenate(parts, axis=0)
            grad_scores = (weights * (grad_weights - delta)).astype(jnp.bfloat16)
            dv += mm(weights.astype(jnp.bfloat16), grads)
            dk += mm(grad_scores, queries)
            dq = mm(keys_t, grad_scores)
            for i, u in enumerate(chips):
                dqa[u] += dq[:, i * PAIR : (i + 1) * PAIR]
        dkvo[slot, pair, 0] = (dk * SCALE).astype(jnp.bfloat16).reshape(2, ROWS, WIDTH)
        dkvo[slot, pair, 1] = dv.astype(jnp.bfloat16).reshape(2, ROWS, WIDTH)
        for b in range(2):
            give(DKV, slot, head, 2 * c + b)

        @pl.when(step == HALF - 1)
        def _():
            def part(i, carry):
                part_out[i] = dqa[far(i)].T.astype(jnp.bfloat16)
                pass_part(i).start()
                dqn[i] = dqa[near(i)].T
                return carry

            lax.fori_loop(0, HALF, part, 0)

        @pl.when(shares & (step == HALF + 5))
        def _():
            def total(i, carry):
                pass_part(i).wait_recv()
                done = ((dqn[i] + part_in[i].astype(jnp.float32)) * SCALE).astype(jnp.bfloat16)
                c = near(i)
                dqo[0, pl.ds(2 * c, 2)] = done.reshape(2, ROWS, WIDTH)
                for b in range(2):
                    give(DQ, 0, N + chip // 2, 2 * c + b)
                return carry

            lax.fori_loop(0, HALF, total, 0)

        @pl.when(step == HALF + CHIPS - 1)
        def _():
            def finish(i, carry):
                c = around(i)
                done = (dqa[c] * SCALE).T.astype(jnp.bfloat16)
                dqo[1, pl.ds(2 * c, 2)] = done.reshape(2, ROWS, WIDTH)
                for b in range(2):
                    give(DQ, 1, me, 2 * c + b)
                return carry

            lax.fori_loop(0, CHIPS, finish, 0)

        return carry

    lax.fori_loop(jnp.where(shares, 0, HALF), HALF + CHIPS, one_pair, 0)

    def drain_in(h, carry):
        owner = jnp.where(h < N, h, nearer(jnp.maximum(h - N, 0)))

        @pl.when(owner != me)
        def _():
            for kind in range(3):
                wait(sources[kind].at[h], in_send.at[kind, h])

        return carry

    lax.fori_loop(0, HEADS, drain_in, 0)

    def drain_out(slot, dest):
        @pl.when(dest != me)
        def _():
            for kind in range(2):
                wait(staged[kind].at[slot, dest], out_send.at[kind, slot, dest])

    def drain_main(dest, carry):
        drain_out(1, dest)
        return carry

    lax.fori_loop(0, N, drain_main, 0)

    @pl.when(shares)
    def _():
        def drain_shared(i, carry):
            pass_part(i).wait_send()
            for b in range(2):
                block = 2 * near(i) + b
                drain_out(0, block)
                for kind in (AUX, QG):
                    wait(landing[kind].at[0, block], fwd_send.at[kind - QG, block])
            return carry

        lax.fori_loop(0, HALF, drain_shared, 0)

    def collect(h, carry):
        for kind in range(2):
            wait(results[kind].at[h], out_recv.at[kind, h])
        return carry

    lax.fori_loop(0, HEADS, collect, 0)


def hand_on(dq_ref, dkv_ref, dq_out, dk_out, dv_out, sem):
    copies = [
        pltpu.make_async_copy(src, dst, sem.at[i])
        for i, (src, dst) in enumerate(
            ((dq_ref, dq_out), (dkv_ref.at[:, 0], dk_out), (dkv_ref.at[:, 1], dv_out))
        )
    ]
    for copy in copies:
        copy.start()
    for copy in copies:
        copy.wait()


def body(queries, keys, values, outputs, grad_out, log_norm, block_position):
    by_head = [jnp.transpose(x, (1, 0, 2)) for x in (queries, keys, values, outputs, grad_out)]
    whole = jax.ShapeDtypeStruct((HEADS, ROWS, WIDTH), jnp.bfloat16)
    doubles = pltpu.VMEM((HEADS, 2, ROWS, WIDTH), jnp.bfloat16)
    blocks = pltpu.VMEM((2, N, ROWS, WIDTH), jnp.bfloat16)
    double_blocks = pltpu.VMEM((2, N, 2, ROWS, WIDTH), jnp.bfloat16)
    results = pl.pallas_call(
        kernel,
        out_shape=(pltpu.VMEM((HEADS, ROWS, WIDTH), jnp.bfloat16), doubles),
        in_specs=[pl.BlockSpec(memory_space=pl.ANY)] * 5
        + [pl.BlockSpec(memory_space=pltpu.VMEM), pl.BlockSpec(memory_space=pltpu.SMEM)],
        out_specs=[pl.BlockSpec(memory_space=pltpu.VMEM)] * 2,
        scratch_shapes=[
            doubles, doubles,
            pltpu.VMEM((HEADS, 2, ROWS), jnp.float32),
            double_blocks, double_blocks,
            pltpu.VMEM((2, N, 2, ROWS), jnp.float32),
            pltpu.VMEM((HEADS, ROWS, WIDTH), jnp.bfloat16),
            pltpu.VMEM((CHIPS, WIDTH, PAIR), jnp.bfloat16),
            pltpu.VMEM((CHIPS, WIDTH, PAIR), jnp.bfloat16),
            pltpu.VMEM((2, ROWS, ROWS), jnp.float32),
            pltpu.VMEM((CHIPS, WIDTH, PAIR), jnp.float32),
            blocks, double_blocks,
            pltpu.VMEM((HALF, PAIR, WIDTH), jnp.float32),
            pltpu.VMEM((HALF, PAIR, WIDTH), jnp.bfloat16),
            pltpu.VMEM((HALF, PAIR, WIDTH), jnp.bfloat16),
            pltpu.SemaphoreType.DMA((5,)),
            pltpu.SemaphoreType.DMA((3, HEADS)),
            pltpu.SemaphoreType.DMA((3, 2, N)),
            pltpu.SemaphoreType.DMA((2, N)),
            pltpu.SemaphoreType.DMA((HALF,)),
            pltpu.SemaphoreType.DMA((HALF,)),
            pltpu.SemaphoreType.DMA((2, 2, N)),
            pltpu.SemaphoreType.DMA((2, HEADS)),
        ],
        compiler_params=pltpu.CompilerParams(
            collective_id=0, has_side_effects=True, vmem_limit_bytes=60 * 1024 * 1024
        ),
        name="attention_backward",
    )(*by_head, log_norm.T, block_position)
    results = pl.pallas_call(
        hand_on,
        out_shape=(whole, whole, whole),
        in_specs=[pl.BlockSpec(memory_space=pltpu.VMEM)] * 2,
        out_specs=[pl.BlockSpec(memory_space=pl.ANY)] * 3,
        scratch_shapes=[pltpu.SemaphoreType.DMA((3,))],
        compiler_params=pltpu.CompilerParams(vmem_limit_bytes=8 * 1024 * 1024),
        name="hand_on",
    )(*results)
    return tuple(jnp.transpose(x, (1, 0, 2)) for x in results)


def solution(mesh):
    rows = P(("seq", "ctx"), None, None)
    return jax.shard_map(
        body,
        mesh=mesh,
        in_specs=(rows, rows, rows, rows, rows, P(("seq", "ctx"), None), P("seq")),
        out_specs=(rows, rows, rows),
        check_vma=False,
    )
```

```python
import math

import jax
import jax.numpy as jnp
from jax import lax
from jax.experimental import pallas as pl
from jax.experimental.pallas import tpu as pltpu
from jax.sharding import PartitionSpec as P

N = 16
ROWS = 128
WIDTH = 128
HEADS = 20
EXTRA = HEADS - N
CHIPS = N // 2
HALF = CHIPS // 2
TILE = 4
PAIR = 2 * ROWS
LOG2E = math.log2(math.e)
SCALE = 1.0 / math.sqrt(WIDTH)
HIDE = 1e30
KV, QG, AUX = range(3)
DQ, DKV = range(2)


FAR_TO_NEAR = (4, 3, 5, 2, 6, 1, 7)


def sent_at(step):
    offset = 0
    for i, sent in enumerate(FAR_TO_NEAR):
        offset = jnp.where(step == i + 1, sent, offset)
    return offset


def mm(a, b):
    return lax.dot_general(a, b, (((1,), (0,)), ((), ())), preferred_element_type=jnp.float32)


def mm_nt(a, b):
    return lax.dot_general(a, b, (((1,), (1,)), ((), ())), preferred_element_type=jnp.float32)


def kernel(
    q_ref, k_ref, v_ref, o_ref, g_ref, ln_ref, pos_ref,
    dq_ref, dkv_ref,
    kv, qg, auxs, kvb, qgb, auxb, ov, qt, gt, tri, dqa, dqo, dkvo, dqn, part_out, part_in,
    load_sem, in_send, in_recv, fwd_send, part_send, part_recv, out_send, out_recv,
):
    me = lax.axis_index("ctx")
    chip = me // 2
    core = me % 2
    sign = 1 - 2 * core
    shares = core == 0
    toward = 2 * (chip % 2) - 1
    partner = me - 2 * toward
    sources = (kv, qg, auxs)
    landing = (kvb, qgb, auxb)
    staged = (dqo, dkvo)
    results = (dq_ref, dkv_ref)

    def wait(ref, sem):
        pltpu.make_async_copy(ref, ref, sem).wait()

    def near(i):
        return (chip + toward * i + CHIPS) % CHIPS

    def far(i):
        return (chip - toward * (i + 1) + CHIPS) % CHIPS

    def nearer(which):
        offset = (chip - 2 * which + CHIPS) % CHIPS
        side = jnp.where((offset >= 1) & (offset <= CHIPS // 2), 1, 0)
        return 2 * (2 * which + side)

    def send(kind, head, slot, dest):
        pltpu.make_async_remote_copy(
            src_ref=sources[kind].at[head],
            dst_ref=landing[kind].at[slot, me],
            send_sem=in_send.at[kind, head],
            recv_sem=in_recv.at[kind, slot, me],
            device_id={"ctx": dest},
            device_id_type=pl.DeviceIdType.MESH,
        ).start()

    def keep(kind, head, slot):
        pltpu.make_async_copy(
            sources[kind].at[head], landing[kind].at[slot, me], in_recv.at[kind, slot, me]
        ).start()

    def send_extra(kinds, i):
        which = (chip // 2 + i) % EXTRA
        dest = nearer(which)

        @pl.when(dest != me)
        def _():
            for kind in kinds:
                send(kind, N + which, 0, dest)

        @pl.when(dest == me)
        def _():
            for kind in kinds:
                keep(kind, N + which, 0)

    def send_own_chip(kinds):
        for kind in kinds:
            keep(kind, me, 1)
        for kind in kinds:
            send(kind, 2 * chip + 1 - core, 1, 2 * chip + 1 - core)

    def send_main(kinds, i):
        for b in range(2):
            dest = 2 * ((chip + sign * FAR_TO_NEAR[i] + CHIPS) % CHIPS) + (core + b) % 2
            for kind in kinds:
                send(kind, dest, 1, dest)

    barrier = pltpu.get_barrier_semaphore()

    def greet(i, carry):
        pl.semaphore_signal(
            barrier, inc=1, device_id={"ctx": (me + i) % N}, device_id_type=pl.DeviceIdType.MESH
        )
        return carry

    lax.fori_loop(1, N, greet, 0)
    loads = [
        pltpu.make_async_copy(src, dst, load_sem.at[i])
        for i, (src, dst) in enumerate(
            (
                (q_ref, qg.at[:, 0]),
                (g_ref, qg.at[:, 1]),
                (o_ref, ov),
                (k_ref, kv.at[:, 0]),
                (v_ref, kv.at[:, 1]),
            )
        )
    ]
    for load in loads:
        load.start()
    pl.semaphore_wait(barrier, N - 1)

    loads[0].wait()
    loads[1].wait()
    send_own_chip((QG,))
    for i in range(2):
        send_main((QG,), i)
        send_extra((QG,), i)

    loads[2].wait()
    norm = ln_ref[...].astype(jnp.float32) * LOG2E
    ones = jnp.ones((8, WIDTH), jnp.bfloat16)
    first = lax.broadcasted_iota(jnp.int32, (2, ROWS), 0) == 0
    for h in range(HEADS):
        product = qg[h, 1].astype(jnp.float32) * ov[h].astype(jnp.float32)
        high = product.astype(jnp.bfloat16)
        low = (product - high.astype(jnp.float32)).astype(jnp.bfloat16)
        delta = (mm_nt(ones, high) + mm_nt(ones, low)).astype(jnp.bfloat16).astype(jnp.float32)
        auxs[h] = jnp.where(first, norm[h : h + 1, :], delta[:2])
    for i in range(EXTRA):
        send_extra((AUX,), i)
    send_own_chip((AUX,))
    for i in range(CHIPS - 1):
        send_main((AUX,), i)
    loads[3].wait()
    loads[4].wait()
    for i in range(2, CHIPS - 1):
        send_main((QG,), i)
        if i < EXTRA:
            send_extra((QG,), i)
        if i < 2 + EXTRA:
            send_extra((KV,), i - 2)

    @pl.when(shares)
    def _():
        def forward(i, carry):
            for b in range(2):
                block = 2 * near(i) + b
                for kind in (AUX, QG):
                    wait(landing[kind].at[0, block], in_recv.at[kind, 0, block])
                    pltpu.make_async_remote_copy(
                        src_ref=landing[kind].at[0, block],
                        dst_ref=landing[kind].at[0, block],
                        send_sem=fwd_send.at[kind - QG, block],
                        recv_sem=in_recv.at[kind, 0, block],
                        device_id={"ctx": partner},
                        device_id_type=pl.DeviceIdType.MESH,
                    ).start()
            return carry

        lax.fori_loop(0, HALF, forward, 0)

    send_own_chip((KV,))
    for i in range(CHIPS - 1):
        send_main((KV,), i)

    below = lax.broadcasted_iota(jnp.int32, (ROWS, ROWS), 0) > lax.broadcasted_iota(
        jnp.int32, (ROWS, ROWS), 1
    )
    tri[0] = jnp.zeros((ROWS, ROWS), jnp.float32)
    tri[1] = jnp.where(below, HIDE, 0.0)

    def give(kind, slot, head, dest):
        src = staged[kind].at[slot, dest]
        dst = results[kind].at[head]

        @pl.when(dest != me)
        def _():
            pltpu.make_async_remote_copy(
                src_ref=src,
                dst_ref=dst,
                send_sem=out_send.at[kind, slot, dest],
                recv_sem=out_recv.at[kind, head],
                device_id={"ctx": dest},
                device_id_type=pl.DeviceIdType.MESH,
            ).start()

        @pl.when(dest == me)
        def _():
            pltpu.make_async_copy(src, dst, out_recv.at[kind, head]).start()

    def around(i):
        return (chip - sign * sent_at(i) + CHIPS) % CHIPS

    def pass_part(i):
        return pltpu.make_async_remote_copy(
            src_ref=part_out.at[i],
            dst_ref=part_in.at[i],
            send_sem=part_send.at[i],
            recv_sem=part_recv.at[i],
            device_id={"ctx": partner},
            device_id_type=pl.DeviceIdType.MESH,
        )

    def turned(slot, c):
        qt[c] = qgb[slot, pl.ds(2 * c, 2), 0].reshape(PAIR, WIDTH).T
        gt[c] = qgb[slot, pl.ds(2 * c, 2), 1].reshape(PAIR, WIDTH).T

    def queries_arrived(slot, c):
        for b in range(2):
            for kind in (AUX, QG):
                wait(landing[kind].at[slot, 2 * c + b], in_recv.at[kind, slot, 2 * c + b])
        turned(slot, c)

    def one_pair(step, carry):
        slot = jnp.where(step < HALF, 0, 1)
        turn = step - HALF * slot
        head = jnp.where(slot == 0, N + chip // 2, me)

        @pl.when(turn == 0)
        def _():
            dqa[...] = jnp.zeros_like(dqa)

        @pl.when(step == 0)
        def _():
            def ready(i, carry):
                turned(0, near(i))
                queries_arrived(0, far(i))
                return carry

            lax.fori_loop(0, HALF, ready, 0)

        @pl.when(step == HALF)
        def _():
            def ready(i, carry):
                queries_arrived(1, around(i))
                return carry

            lax.fori_loop(0, CHIPS, ready, 0)

        c = jnp.where(slot == 0, near(turn), around(turn))
        for b in range(2):
            for kind in (KV,):
                wait(landing[kind].at[slot, 2 * c + b], in_recv.at[kind, slot, 2 * c + b])
        pair = pl.ds(2 * c, 2)
        keys = kvb[slot, pair, 0].reshape(PAIR, WIDTH)
        vals = kvb[slot, pair, 1].reshape(PAIR, WIDTH)
        keys_t = keys.T
        dk = jnp.zeros((PAIR, WIDTH), jnp.float32)
        dv = jnp.zeros((PAIR, WIDTH), jnp.float32)
        for t in range(0, N, TILE):
            spot = slice(t, t + TILE)
            queries = qgb[slot, spot, 0].reshape(TILE * ROWS, WIDTH)
            grads = qgb[slot, spot, 1].reshape(TILE * ROWS, WIDTH)
            chips = range(t // 2, (t + TILE) // 2)
            norms = [auxb[slot, t + b, 0:1, :] for b in range(TILE)]
            delta = jnp.concatenate([auxb[slot, t + b, 1:2, :] for b in range(TILE)], axis=1)
            diagonal = [tri[jnp.where(c == u, 1, 0)] for u in chips]
            scores = mm(keys, jnp.concatenate([qt[u] for u in chips], axis=1)) * (SCALE * LOG2E)
            grad_weights = mm(vals, jnp.concatenate([gt[u] for u in chips], axis=1))
            parts = []
            for kblock in range(2):
                bias = []
                for b in range(TILE):
                    later = pos_ref[2 * c + kblock] > pos_ref[t + b]
                    row = norms[b] + jnp.where(later, HIDE, 0.0)
                    bias.append(
                        row + diagonal[b // 2]
                        if kblock == b % 2
                        else jnp.broadcast_to(row, (ROWS, ROWS))
                    )
                part = scores[kblock * ROWS : (kblock + 1) * ROWS]
                parts.append(jnp.exp2(part - jnp.concatenate(bias, axis=1)))
            weights = jnp.concatenate(parts, axis=0)
            grad_scores = (weights * (grad_weights - delta)).astype(jnp.bfloat16)
            dv += mm(weights.astype(jnp.bfloat16), grads)
            dk += mm(grad_scores, queries)
            dq = mm(keys_t, grad_scores)
            for i, u in enumerate(chips):
                dqa[u] += dq[:, i * PAIR : (i + 1) * PAIR]
        dkvo[slot, pair, 0] = (dk * SCALE).astype(jnp.bfloat16).reshape(2, ROWS, WIDTH)
        dkvo[slot, pair, 1] = dv.astype(jnp.bfloat16).reshape(2, ROWS, WIDTH)
        for b in range(2):
            give(DKV, slot, head, 2 * c + b)

        @pl.when(step == HALF - 1)
        def _():
            def part(i, carry):
                part_out[i] = dqa[far(i)].T.astype(jnp.bfloat16)
                pass_part(i).start()
                dqn[i] = dqa[near(i)].T
                return carry

            lax.fori_loop(0, HALF, part, 0)

        @pl.when(shares & (step == HALF + 5))
        def _():
            def total(i, carry):
                pass_part(i).wait_recv()
                done = ((dqn[i] + part_in[i].astype(jnp.float32)) * SCALE).astype(jnp.bfloat16)
                c = near(i)
                dqo[0, pl.ds(2 * c, 2)] = done.reshape(2, ROWS, WIDTH)
                for b in range(2):
                    give(DQ, 0, N + chip // 2, 2 * c + b)
                return carry

            lax.fori_loop(0, HALF, total, 0)

        @pl.when(step == HALF + CHIPS - 1)
        def _():
            def finish(i, carry):
                c = around((i + 1) % CHIPS)
                done = (dqa[c] * SCALE).T.astype(jnp.bfloat16)
                dqo[1, pl.ds(2 * c, 2)] = done.reshape(2, ROWS, WIDTH)
                for b in range(2):
                    give(DQ, 1, me, 2 * c + b)
                return carry

            lax.fori_loop(0, CHIPS, finish, 0)

        return carry

    lax.fori_loop(jnp.where(shares, 0, HALF), HALF + CHIPS, one_pair, 0)

    def drain_in(h, carry):
        owner = jnp.where(h < N, h, nearer(jnp.maximum(h - N, 0)))

        @pl.when(owner != me)
        def _():
            for kind in range(3):
                wait(sources[kind].at[h], in_send.at[kind, h])

        return carry

    lax.fori_loop(0, HEADS, drain_in, 0)

    def drain_out(slot, dest):
        @pl.when(dest != me)
        def _():
            for kind in range(2):
                wait(staged[kind].at[slot, dest], out_send.at[kind, slot, dest])

    def drain_main(dest, carry):
        drain_out(1, dest)
        return carry

    lax.fori_loop(0, N, drain_main, 0)

    @pl.when(shares)
    def _():
        def drain_shared(i, carry):
            pass_part(i).wait_send()
            for b in range(2):
                block = 2 * near(i) + b
                drain_out(0, block)
                for kind in (AUX, QG):
                    wait(landing[kind].at[0, block], fwd_send.at[kind - QG, block])
            return carry

        lax.fori_loop(0, HALF, drain_shared, 0)

    def collect(h, carry):
        for kind in range(2):
            wait(results[kind].at[h], out_recv.at[kind, h])
        return carry

    lax.fori_loop(0, HEADS, collect, 0)


def hand_on(dq_ref, dkv_ref, dq_out, dk_out, dv_out, sem):
    copies = [
        pltpu.make_async_copy(src, dst, sem.at[i])
        for i, (src, dst) in enumerate(
            ((dq_ref, dq_out), (dkv_ref.at[:, 0], dk_out), (dkv_ref.at[:, 1], dv_out))
        )
    ]
    for copy in copies:
        copy.start()
    for copy in copies:
        copy.wait()


def body(queries, keys, values, outputs, grad_out, log_norm, block_position):
    by_head = [jnp.transpose(x, (1, 0, 2)) for x in (queries, keys, values, outputs, grad_out)]
    whole = jax.ShapeDtypeStruct((HEADS, ROWS, WIDTH), jnp.bfloat16)
    doubles = pltpu.VMEM((HEADS, 2, ROWS, WIDTH), jnp.bfloat16)
    blocks = pltpu.VMEM((2, N, ROWS, WIDTH), jnp.bfloat16)
    double_blocks = pltpu.VMEM((2, N, 2, ROWS, WIDTH), jnp.bfloat16)
    results = pl.pallas_call(
        kernel,
        out_shape=(pltpu.VMEM((HEADS, ROWS, WIDTH), jnp.bfloat16), doubles),
        in_specs=[pl.BlockSpec(memory_space=pl.ANY)] * 5
        + [pl.BlockSpec(memory_space=pltpu.VMEM), pl.BlockSpec(memory_space=pltpu.SMEM)],
        out_specs=[pl.BlockSpec(memory_space=pltpu.VMEM)] * 2,
        scratch_shapes=[
            doubles, doubles,
            pltpu.VMEM((HEADS, 2, ROWS), jnp.float32),
            double_blocks, double_blocks,
            pltpu.VMEM((2, N, 2, ROWS), jnp.float32),
            pltpu.VMEM((HEADS, ROWS, WIDTH), jnp.bfloat16),
            pltpu.VMEM((CHIPS, WIDTH, PAIR), jnp.bfloat16),
            pltpu.VMEM((CHIPS, WIDTH, PAIR), jnp.bfloat16),
            pltpu.VMEM((2, ROWS, ROWS), jnp.float32),
            pltpu.VMEM((CHIPS, WIDTH, PAIR), jnp.float32),
            blocks, double_blocks,
            pltpu.VMEM((HALF, PAIR, WIDTH), jnp.float32),
            pltpu.VMEM((HALF, PAIR, WIDTH), jnp.bfloat16),
            pltpu.VMEM((HALF, PAIR, WIDTH), jnp.bfloat16),
            pltpu.SemaphoreType.DMA((5,)),
            pltpu.SemaphoreType.DMA((3, HEADS)),
            pltpu.SemaphoreType.DMA((3, 2, N)),
            pltpu.SemaphoreType.DMA((2, N)),
            pltpu.SemaphoreType.DMA((HALF,)),
            pltpu.SemaphoreType.DMA((HALF,)),
            pltpu.SemaphoreType.DMA((2, 2, N)),
            pltpu.SemaphoreType.DMA((2, HEADS)),
        ],
        compiler_params=pltpu.CompilerParams(
            collective_id=0, has_side_effects=True, vmem_limit_bytes=60 * 1024 * 1024
        ),
        name="attention_backward",
    )(*by_head, log_norm.T, block_position)
    results = pl.pallas_call(
        hand_on,
        out_shape=(whole, whole, whole),
        in_specs=[pl.BlockSpec(memory_space=pltpu.VMEM)] * 2,
        out_specs=[pl.BlockSpec(memory_space=pl.ANY)] * 3,
        scratch_shapes=[pltpu.SemaphoreType.DMA((3,))],
        compiler_params=pltpu.CompilerParams(vmem_limit_bytes=8 * 1024 * 1024),
        name="hand_on",
    )(*results)
    return tuple(jnp.transpose(x, (1, 0, 2)) for x in results)


def solution(mesh):
    rows = P(("seq", "ctx"), None, None)
    return jax.shard_map(
        body,
        mesh=mesh,
        in_specs=(rows, rows, rows, rows, rows, P(("seq", "ctx"), None), P("seq")),
        out_specs=(rows, rows, rows),
        check_vma=False,
    )
```

```python
import math

import jax
import jax.numpy as jnp
from jax import lax
from jax.experimental import pallas as pl
from jax.experimental.pallas import tpu as pltpu
from jax.sharding import PartitionSpec as P

N = 16
ROWS = 128
WIDTH = 128
HEADS = 20
EXTRA = HEADS - N
CHIPS = N // 2
HALF = CHIPS // 2
TILE = 4
PAIR = 2 * ROWS
LOG2E = math.log2(math.e)
SCALE = 1.0 / math.sqrt(WIDTH)
HIDE = 1e30
KV, QG, AUX = range(3)
DQ, DKV = range(2)


FAR_TO_NEAR = (4, 3, 5, 2, 6, 1, 7)


def sent_at(step):
    offset = 0
    for i, sent in enumerate(FAR_TO_NEAR):
        offset = jnp.where(step == i + 1, sent, offset)
    return offset


LAST_ORDERS = (
    (4, 3, 2, 5, 1, 0, 6, 7),
    (5, 4, 3, 0, 2, 1, 6, 7),
    (6, 7, 0, 3, 1, 2, 5, 4),
    (7, 0, 6, 1, 2, 3, 5, 4),
    (0, 1, 7, 2, 3, 6, 4, 5),
    (1, 0, 2, 3, 7, 5, 4, 6),
    (2, 3, 1, 0, 4, 6, 7, 5),
    (3, 2, 1, 0, 4, 7, 5, 6),
)


def last_order(chip):
    code = 0
    for i, order in enumerate(LAST_ORDERS):
        code = jnp.where(chip == i, sum(c * 8**j for j, c in enumerate(order)), code)
    return code


def mm(a, b):
    return lax.dot_general(a, b, (((1,), (0,)), ((), ())), preferred_element_type=jnp.float32)


def mm_nt(a, b):
    return lax.dot_general(a, b, (((1,), (1,)), ((), ())), preferred_element_type=jnp.float32)


def kernel(
    q_ref, k_ref, v_ref, o_ref, g_ref, ln_ref, pos_ref,
    dq_ref, dkv_ref,
    kv, qg, auxs, kvb, qgb, auxb, ov, qt, gt, tri, dqa, dqo, dkvo, dqn, part_out, part_in,
    load_sem, in_send, in_recv, fwd_send, part_send, part_recv, out_send, out_recv,
):
    me = lax.axis_index("ctx")
    chip = me // 2
    core = me % 2
    sign = 1 - 2 * core
    shares = core == 0
    toward = 2 * (chip % 2) - 1
    partner = me - 2 * toward
    sources = (kv, qg, auxs)
    landing = (kvb, qgb, auxb)
    staged = (dqo, dkvo)
    results = (dq_ref, dkv_ref)

    def wait(ref, sem):
        pltpu.make_async_copy(ref, ref, sem).wait()

    def near(i):
        return (chip + toward * i + CHIPS) % CHIPS

    def far(i):
        return (chip - toward * (i + 1) + CHIPS) % CHIPS

    def nearer(which):
        offset = (chip - 2 * which + CHIPS) % CHIPS
        side = jnp.where((offset >= 1) & (offset <= CHIPS // 2), 1, 0)
        return 2 * (2 * which + side)

    def send(kind, head, slot, dest):
        pltpu.make_async_remote_copy(
            src_ref=sources[kind].at[head],
            dst_ref=landing[kind].at[slot, me],
            send_sem=in_send.at[kind, head],
            recv_sem=in_recv.at[kind, slot, me],
            device_id={"ctx": dest},
            device_id_type=pl.DeviceIdType.MESH,
        ).start()

    def keep(kind, head, slot):
        pltpu.make_async_copy(
            sources[kind].at[head], landing[kind].at[slot, me], in_recv.at[kind, slot, me]
        ).start()

    def send_extra(kinds, i):
        which = (chip // 2 + i) % EXTRA
        dest = nearer(which)

        @pl.when(dest != me)
        def _():
            for kind in kinds:
                send(kind, N + which, 0, dest)

        @pl.when(dest == me)
        def _():
            for kind in kinds:
                keep(kind, N + which, 0)

    def send_own_chip(kinds):
        for kind in kinds:
            keep(kind, me, 1)
        for kind in kinds:
            send(kind, 2 * chip + 1 - core, 1, 2 * chip + 1 - core)

    def send_main(kinds, i):
        for b in range(2):
            dest = 2 * ((chip + sign * FAR_TO_NEAR[i] + CHIPS) % CHIPS) + (core + b) % 2
            for kind in kinds:
                send(kind, dest, 1, dest)

    barrier = pltpu.get_barrier_semaphore()

    def greet(i, carry):
        pl.semaphore_signal(
            barrier, inc=1, device_id={"ctx": (me + i) % N}, device_id_type=pl.DeviceIdType.MESH
        )
        return carry

    lax.fori_loop(1, N, greet, 0)
    loads = [
        pltpu.make_async_copy(src, dst, load_sem.at[i])
        for i, (src, dst) in enumerate(
            (
                (q_ref, qg.at[:, 0]),
                (g_ref, qg.at[:, 1]),
                (o_ref, ov),
                (k_ref, kv.at[:, 0]),
                (v_ref, kv.at[:, 1]),
            )
        )
    ]
    for load in loads:
        load.start()
    pl.semaphore_wait(barrier, N - 1)

    loads[0].wait()
    loads[1].wait()
    send_own_chip((QG,))
    for i in range(2):
        send_main((QG,), i)
        send_extra((QG,), i)

    loads[2].wait()
    norm = ln_ref[...].astype(jnp.float32) * LOG2E
    ones = jnp.ones((8, WIDTH), jnp.bfloat16)
    first = lax.broadcasted_iota(jnp.int32, (2, ROWS), 0) == 0
    for h in range(HEADS):
        product = qg[h, 1].astype(jnp.float32) * ov[h].astype(jnp.float32)
        high = product.astype(jnp.bfloat16)
        low = (product - high.astype(jnp.float32)).astype(jnp.bfloat16)
        delta = (mm_nt(ones, high) + mm_nt(ones, low)).astype(jnp.bfloat16).astype(jnp.float32)
        auxs[h] = jnp.where(first, norm[h : h + 1, :], delta[:2])
    for i in range(EXTRA):
        send_extra((AUX,), i)
    send_own_chip((AUX,))
    for i in range(CHIPS - 1):
        send_main((AUX,), i)
    loads[3].wait()
    loads[4].wait()
    for i in range(2, CHIPS - 1):
        send_main((QG,), i)
        if i < EXTRA:
            send_extra((QG,), i)
        if i < 2 + EXTRA:
            send_extra((KV,), i - 2)

    @pl.when(shares)
    def _():
        def forward(i, carry):
            for b in range(2):
                block = 2 * near(i) + b
                for kind in (AUX, QG):
                    wait(landing[kind].at[0, block], in_recv.at[kind, 0, block])
                    pltpu.make_async_remote_copy(
                        src_ref=landing[kind].at[0, block],
                        dst_ref=landing[kind].at[0, block],
                        send_sem=fwd_send.at[kind - QG, block],
                        recv_sem=in_recv.at[kind, 0, block],
                        device_id={"ctx": partner},
                        device_id_type=pl.DeviceIdType.MESH,
                    ).start()
            return carry

        lax.fori_loop(0, HALF, forward, 0)

    send_own_chip((KV,))
    for i in range(CHIPS - 1):
        send_main((KV,), i)

    below = lax.broadcasted_iota(jnp.int32, (ROWS, ROWS), 0) > lax.broadcasted_iota(
        jnp.int32, (ROWS, ROWS), 1
    )
    tri[0] = jnp.zeros((ROWS, ROWS), jnp.float32)
    tri[1] = jnp.where(below, HIDE, 0.0)

    def give(kind, slot, head, dest):
        src = staged[kind].at[slot, dest]
        dst = results[kind].at[head]

        @pl.when(dest != me)
        def _():
            pltpu.make_async_remote_copy(
                src_ref=src,
                dst_ref=dst,
                send_sem=out_send.at[kind, slot, dest],
                recv_sem=out_recv.at[kind, head],
                device_id={"ctx": dest},
                device_id_type=pl.DeviceIdType.MESH,
            ).start()

        @pl.when(dest == me)
        def _():
            pltpu.make_async_copy(src, dst, out_recv.at[kind, head]).start()

    def around(i):
        return (chip - sign * sent_at(i) + CHIPS) % CHIPS

    def pass_part(i):
        return pltpu.make_async_remote_copy(
            src_ref=part_out.at[i],
            dst_ref=part_in.at[i],
            send_sem=part_send.at[i],
            recv_sem=part_recv.at[i],
            device_id={"ctx": partner},
            device_id_type=pl.DeviceIdType.MESH,
        )

    def turned(slot, c):
        qt[c] = qgb[slot, pl.ds(2 * c, 2), 0].reshape(PAIR, WIDTH).T
        gt[c] = qgb[slot, pl.ds(2 * c, 2), 1].reshape(PAIR, WIDTH).T

    def queries_arrived(slot, c):
        for b in range(2):
            for kind in (AUX, QG):
                wait(landing[kind].at[slot, 2 * c + b], in_recv.at[kind, slot, 2 * c + b])
        turned(slot, c)

    def one_pair(step, carry):
        slot = jnp.where(step < HALF, 0, 1)
        turn = step - HALF * slot
        head = jnp.where(slot == 0, N + chip // 2, me)

        @pl.when(turn == 0)
        def _():
            dqa[...] = jnp.zeros_like(dqa)

        @pl.when(step == 0)
        def _():
            def ready(i, carry):
                turned(0, near(i))
                queries_arrived(0, far(i))
                return carry

            lax.fori_loop(0, HALF, ready, 0)

        @pl.when(step == HALF)
        def _():
            def ready(i, carry):
                queries_arrived(1, around(i))
                return carry

            lax.fori_loop(0, CHIPS, ready, 0)

        c = jnp.where(slot == 0, near(turn), around(turn))
        for b in range(2):
            for kind in (KV,):
                wait(landing[kind].at[slot, 2 * c + b], in_recv.at[kind, slot, 2 * c + b])
        pair = pl.ds(2 * c, 2)
        keys = kvb[slot, pair, 0].reshape(PAIR, WIDTH)
        vals = kvb[slot, pair, 1].reshape(PAIR, WIDTH)
        keys_t = keys.T
        dk = jnp.zeros((PAIR, WIDTH), jnp.float32)
        dv = jnp.zeros((PAIR, WIDTH), jnp.float32)
        for t in range(0, N, TILE):
            spot = slice(t, t + TILE)
            queries = qgb[slot, spot, 0].reshape(TILE * ROWS, WIDTH)
            grads = qgb[slot, spot, 1].reshape(TILE * ROWS, WIDTH)
            chips = range(t // 2, (t + TILE) // 2)
            norms = [auxb[slot, t + b, 0:1, :] for b in range(TILE)]
            delta = jnp.concatenate([auxb[slot, t + b, 1:2, :] for b in range(TILE)], axis=1)
            diagonal = [tri[jnp.where(c == u, 1, 0)] for u in chips]
            scores = mm(keys, jnp.concatenate([qt[u] for u in chips], axis=1)) * (SCALE * LOG2E)
            grad_weights = mm(vals, jnp.concatenate([gt[u] for u in chips], axis=1))
            parts = []
            for kblock in range(2):
                bias = []
                for b in range(TILE):
                    later = pos_ref[2 * c + kblock] > pos_ref[t + b]
                    row = norms[b] + jnp.where(later, HIDE, 0.0)
                    bias.append(
                        row + diagonal[b // 2]
                        if kblock == b % 2
                        else jnp.broadcast_to(row, (ROWS, ROWS))
                    )
                part = scores[kblock * ROWS : (kblock + 1) * ROWS]
                parts.append(jnp.exp2(part - jnp.concatenate(bias, axis=1)))
            weights = jnp.concatenate(parts, axis=0)
            grad_scores = (weights * (grad_weights - delta)).astype(jnp.bfloat16)
            dv += mm(weights.astype(jnp.bfloat16), grads)
            dk += mm(grad_scores, queries)
            dq = mm(keys_t, grad_scores)
            for i, u in enumerate(chips):
                dqa[u] += dq[:, i * PAIR : (i + 1) * PAIR]
        dkvo[slot, pair, 0] = (dk * SCALE).astype(jnp.bfloat16).reshape(2, ROWS, WIDTH)
        dkvo[slot, pair, 1] = dv.astype(jnp.bfloat16).reshape(2, ROWS, WIDTH)
        for b in range(2):
            give(DKV, slot, head, 2 * c + b)

        @pl.when(step == HALF - 1)
        def _():
            def part(i, carry):
                part_out[i] = dqa[far(i)].T.astype(jnp.bfloat16)
                pass_part(i).start()
                dqn[i] = dqa[near(i)].T
                return carry

            lax.fori_loop(0, HALF, part, 0)

        @pl.when(shares & (step == HALF + 5))
        def _():
            def total(i, carry):
                pass_part(i).wait_recv()
                done = ((dqn[i] + part_in[i].astype(jnp.float32)) * SCALE).astype(jnp.bfloat16)
                c = near(i)
                dqo[0, pl.ds(2 * c, 2)] = done.reshape(2, ROWS, WIDTH)
                for b in range(2):
                    give(DQ, 0, N + chip // 2, 2 * c + b)
                return carry

            lax.fori_loop(0, HALF, total, 0)

        @pl.when(step == HALF + CHIPS - 1)
        def _():
            def finish(i, orders):
                c = orders % 8
                done = (dqa[c] * SCALE).T.astype(jnp.bfloat16)
                dqo[1, pl.ds(2 * c, 2)] = done.reshape(2, ROWS, WIDTH)
                for b in range(2):
                    give(DQ, 1, me, 2 * c + b)
                return orders // 8

            lax.fori_loop(0, CHIPS, finish, last_order(chip))

        return carry

    lax.fori_loop(jnp.where(shares, 0, HALF), HALF + CHIPS, one_pair, 0)

    def drain_in(h, carry):
        owner = jnp.where(h < N, h, nearer(jnp.maximum(h - N, 0)))

        @pl.when(owner != me)
        def _():
            for kind in range(3):
                wait(sources[kind].at[h], in_send.at[kind, h])

        return carry

    lax.fori_loop(0, HEADS, drain_in, 0)

    def drain_out(slot, dest):
        @pl.when(dest != me)
        def _():
            for kind in range(2):
                wait(staged[kind].at[slot, dest], out_send.at[kind, slot, dest])

    def drain_main(dest, carry):
        drain_out(1, dest)
        return carry

    lax.fori_loop(0, N, drain_main, 0)

    @pl.when(shares)
    def _():
        def drain_shared(i, carry):
            pass_part(i).wait_send()
            for b in range(2):
                block = 2 * near(i) + b
                drain_out(0, block)
                for kind in (AUX, QG):
                    wait(landing[kind].at[0, block], fwd_send.at[kind - QG, block])
            return carry

        lax.fori_loop(0, HALF, drain_shared, 0)

    def collect(h, carry):
        for kind in range(2):
            wait(results[kind].at[h], out_recv.at[kind, h])
        return carry

    lax.fori_loop(0, HEADS, collect, 0)


def hand_on(dq_ref, dkv_ref, dq_out, dk_out, dv_out, sem):
    copies = [
        pltpu.make_async_copy(src, dst, sem.at[i])
        for i, (src, dst) in enumerate(
            ((dq_ref, dq_out), (dkv_ref.at[:, 0], dk_out), (dkv_ref.at[:, 1], dv_out))
        )
    ]
    for copy in copies:
        copy.start()
    for copy in copies:
        copy.wait()


def body(queries, keys, values, outputs, grad_out, log_norm, block_position):
    by_head = [jnp.transpose(x, (1, 0, 2)) for x in (queries, keys, values, outputs, grad_out)]
    whole = jax.ShapeDtypeStruct((HEADS, ROWS, WIDTH), jnp.bfloat16)
    doubles = pltpu.VMEM((HEADS, 2, ROWS, WIDTH), jnp.bfloat16)
    blocks = pltpu.VMEM((2, N, ROWS, WIDTH), jnp.bfloat16)
    double_blocks = pltpu.VMEM((2, N, 2, ROWS, WIDTH), jnp.bfloat16)
    results = pl.pallas_call(
        kernel,
        out_shape=(pltpu.VMEM((HEADS, ROWS, WIDTH), jnp.bfloat16), doubles),
        in_specs=[pl.BlockSpec(memory_space=pl.ANY)] * 5
        + [pl.BlockSpec(memory_space=pltpu.VMEM), pl.BlockSpec(memory_space=pltpu.SMEM)],
        out_specs=[pl.BlockSpec(memory_space=pltpu.VMEM)] * 2,
        scratch_shapes=[
            doubles, doubles,
            pltpu.VMEM((HEADS, 2, ROWS), jnp.float32),
            double_blocks, double_blocks,
            pltpu.VMEM((2, N, 2, ROWS), jnp.float32),
            pltpu.VMEM((HEADS, ROWS, WIDTH), jnp.bfloat16),
            pltpu.VMEM((CHIPS, WIDTH, PAIR), jnp.bfloat16),
            pltpu.VMEM((CHIPS, WIDTH, PAIR), jnp.bfloat16),
            pltpu.VMEM((2, ROWS, ROWS), jnp.float32),
            pltpu.VMEM((CHIPS, WIDTH, PAIR), jnp.float32),
            blocks, double_blocks,
            pltpu.VMEM((HALF, PAIR, WIDTH), jnp.float32),
            pltpu.VMEM((HALF, PAIR, WIDTH), jnp.bfloat16),
            pltpu.VMEM((HALF, PAIR, WIDTH), jnp.bfloat16),
            pltpu.SemaphoreType.DMA((5,)),
            pltpu.SemaphoreType.DMA((3, HEADS)),
            pltpu.SemaphoreType.DMA((3, 2, N)),
            pltpu.SemaphoreType.DMA((2, N)),
            pltpu.SemaphoreType.DMA((HALF,)),
            pltpu.SemaphoreType.DMA((HALF,)),
            pltpu.SemaphoreType.DMA((2, 2, N)),
            pltpu.SemaphoreType.DMA((2, HEADS)),
        ],
        compiler_params=pltpu.CompilerParams(
            collective_id=0, has_side_effects=True, vmem_limit_bytes=60 * 1024 * 1024
        ),
        name="attention_backward",
    )(*by_head, log_norm.T, block_position)
    results = pl.pallas_call(
        hand_on,
        out_shape=(whole, whole, whole),
        in_specs=[pl.BlockSpec(memory_space=pltpu.VMEM)] * 2,
        out_specs=[pl.BlockSpec(memory_space=pl.ANY)] * 3,
        scratch_shapes=[pltpu.SemaphoreType.DMA((3,))],
        compiler_params=pltpu.CompilerParams(vmem_limit_bytes=8 * 1024 * 1024),
        name="hand_on",
    )(*results)
    return tuple(jnp.transpose(x, (1, 0, 2)) for x in results)


def solution(mesh):
    rows = P(("seq", "ctx"), None, None)
    return jax.shard_map(
        body,
        mesh=mesh,
        in_specs=(rows, rows, rows, rows, rows, P(("seq", "ctx"), None), P("seq")),
        out_specs=(rows, rows, rows),
        check_vma=False,
    )
```

```python
import math

import jax
import jax.numpy as jnp
from jax import lax
from jax.experimental import pallas as pl
from jax.experimental.pallas import tpu as pltpu
from jax.sharding import PartitionSpec as P

N = 16
ROWS = 128
WIDTH = 128
HEADS = 20
EXTRA = HEADS - N
CHIPS = N // 2
HALF = CHIPS // 2
TILE = 4
PAIR = 2 * ROWS
LOG2E = math.log2(math.e)
SCALE = 1.0 / math.sqrt(WIDTH)
HIDE = 1e30
KV, QG, AUX = range(3)
DQ, DKV = range(2)


FAR_TO_NEAR = (4, 3, 5, 2, 6, 1, 7)


def sent_at(step):
    offset = 0
    for i, sent in enumerate(FAR_TO_NEAR):
        offset = jnp.where(step == i + 1, sent, offset)
    return offset


def mm(a, b):
    return lax.dot_general(a, b, (((1,), (0,)), ((), ())), preferred_element_type=jnp.float32)


def mm_nt(a, b):
    return lax.dot_general(a, b, (((1,), (1,)), ((), ())), preferred_element_type=jnp.float32)


def kernel(
    q_ref, k_ref, v_ref, o_ref, g_ref, ln_ref, pos_ref,
    dq_ref, dkv_ref,
    kv, qg, auxs, kvb, qgb, auxb, ov, qt, gt, tri, dqa, dqo, dkvo, dqn, part_out, part_in,
    load_sem, in_send, in_recv, fwd_send, part_send, part_recv, out_send, out_recv,
):
    me = lax.axis_index("ctx")
    chip = me // 2
    core = me % 2
    sign = 1 - 2 * core
    shares = core == 0
    toward = 2 * (chip % 2) - 1
    partner = me - 2 * toward
    sources = (kv, qg, auxs)
    landing = (kvb, qgb, auxb)
    staged = (dqo, dkvo)
    results = (dq_ref, dkv_ref)

    def wait(ref, sem):
        pltpu.make_async_copy(ref, ref, sem).wait()

    def near(i):
        return (chip + toward * i + CHIPS) % CHIPS

    def far(i):
        return (chip - toward * (i + 1) + CHIPS) % CHIPS

    def nearer(which):
        offset = (chip - 2 * which + CHIPS) % CHIPS
        side = jnp.where((offset >= 1) & (offset <= CHIPS // 2), 1, 0)
        return 2 * (2 * which + side)

    def send(kind, head, slot, dest):
        pltpu.make_async_remote_copy(
            src_ref=sources[kind].at[head],
            dst_ref=landing[kind].at[slot, me],
            send_sem=in_send.at[kind],
            recv_sem=in_recv.at[kind, slot, me],
            device_id={"ctx": dest},
            device_id_type=pl.DeviceIdType.MESH,
        ).start()

    def keep(kind, head, slot):
        pltpu.make_async_copy(
            sources[kind].at[head], landing[kind].at[slot, me], in_recv.at[kind, slot, me]
        ).start()

    def send_extra(kinds, i):
        which = (chip // 2 + i) % EXTRA
        dest = nearer(which)

        @pl.when(dest != me)
        def _():
            for kind in kinds:
                send(kind, N + which, 0, dest)

        @pl.when(dest == me)
        def _():
            for kind in kinds:
                keep(kind, N + which, 0)

    def send_own_chip(kinds):
        for kind in kinds:
            keep(kind, me, 1)
        for kind in kinds:
            send(kind, 2 * chip + 1 - core, 1, 2 * chip + 1 - core)

    def send_main(kinds, i):
        for b in range(2):
            dest = 2 * ((chip + sign * FAR_TO_NEAR[i] + CHIPS) % CHIPS) + (core + b) % 2
            for kind in kinds:
                send(kind, dest, 1, dest)

    barrier = pltpu.get_barrier_semaphore()

    def greet(i, carry):
        pl.semaphore_signal(
            barrier, inc=1, device_id={"ctx": (me + i) % N}, device_id_type=pl.DeviceIdType.MESH
        )
        return carry

    lax.fori_loop(1, N, greet, 0)
    loads = [
        pltpu.make_async_copy(src, dst, load_sem.at[i])
        for i, (src, dst) in enumerate(
            (
                (q_ref, qg.at[:, 0]),
                (g_ref, qg.at[:, 1]),
                (o_ref, ov),
                (k_ref, kv.at[:, 0]),
                (v_ref, kv.at[:, 1]),
            )
        )
    ]
    for load in loads:
        load.start()
    pl.semaphore_wait(barrier, N - 1)

    loads[0].wait()
    loads[1].wait()
    send_own_chip((QG,))
    for i in range(2):
        send_main((QG,), i)
        send_extra((QG,), i)

    loads[2].wait()
    norm = ln_ref[...].astype(jnp.float32) * LOG2E
    ones = jnp.ones((8, WIDTH), jnp.bfloat16)
    first = lax.broadcasted_iota(jnp.int32, (2, ROWS), 0) == 0
    for h in range(HEADS):
        product = qg[h, 1].astype(jnp.float32) * ov[h].astype(jnp.float32)
        high = product.astype(jnp.bfloat16)
        low = (product - high.astype(jnp.float32)).astype(jnp.bfloat16)
        delta = (mm_nt(ones, high) + mm_nt(ones, low)).astype(jnp.bfloat16).astype(jnp.float32)
        auxs[h] = jnp.where(first, norm[h : h + 1, :], delta[:2])
    for i in range(EXTRA):
        send_extra((AUX,), i)
    send_own_chip((AUX,))
    for i in range(CHIPS - 1):
        send_main((AUX,), i)
    loads[3].wait()
    loads[4].wait()
    for i in range(2, CHIPS - 1):
        send_main((QG,), i)
        if i < EXTRA:
            send_extra((QG,), i)
        if i < 2 + EXTRA:
            send_extra((KV,), i - 2)

    @pl.when(shares)
    def _():
        def forward(i, carry):
            for b in range(2):
                block = 2 * near(i) + b
                for kind in (AUX, QG):
                    wait(landing[kind].at[0, block], in_recv.at[kind, 0, block])
                    pltpu.make_async_remote_copy(
                        src_ref=landing[kind].at[0, block],
                        dst_ref=landing[kind].at[0, block],
                        send_sem=fwd_send.at[kind - QG],
                        recv_sem=in_recv.at[kind, 0, block],
                        device_id={"ctx": partner},
                        device_id_type=pl.DeviceIdType.MESH,
                    ).start()
            return carry

        lax.fori_loop(0, HALF, forward, 0)

    send_own_chip((KV,))
    for i in range(CHIPS - 1):
        send_main((KV,), i)

    below = lax.broadcasted_iota(jnp.int32, (ROWS, ROWS), 0) > lax.broadcasted_iota(
        jnp.int32, (ROWS, ROWS), 1
    )
    tri[0] = jnp.zeros((ROWS, ROWS), jnp.float32)
    tri[1] = jnp.where(below, HIDE, 0.0)

    def give(kind, slot, head, dest):
        src = staged[kind].at[slot, dest]
        dst = results[kind].at[head]

        @pl.when(dest != me)
        def _():
            pltpu.make_async_remote_copy(
                src_ref=src,
                dst_ref=dst,
                send_sem=out_send.at[kind, slot],
                recv_sem=out_recv.at[kind],
                device_id={"ctx": dest},
                device_id_type=pl.DeviceIdType.MESH,
            ).start()

        @pl.when(dest == me)
        def _():
            pltpu.make_async_copy(src, dst, out_recv.at[kind]).start()

    def around(i):
        return (chip - sign * sent_at(i) + CHIPS) % CHIPS

    def pass_part(i):
        return pltpu.make_async_remote_copy(
            src_ref=part_out.at[i],
            dst_ref=part_in.at[i],
            send_sem=part_send.at[0],
            recv_sem=part_recv.at[i],
            device_id={"ctx": partner},
            device_id_type=pl.DeviceIdType.MESH,
        )

    def turned(slot, c):
        qt[c] = qgb[slot, pl.ds(2 * c, 2), 0].reshape(PAIR, WIDTH).T
        gt[c] = qgb[slot, pl.ds(2 * c, 2), 1].reshape(PAIR, WIDTH).T

    def queries_arrived(slot, c):
        for b in range(2):
            for kind in (AUX, QG):
                wait(landing[kind].at[slot, 2 * c + b], in_recv.at[kind, slot, 2 * c + b])
        turned(slot, c)

    def one_pair(step, carry):
        slot = jnp.where(step < HALF, 0, 1)
        turn = step - HALF * slot
        head = jnp.where(slot == 0, N + chip // 2, me)

        @pl.when(turn == 0)
        def _():
            dqa[...] = jnp.zeros_like(dqa)

        @pl.when(step == 0)
        def _():
            def ready(i, carry):
                turned(0, near(i))
                queries_arrived(0, far(i))
                return carry

            lax.fori_loop(0, HALF, ready, 0)

        @pl.when(step == HALF)
        def _():
            def ready(i, carry):
                queries_arrived(1, around(i))
                return carry

            lax.fori_loop(0, CHIPS, ready, 0)

        c = jnp.where(slot == 0, near(turn), around(turn))
        for b in range(2):
            for kind in (KV,):
                wait(landing[kind].at[slot, 2 * c + b], in_recv.at[kind, slot, 2 * c + b])
        pair = pl.ds(2 * c, 2)
        keys = kvb[slot, pair, 0].reshape(PAIR, WIDTH)
        vals = kvb[slot, pair, 1].reshape(PAIR, WIDTH)
        keys_t = keys.T
        dk = jnp.zeros((PAIR, WIDTH), jnp.float32)
        dv = jnp.zeros((PAIR, WIDTH), jnp.float32)
        for t in range(0, N, TILE):
            spot = slice(t, t + TILE)
            queries = qgb[slot, spot, 0].reshape(TILE * ROWS, WIDTH)
            grads = qgb[slot, spot, 1].reshape(TILE * ROWS, WIDTH)
            chips = range(t // 2, (t + TILE) // 2)
            norms = [auxb[slot, t + b, 0:1, :] for b in range(TILE)]
            delta = jnp.concatenate([auxb[slot, t + b, 1:2, :] for b in range(TILE)], axis=1)
            diagonal = [tri[jnp.where(c == u, 1, 0)] for u in chips]
            scores = mm(keys, jnp.concatenate([qt[u] for u in chips], axis=1)) * (SCALE * LOG2E)
            grad_weights = mm(vals, jnp.concatenate([gt[u] for u in chips], axis=1))
            parts = []
            for kblock in range(2):
                bias = []
                for b in range(TILE):
                    later = pos_ref[2 * c + kblock] > pos_ref[t + b]
                    row = norms[b] + jnp.where(later, HIDE, 0.0)
                    bias.append(
                        row + diagonal[b // 2]
                        if kblock == b % 2
                        else jnp.broadcast_to(row, (ROWS, ROWS))
                    )
                part = scores[kblock * ROWS : (kblock + 1) * ROWS]
                parts.append(jnp.exp2(part - jnp.concatenate(bias, axis=1)))
            weights = jnp.concatenate(parts, axis=0)
            grad_scores = (weights * (grad_weights - delta)).astype(jnp.bfloat16)
            dv += mm(weights.astype(jnp.bfloat16), grads)
            dk += mm(grad_scores, queries)
            dq = mm(keys_t, grad_scores)
            for i, u in enumerate(chips):
                dqa[u] += dq[:, i * PAIR : (i + 1) * PAIR]
        dkvo[slot, pair, 0] = (dk * SCALE).astype(jnp.bfloat16).reshape(2, ROWS, WIDTH)
        dkvo[slot, pair, 1] = dv.astype(jnp.bfloat16).reshape(2, ROWS, WIDTH)
        for b in range(2):
            give(DKV, slot, head, 2 * c + b)

        @pl.when(step == HALF - 1)
        def _():
            def part(i, carry):
                part_out[i] = dqa[far(i)].T.astype(jnp.bfloat16)
                pass_part(i).start()
                dqn[i] = dqa[near(i)].T
                return carry

            lax.fori_loop(0, HALF, part, 0)

        @pl.when(shares & (step == HALF + 5))
        def _():
            def total(i, carry):
                pass_part(i).wait_recv()
                done = ((dqn[i] + part_in[i].astype(jnp.float32)) * SCALE).astype(jnp.bfloat16)
                c = near(i)
                dqo[0, pl.ds(2 * c, 2)] = done.reshape(2, ROWS, WIDTH)
                for b in range(2):
                    give(DQ, 0, N + chip // 2, 2 * c + b)
                return carry

            lax.fori_loop(0, HALF, total, 0)

        @pl.when(step == HALF + CHIPS - 1)
        def _():
            def finish(i, carry):
                c = around((i + 1) % CHIPS)
                done = (dqa[c] * SCALE).T.astype(jnp.bfloat16)
                dqo[1, pl.ds(2 * c, 2)] = done.reshape(2, ROWS, WIDTH)
                for b in range(2):
                    give(DQ, 1, me, 2 * c + b)
                return carry

            lax.fori_loop(0, CHIPS, finish, 0)

        return carry

    lax.fori_loop(jnp.where(shares, 0, HALF), HALF + CHIPS, one_pair, 0)

    @pl.when(shares)
    def _():
        for kind in range(3):
            wait(sources[kind].at[pl.ds(0, HEADS - 2)], in_send.at[kind])
        for kind in (AUX, QG):
            wait(landing[kind].at[0, pl.ds(0, CHIPS)], fwd_send.at[kind - QG])
        wait(part_out, part_send.at[0])
        for kind in range(2):
            wait(staged[kind].at[0, pl.ds(0, CHIPS - 1)], out_send.at[kind, 0])

    @pl.when(jnp.logical_not(shares))
    def _():
        for kind in range(3):
            wait(sources[kind].at[pl.ds(0, HEADS - 1)], in_send.at[kind])

    for kind in (DKV, DQ):
        wait(staged[kind].at[1, pl.ds(0, N - 1)], out_send.at[kind, 1])
        wait(results[kind], out_recv.at[kind])


def hand_on(dq_ref, dkv_ref, dq_out, dk_out, dv_out, sem):
    copies = [
        pltpu.make_async_copy(src, dst, sem.at[i])
        for i, (src, dst) in enumerate(
            ((dq_ref, dq_out), (dkv_ref.at[:, 0], dk_out), (dkv_ref.at[:, 1], dv_out))
        )
    ]
    for copy in copies:
        copy.start()
    for copy in copies:
        copy.wait()


def body(queries, keys, values, outputs, grad_out, log_norm, block_position):
    by_head = [jnp.transpose(x, (1, 0, 2)) for x in (queries, keys, values, outputs, grad_out)]
    whole = jax.ShapeDtypeStruct((HEADS, ROWS, WIDTH), jnp.bfloat16)
    doubles = pltpu.VMEM((HEADS, 2, ROWS, WIDTH), jnp.bfloat16)
    blocks = pltpu.VMEM((2, N, ROWS, WIDTH), jnp.bfloat16)
    double_blocks = pltpu.VMEM((2, N, 2, ROWS, WIDTH), jnp.bfloat16)
    results = pl.pallas_call(
        kernel,
        out_shape=(pltpu.VMEM((HEADS, ROWS, WIDTH), jnp.bfloat16), doubles),
        in_specs=[pl.BlockSpec(memory_space=pl.ANY)] * 5
        + [pl.BlockSpec(memory_space=pltpu.VMEM), pl.BlockSpec(memory_space=pltpu.SMEM)],
        out_specs=[pl.BlockSpec(memory_space=pltpu.VMEM)] * 2,
        scratch_shapes=[
            doubles, doubles,
            pltpu.VMEM((HEADS, 2, ROWS), jnp.float32),
            double_blocks, double_blocks,
            pltpu.VMEM((2, N, 2, ROWS), jnp.float32),
            pltpu.VMEM((HEADS, ROWS, WIDTH), jnp.bfloat16),
            pltpu.VMEM((CHIPS, WIDTH, PAIR), jnp.bfloat16),
            pltpu.VMEM((CHIPS, WIDTH, PAIR), jnp.bfloat16),
            pltpu.VMEM((2, ROWS, ROWS), jnp.float32),
            pltpu.VMEM((CHIPS, WIDTH, PAIR), jnp.float32),
            blocks, double_blocks,
            pltpu.VMEM((HALF, PAIR, WIDTH), jnp.float32),
            pltpu.VMEM((HALF, PAIR, WIDTH), jnp.bfloat16),
            pltpu.VMEM((HALF, PAIR, WIDTH), jnp.bfloat16),
            pltpu.SemaphoreType.DMA((5,)),
            pltpu.SemaphoreType.DMA((3,)),
            pltpu.SemaphoreType.DMA((3, 2, N)),
            pltpu.SemaphoreType.DMA((2,)),
            pltpu.SemaphoreType.DMA((1,)),
            pltpu.SemaphoreType.DMA((HALF,)),
            pltpu.SemaphoreType.DMA((2, 2)),
            pltpu.SemaphoreType.DMA((2,)),
        ],
        compiler_params=pltpu.CompilerParams(
            collective_id=0, has_side_effects=True, vmem_limit_bytes=60 * 1024 * 1024
        ),
        name="attention_backward",
    )(*by_head, log_norm.T, block_position)
    results = pl.pallas_call(
        hand_on,
        out_shape=(whole, whole, whole),
        in_specs=[pl.BlockSpec(memory_space=pltpu.VMEM)] * 2,
        out_specs=[pl.BlockSpec(memory_space=pl.ANY)] * 3,
        scratch_shapes=[pltpu.SemaphoreType.DMA((3,))],
        compiler_params=pltpu.CompilerParams(vmem_limit_bytes=8 * 1024 * 1024),
        name="hand_on",
    )(*results)
    return tuple(jnp.transpose(x, (1, 0, 2)) for x in results)


def solution(mesh):
    rows = P(("seq", "ctx"), None, None)
    return jax.shard_map(
        body,
        mesh=mesh,
        in_specs=(rows, rows, rows, rows, rows, P(("seq", "ctx"), None), P("seq")),
        out_specs=(rows, rows, rows),
        check_vma=False,
    )
```

```python
import math

import jax
import jax.numpy as jnp
from jax import lax
from jax.experimental import pallas as pl
from jax.experimental.pallas import tpu as pltpu
from jax.sharding import PartitionSpec as P

N = 16
ROWS = 128
WIDTH = 128
HEADS = 20
EXTRA = HEADS - N
CHIPS = N // 2
HALF = CHIPS // 2
TILE = 4
PAIR = 2 * ROWS
LOG2E = math.log2(math.e)
SCALE = 1.0 / math.sqrt(WIDTH)
HIDE = 1e30
KV, QG, AUX = range(3)
DQ, DKV = range(2)


FAR_TO_NEAR = (4, 3, 5, 2, 6, 1, 7)


def sent_at(step):
    offset = 0
    for i, sent in enumerate(FAR_TO_NEAR):
        offset = jnp.where(step == i + 1, sent, offset)
    return offset


def mm(a, b):
    return lax.dot_general(a, b, (((1,), (0,)), ((), ())), preferred_element_type=jnp.float32)


def mm_nt(a, b):
    return lax.dot_general(a, b, (((1,), (1,)), ((), ())), preferred_element_type=jnp.float32)


def kernel(
    q_ref, k_ref, v_ref, o_ref, g_ref, ln_ref, pos_ref,
    dq_ref, dkv_ref,
    kv, qg, auxs, kvb, qgb, auxb, ov, qt, gt, tri, dqa, dqo, dkvo, dqn, part_out, part_in,
    load_sem, in_send, in_recv, fwd_send, part_send, part_recv, out_send, out_recv,
):
    me = lax.axis_index("ctx")
    chip = me // 2
    core = me % 2
    sign = 1 - 2 * core
    shares = core == 0
    toward = 2 * (chip % 2) - 1
    partner = me - 2 * toward
    sources = (kv, qg, auxs)
    landing = (kvb, qgb, auxb)
    staged = (dqo, dkvo)
    results = (dq_ref, dkv_ref)

    def wait(ref, sem):
        pltpu.make_async_copy(ref, ref, sem).wait()

    def near(i):
        return (chip + toward * i + CHIPS) % CHIPS

    def far(i):
        return (chip - toward * (i + 1) + CHIPS) % CHIPS

    def nearer(which):
        offset = (chip - 2 * which + CHIPS) % CHIPS
        side = jnp.where((offset >= 1) & (offset <= CHIPS // 2), 1, 0)
        return 2 * (2 * which + side)

    def send(kind, head, slot, dest):
        pltpu.make_async_remote_copy(
            src_ref=sources[kind].at[head],
            dst_ref=landing[kind].at[slot, me],
            send_sem=in_send.at[kind],
            recv_sem=in_recv.at[kind, slot, chip],
            device_id={"ctx": dest},
            device_id_type=pl.DeviceIdType.MESH,
        ).start()

    def keep(kind, head, slot):
        pltpu.make_async_copy(
            sources[kind].at[head], landing[kind].at[slot, me], in_recv.at[kind, slot, chip]
        ).start()

    def send_extra(kinds, i):
        which = (chip // 2 + i) % EXTRA
        dest = nearer(which)

        @pl.when(dest != me)
        def _():
            for kind in kinds:
                send(kind, N + which, 0, dest)

        @pl.when(dest == me)
        def _():
            for kind in kinds:
                keep(kind, N + which, 0)

    def send_own_chip(kinds):
        for kind in kinds:
            keep(kind, me, 1)
        for kind in kinds:
            send(kind, 2 * chip + 1 - core, 1, 2 * chip + 1 - core)

    def send_main(kinds, i):
        for b in range(2):
            dest = 2 * ((chip + sign * FAR_TO_NEAR[i] + CHIPS) % CHIPS) + (core + b) % 2
            for kind in kinds:
                send(kind, dest, 1, dest)

    barrier = pltpu.get_barrier_semaphore()

    def greet(i, carry):
        pl.semaphore_signal(
            barrier, inc=1, device_id={"ctx": (me + i) % N}, device_id_type=pl.DeviceIdType.MESH
        )
        return carry

    lax.fori_loop(1, N, greet, 0)
    loads = [
        pltpu.make_async_copy(src, dst, load_sem.at[i])
        for i, (src, dst) in enumerate(
            (
                (q_ref, qg.at[:, 0]),
                (g_ref, qg.at[:, 1]),
                (o_ref, ov),
                (k_ref, kv.at[:, 0]),
                (v_ref, kv.at[:, 1]),
            )
        )
    ]
    for load in loads:
        load.start()
    pl.semaphore_wait(barrier, N - 1)

    loads[0].wait()
    loads[1].wait()
    for i in range(2):
        send_main((QG,), i)
        send_extra((QG,), i)
    send_own_chip((QG,))

    loads[2].wait()
    norm = ln_ref[...].astype(jnp.float32) * LOG2E
    ones = jnp.ones((8, WIDTH), jnp.bfloat16)
    first = lax.broadcasted_iota(jnp.int32, (2, ROWS), 0) == 0
    for h in range(HEADS):
        product = qg[h, 1].astype(jnp.float32) * ov[h].astype(jnp.float32)
        high = product.astype(jnp.bfloat16)
        low = (product - high.astype(jnp.float32)).astype(jnp.bfloat16)
        delta = (mm_nt(ones, high) + mm_nt(ones, low)).astype(jnp.bfloat16).astype(jnp.float32)
        auxs[h] = jnp.where(first, norm[h : h + 1, :], delta[:2])
    for i in range(EXTRA):
        send_extra((AUX,), i)
    send_own_chip((AUX,))
    for i in range(CHIPS - 1):
        send_main((AUX,), i)
    loads[3].wait()
    loads[4].wait()
    for i in range(2, CHIPS - 1):
        send_main((QG,), i)
        if i < EXTRA:
            send_extra((QG,), i)
        if i < 2 + EXTRA:
            send_extra((KV,), i - 2)

    @pl.when(shares)
    def _():
        def forward(i, carry):
            pair = pl.ds(2 * near(i), 2)
            for kind in (AUX, QG):
                wait(landing[kind].at[0, pair], in_recv.at[kind, 0, near(i)])
                pltpu.make_async_remote_copy(
                    src_ref=landing[kind].at[0, pair],
                    dst_ref=landing[kind].at[0, pair],
                    send_sem=fwd_send.at[kind - QG],
                    recv_sem=in_recv.at[kind, 0, near(i)],
                    device_id={"ctx": partner},
                    device_id_type=pl.DeviceIdType.MESH,
                ).start()
            return carry

        lax.fori_loop(0, HALF, forward, 0)

    send_own_chip((KV,))
    for i in range(CHIPS - 1):
        send_main((KV,), i)

    below = lax.broadcasted_iota(jnp.int32, (ROWS, ROWS), 0) > lax.broadcasted_iota(
        jnp.int32, (ROWS, ROWS), 1
    )
    tri[0] = jnp.zeros((ROWS, ROWS), jnp.float32)
    tri[1] = jnp.where(below, HIDE, 0.0)

    def give(kind, slot, head, dest):
        src = staged[kind].at[slot, dest]
        dst = results[kind].at[head]

        @pl.when(dest != me)
        def _():
            pltpu.make_async_remote_copy(
                src_ref=src,
                dst_ref=dst,
                send_sem=out_send.at[kind, slot],
                recv_sem=out_recv.at[kind],
                device_id={"ctx": dest},
                device_id_type=pl.DeviceIdType.MESH,
            ).start()

        @pl.when(dest == me)
        def _():
            pltpu.make_async_copy(src, dst, out_recv.at[kind]).start()

    def around(i):
        return (chip - sign * sent_at(i) + CHIPS) % CHIPS

    def pass_part(i):
        return pltpu.make_async_remote_copy(
            src_ref=part_out.at[i],
            dst_ref=part_in.at[i],
            send_sem=part_send.at[0],
            recv_sem=part_recv.at[i],
            device_id={"ctx": partner},
            device_id_type=pl.DeviceIdType.MESH,
        )

    def turned(slot, c):
        qt[c] = qgb[slot, pl.ds(2 * c, 2), 0].reshape(PAIR, WIDTH).T
        gt[c] = qgb[slot, pl.ds(2 * c, 2), 1].reshape(PAIR, WIDTH).T

    def queries_arrived(slot, c):
        for kind in (AUX, QG):
            wait(landing[kind].at[slot, pl.ds(2 * c, 2)], in_recv.at[kind, slot, c])
        turned(slot, c)

    def one_pair(step, carry):
        slot = jnp.where(step < HALF, 0, 1)
        turn = step - HALF * slot
        head = jnp.where(slot == 0, N + chip // 2, me)

        @pl.when(turn == 0)
        def _():
            dqa[...] = jnp.zeros_like(dqa)

        @pl.when(step == 0)
        def _():
            def ready(i, carry):
                turned(0, near(i))
                queries_arrived(0, far(i))
                return carry

            lax.fori_loop(0, HALF, ready, 0)

        @pl.when(step == HALF)
        def _():
            def ready(i, carry):
                queries_arrived(1, around(i))
                return carry

            lax.fori_loop(0, CHIPS, ready, 0)

        c = jnp.where(slot == 0, near(turn), around(turn))
        wait(landing[KV].at[slot, pl.ds(2 * c, 2)], in_recv.at[KV, slot, c])
        pair = pl.ds(2 * c, 2)
        keys = kvb[slot, pair, 0].reshape(PAIR, WIDTH)
        vals = kvb[slot, pair, 1].reshape(PAIR, WIDTH)
        keys_t = keys.T
        dk = jnp.zeros((PAIR, WIDTH), jnp.float32)
        dv = jnp.zeros((PAIR, WIDTH), jnp.float32)
        for t in range(0, N, TILE):
            spot = slice(t, t + TILE)
            queries = qgb[slot, spot, 0].reshape(TILE * ROWS, WIDTH)
            grads = qgb[slot, spot, 1].reshape(TILE * ROWS, WIDTH)
            chips = range(t // 2, (t + TILE) // 2)
            norms = [auxb[slot, t + b, 0:1, :] for b in range(TILE)]
            delta = jnp.concatenate([auxb[slot, t + b, 1:2, :] for b in range(TILE)], axis=1)
            diagonal = [tri[jnp.where(c == u, 1, 0)] for u in chips]
            scores = mm(keys, jnp.concatenate([qt[u] for u in chips], axis=1)) * (SCALE * LOG2E)
            grad_weights = mm(vals, jnp.concatenate([gt[u] for u in chips], axis=1))
            parts = []
            for kblock in range(2):
                bias = []
                for b in range(TILE):
                    later = pos_ref[2 * c + kblock] > pos_ref[t + b]
                    row = norms[b] + jnp.where(later, HIDE, 0.0)
                    bias.append(
                        row + diagonal[b // 2]
                        if kblock == b % 2
                        else jnp.broadcast_to(row, (ROWS, ROWS))
                    )
                part = scores[kblock * ROWS : (kblock + 1) * ROWS]
                parts.append(jnp.exp2(part - jnp.concatenate(bias, axis=1)))
            weights = jnp.concatenate(parts, axis=0)
            grad_scores = (weights * (grad_weights - delta)).astype(jnp.bfloat16)
            dv += mm(weights.astype(jnp.bfloat16), grads)
            dk += mm(grad_scores, queries)
            dq = mm(keys_t, grad_scores)
            for i, u in enumerate(chips):
                dqa[u] += dq[:, i * PAIR : (i + 1) * PAIR]
        dkvo[slot, pair, 0] = (dk * SCALE).astype(jnp.bfloat16).reshape(2, ROWS, WIDTH)
        dkvo[slot, pair, 1] = dv.astype(jnp.bfloat16).reshape(2, ROWS, WIDTH)
        for b in range(2):
            give(DKV, slot, head, 2 * c + b)

        @pl.when(step == HALF - 1)
        def _():
            def part(i, carry):
                part_out[i] = dqa[far(i)].T.astype(jnp.bfloat16)
                pass_part(i).start()
                dqn[i] = dqa[near(i)].T
                return carry

            lax.fori_loop(0, HALF, part, 0)

        @pl.when(shares & (step == HALF + 5))
        def _():
            def total(i, carry):
                pass_part(i).wait_recv()
                done = ((dqn[i] + part_in[i].astype(jnp.float32)) * SCALE).astype(jnp.bfloat16)
                c = near(i)
                dqo[0, pl.ds(2 * c, 2)] = done.reshape(2, ROWS, WIDTH)
                for b in range(2):
                    give(DQ, 0, N + chip // 2, 2 * c + b)
                return carry

            lax.fori_loop(0, HALF, total, 0)

        @pl.when(step == HALF + CHIPS - 1)
        def _():
            def finish(i, carry):
                c = around((i + 1) % CHIPS)
                done = (dqa[c] * SCALE).T.astype(jnp.bfloat16)
                dqo[1, pl.ds(2 * c, 2)] = done.reshape(2, ROWS, WIDTH)
                for b in range(2):
                    give(DQ, 1, me, 2 * c + b)
                return carry

            lax.fori_loop(0, CHIPS, finish, 0)

        return carry

    lax.fori_loop(jnp.where(shares, 0, HALF), HALF + CHIPS, one_pair, 0)

    @pl.when(shares)
    def _():
        for kind in range(3):
            wait(sources[kind].at[pl.ds(0, HEADS - 2)], in_send.at[kind])
        for kind in (AUX, QG):
            wait(landing[kind].at[0, pl.ds(0, CHIPS)], fwd_send.at[kind - QG])
        wait(part_out, part_send.at[0])
        for kind in range(2):
            wait(staged[kind].at[0, pl.ds(0, CHIPS - 1)], out_send.at[kind, 0])

    @pl.when(jnp.logical_not(shares))
    def _():
        for kind in range(3):
            wait(sources[kind].at[pl.ds(0, HEADS - 1)], in_send.at[kind])

    for kind in (DKV, DQ):
        wait(staged[kind].at[1, pl.ds(0, N - 1)], out_send.at[kind, 1])
        wait(results[kind], out_recv.at[kind])


def hand_on(dq_ref, dkv_ref, dq_out, dk_out, dv_out, sem):
    copies = [
        pltpu.make_async_copy(src, dst, sem.at[i])
        for i, (src, dst) in enumerate(
            ((dq_ref, dq_out), (dkv_ref.at[:, 0], dk_out), (dkv_ref.at[:, 1], dv_out))
        )
    ]
    for copy in copies:
        copy.start()
    for copy in copies:
        copy.wait()


def body(queries, keys, values, outputs, grad_out, log_norm, block_position):
    by_head = [jnp.transpose(x, (1, 0, 2)) for x in (queries, keys, values, outputs, grad_out)]
    whole = jax.ShapeDtypeStruct((HEADS, ROWS, WIDTH), jnp.bfloat16)
    doubles = pltpu.VMEM((HEADS, 2, ROWS, WIDTH), jnp.bfloat16)
    blocks = pltpu.VMEM((2, N, ROWS, WIDTH), jnp.bfloat16)
    double_blocks = pltpu.VMEM((2, N, 2, ROWS, WIDTH), jnp.bfloat16)
    results = pl.pallas_call(
        kernel,
        out_shape=(pltpu.VMEM((HEADS, ROWS, WIDTH), jnp.bfloat16), doubles),
        in_specs=[pl.BlockSpec(memory_space=pl.ANY)] * 5
        + [pl.BlockSpec(memory_space=pltpu.VMEM), pl.BlockSpec(memory_space=pltpu.SMEM)],
        out_specs=[pl.BlockSpec(memory_space=pltpu.VMEM)] * 2,
        scratch_shapes=[
            doubles, doubles,
            pltpu.VMEM((HEADS, 2, ROWS), jnp.float32),
            double_blocks, double_blocks,
            pltpu.VMEM((2, N, 2, ROWS), jnp.float32),
            pltpu.VMEM((HEADS, ROWS, WIDTH), jnp.bfloat16),
            pltpu.VMEM((CHIPS, WIDTH, PAIR), jnp.bfloat16),
            pltpu.VMEM((CHIPS, WIDTH, PAIR), jnp.bfloat16),
            pltpu.VMEM((2, ROWS, ROWS), jnp.float32),
            pltpu.VMEM((CHIPS, WIDTH, PAIR), jnp.float32),
            blocks, double_blocks,
            pltpu.VMEM((HALF, PAIR, WIDTH), jnp.float32),
            pltpu.VMEM((HALF, PAIR, WIDTH), jnp.bfloat16),
            pltpu.VMEM((HALF, PAIR, WIDTH), jnp.bfloat16),
            pltpu.SemaphoreType.DMA((5,)),
            pltpu.SemaphoreType.DMA((3,)),
            pltpu.SemaphoreType.DMA((3, 2, CHIPS)),
            pltpu.SemaphoreType.DMA((2,)),
            pltpu.SemaphoreType.DMA((1,)),
            pltpu.SemaphoreType.DMA((HALF,)),
            pltpu.SemaphoreType.DMA((2, 2)),
            pltpu.SemaphoreType.DMA((2,)),
        ],
        compiler_params=pltpu.CompilerParams(
            collective_id=0, has_side_effects=True, vmem_limit_bytes=60 * 1024 * 1024
        ),
        name="attention_backward",
    )(*by_head, log_norm.T, block_position)
    results = pl.pallas_call(
        hand_on,
        out_shape=(whole, whole, whole),
        in_specs=[pl.BlockSpec(memory_space=pltpu.VMEM)] * 2,
        out_specs=[pl.BlockSpec(memory_space=pl.ANY)] * 3,
        scratch_shapes=[pltpu.SemaphoreType.DMA((3,))],
        compiler_params=pltpu.CompilerParams(vmem_limit_bytes=8 * 1024 * 1024),
        name="hand_on",
    )(*results)
    return tuple(jnp.transpose(x, (1, 0, 2)) for x in results)


def solution(mesh):
    rows = P(("seq", "ctx"), None, None)
    return jax.shard_map(
        body,
        mesh=mesh,
        in_specs=(rows, rows, rows, rows, rows, P(("seq", "ctx"), None), P("seq")),
        out_specs=(rows, rows, rows),
        check_vma=False,
    )
```
